32 devices in a mesh: dp: 8 (over z, y), seq: 4 (over x, core).
Axes of the slice: x: 2, y: 2, z: 4, core: 2. Of those that a mesh axis runs over, the one named last changes fastest.
Arguments:
- hidden_in: bfloat16 [512, 64, 768], P('seq', 'dp'), may hold values from -6 to 6
- lengths: int32 [64], P('dp'), may hold values from 64 to 512, as said below
- labels: int32 [64], P(('dp', 'seq')), may hold values from 0 to 2
- out_cotangent: bfloat16 [512, 64, 768], P('seq', 'dp'), may hold values from -6 to 6
- qkv_weight: bfloat16 [768, 2304], replicated, may hold values from -0.21875 to 0.21875
- out_weight: bfloat16 [768, 768], replicated, may hold values from -1.25 to 1.25
- up_weight: bfloat16 [768, 3072], replicated, may hold values from -0.21875 to 0.21875
- down_weight: bfloat16 [3072, 768], replicated, may hold values from -0.109375 to 0.109375
- pool_weight: bfloat16 [768, 768], replicated, may hold values from -0.21875 to 0.21875
- class_weight: bfloat16 [768, 3], replicated, may hold values from -1.75 to 1.75
- norm_gains: float32 [2, 768], replicated, may hold values from 0.4 to 1.6
- biases: float32 [7, 768], replicated, may hold values from -2 to 2
- up_bias: float32 [3072], replicated, may hold values from -2 to 2
- class_bias: float32 [3], replicated, may hold values from -4 to 4
Outputs:
- hidden_out: bfloat16 [512, 64, 768], P('seq', 'dp')
- ramp_logits: float32 [64, 3], P(('dp', 'seq'))
- grad_in: float32 [512, 64, 768], P('seq', 'dp')
- grad_qkv_weight: float32 [768, 2304], P(('dp', 'seq'))
- grad_out_weight: float32 [768, 768], P(('dp', 'seq'))
- grad_up_weight: float32 [768, 3072], P(('dp', 'seq'))
- grad_down_weight: float32 [3072, 768], P(('dp', 'seq'))
- grad_pool_weight: float32 [768, 768], P(('dp', 'seq'))
- grad_class_weight: float32 [768, 3], P(('dp', 'seq'))
- grad_norm_gains: float32 [2, 768], P(None, ('dp', 'seq'))
- grad_biases: float32 [7, 768], P(None, ('dp', 'seq'))
- grad_up_bias: float32 [3072], P(('dp', 'seq'))
- grad_class_bias: float32 [3], replicated
The draws below stay inside these ranges and needn't reach their ends.
Inputs may be any that keep to these rules, and one draw needn't show every extreme that they name: `lengths`: each is at least 64; among the sequences of each index of dp, one is exactly 512 long.
All inputs are finite; a program needn't handle non-finite values.
Results may differ from the reference program's by a relative error of at most 0.012.
Values may be sent and summed in bfloat16 or wider, within the bound.
No kernel may reach another device: no remote copies, remote signals or barrier semaphores. Data moves between devices by JAX's collectives and lax.ppermute only.
A program may use at most 192 MiB of HBM per device.

```python
import jax
import jax.numpy as jnp
from jax import lax

D = 768
HEADS = 12
HEAD_DIM = 64
FF = 3072
CLASSES = 3
L = 512
SEQS = 64
N_DP = 8


def draw_lengths(key, part):
    key = jax.random.fold_in(key, 11)
    key_lens, key_full = jax.random.split(key)
    group_size = SEQS // N_DP
    drawn = jax.random.randint(key_lens, (SEQS,), L // 8, L + 1)
    full_pos = jax.random.randint(key_full, (N_DP,), 0, group_size)
    index_all = jnp.arange(SEQS)
    is_full = index_all % group_size == jnp.repeat(full_pos, group_size)
    return jnp.where(is_full, L, drawn).astype(jnp.int32)


def plant(result, key, low, largest):
    extent = result.shape
    spot = [jax.random.randint(jax.random.fold_in(key, axis), (), 0, extent[axis]) for axis in range(len(extent))]
    result = result.at[tuple(spot)].set(low)
    longest = extent.index(max(extent))
    spot[longest] = (spot[longest] + 1) % extent[longest]
    return result.at[tuple(spot)].set(largest)


def level_of(own_key, shape, cuts, low, high):
    loudness = 1.0
    for axis_at, parts in cuts:
        draws = jax.random.uniform(jax.random.fold_in(jax.random.fold_in(own_key, 6), axis_at), (parts,), jnp.float32, low / len(cuts), high / len(cuts))
        loudness = loudness * jnp.repeat(jnp.exp(draws), shape[axis_at] // parts).reshape((-1,) + (1,) * (len(shape) - 1 - axis_at))
    return loudness


def bell_draw(key, shape, spread, limit, shards=(), dtype=jnp.bfloat16):
    level = level_of(key, shape, shards, -0.22, 0.18) if shards else 1.0
    result = jax.random.normal(key, shape, jnp.float32) * spread * level
    return jnp.minimum(jnp.maximum(result, -limit), limit).astype(dtype)


def setup_inputs(seed: int = 0) -> dict:
    splits = jax.random.split(jax.random.key(seed), 15)
    return {
        "hidden_in": bell_draw(splits[0], (L, SEQS, D), 1.0, 6.0, ((0, 4), (1, 8))),
        "lengths": draw_lengths(jax.random.fold_in(splits[14], 71), 0),
        "labels": plant(jax.random.randint(splits[2], (SEQS,), 0, CLASSES), jax.random.fold_in(splits[2], 1), 0, CLASSES - 1).astype(jnp.int32),
        "out_cotangent": bell_draw(splits[3], (L, SEQS, D), 1.0, 6.0, ((0, 4), (1, 8))),
        "qkv_weight": bell_draw(splits[4], (D, 3 * D), D ** -0.5, 0.21875),
        "out_weight": bell_draw(splits[5], (D, D), (D // 32) ** -0.5, 1.25),
        "up_weight": bell_draw(splits[6], (D, FF), D ** -0.5, 0.21875),
        "down_weight": bell_draw(splits[7], (FF, D), FF ** -0.5, 0.109375),
        "pool_weight": bell_draw(splits[8], (D, D), D ** -0.5, 0.21875),
        "class_weight": bell_draw(splits[9], (D, CLASSES), (D // 64) ** -0.5, 1.75),
        "norm_gains": jnp.clip(1.0 + 0.12 * jax.random.normal(splits[10], (2, D), jnp.float32), 0.4, 1.6),
        "biases": bell_draw(splits[11], (7, D), 0.3, 2.0, (), jnp.float32),
        "up_bias": bell_draw(splits[12], (FF,), 0.3, 2.0, (), jnp.float32),
        "class_bias": bell_draw(splits[13], (CLASSES,), 1.0, 4.0, (), jnp.float32),
    }


@jax.custom_vjp
def low(v):
    return lax.optimization_barrier(v.astype(jnp.bfloat16)).astype(jnp.float32)

@jax.custom_vjp
def low_back(v):
    return v

def low_keep(v):
    return (low(v), None)

def low_pass(kept, grad):
    return (grad,)

def back_keep(v):
    return (v, None)

def back_low(kept, grad):
    return (low(grad),)
low.defvjp(low_keep, low_pass)
low_back.defvjp(back_keep, back_low)
eps = 1e-12
neg_big = -1e+30
highest = lax.Precision.HIGHEST

def matmul(left_in, right_in):
    return jnp.dot(left_in, right_in, precision=highest, preferred_element_type=jnp.float32)

def layer_norm(resid, gain, shift):
    row_mean = lax.optimization_barrier(jnp.mean(resid, axis=-1, keepdims=True))
    centred = resid - row_mean
    variance = lax.optimization_barrier(jnp.mean(centred * centred, axis=-1, keepdims=True))
    return centred * lax.rsqrt(variance + eps) * gain + shift

def forward(params, block_in, live_keys, block_labels):
    qkv_weight, out_weight, up_weight, down_weight, pool_weight, class_weight, norm_gains, biases, up_bias, class_bias = params
    seq_count = block_in.shape[0]
    row_data = block_in.reshape(seq_count * L, D)
    zero_bias = jnp.zeros((D,), jnp.float32)
    qkv_full = matmul(row_data, qkv_weight) + jnp.concatenate([biases[0], zero_bias, biases[1]])
    qkv_full = low(low_back(qkv_full)).reshape(seq_count, L, 3, HEADS, HEAD_DIM)
    queries = qkv_full[:, :, 0]
    keys_in = qkv_full[:, :, 1]
    values = qkv_full[:, :, 2]
    raw_scores = jnp.einsum('bqhd,bkhd->bhqk', queries, keys_in, precision=highest) * HEAD_DIM ** (-0.5)
    scores = jnp.where(live_keys[:, None, None, :], low_back(raw_scores), neg_big)
    weights_low = low(jax.nn.softmax(scores, axis=-1))
    context = jnp.einsum('bhqk,bkhd->bqhd', weights_low, values, precision=highest).reshape(seq_count * L, D)
    context = low(low_back(context))
    attn_out = low_back(matmul(context, out_weight) + biases[2])
    middle = layer_norm(row_data + attn_out, norm_gains[0], biases[3])
    pre_act = low_back(matmul(low(middle), up_weight) + up_bias)
    activated = low(jax.nn.gelu(pre_act, approximate=False))
    branch = low_back(matmul(activated, down_weight) + biases[4])
    final = low(layer_norm(middle + branch, norm_gains[1], biases[5]))
    first_rows = final.reshape(seq_count, L, D)[:, 0, :]
    pooled = jnp.tanh(matmul(first_rows, pool_weight) + biases[6])
    ramp_logits = matmul(pooled, class_weight) + class_bias
    picked = lax.optimization_barrier(jnp.sum(jnp.where(jnp.arange(CLASSES)[None, :] == block_labels[:, None], ramp_logits, 0.0), axis=-1))
    ramp_loss = jnp.sum(jax.scipy.special.logsumexp(ramp_logits, axis=-1) - picked)
    return (final.reshape(seq_count, L, D), ramp_logits, ramp_loss)

def reference(hidden_in, lengths, labels, out_cotangent, qkv_weight, out_weight, up_weight, down_weight, pool_weight, class_weight, norm_gains, biases, up_bias, class_bias):
    params = (qkv_weight.astype(jnp.float32), out_weight.astype(jnp.float32), up_weight.astype(jnp.float32), down_weight.astype(jnp.float32), pool_weight.astype(jnp.float32), class_weight.astype(jnp.float32), norm_gains.astype(jnp.float32), biases.astype(jnp.float32), up_bias.astype(jnp.float32), class_bias.astype(jnp.float32))
    block_count = SEQS // 8
    inputs_all = jnp.transpose(hidden_in.astype(jnp.float32), (1, 0, 2)).reshape(block_count, 8, L, D)
    cots_all = jnp.transpose(out_cotangent.astype(jnp.float32), (1, 0, 2)).reshape(block_count, 8, L, D)
    lens_all = lengths.reshape(block_count, 8)
    labels_all = labels.reshape(block_count, 8)

    def scan_step(totals, packed):
        block_in, block_cot, block_lens, block_labels = packed
        live_keys = jnp.arange(L)[None, :] < block_lens[:, None]

        def run_block(weights_in, rows_in):
            return forward(weights_in, rows_in, live_keys, block_labels)
        results, pull_back = jax.vjp(run_block, params, block_in)
        final, ramp_logits, ramp_loss = results
        weight_grads, input_grad = pull_back((block_cot, jnp.zeros_like(ramp_logits), jnp.ones_like(ramp_loss)))
        return (jax.tree.map(jnp.add, totals, weight_grads), (final.astype(jnp.bfloat16), ramp_logits, input_grad))
    start_totals = jax.tree.map(jnp.zeros_like, params)
    totals, gathered = lax.scan(scan_step, start_totals, (inputs_all, cots_all, lens_all, labels_all))
    finals, logits_all, input_grads = gathered
    grad_qkv, grad_out, grad_up, grad_down, grad_pool, grad_class, grad_gains, grad_biases, grad_up_bias, grad_class_bias = totals
    finals_out = jnp.transpose(finals.reshape(SEQS, L, D), (1, 0, 2))
    grads_out = jnp.transpose(input_grads.reshape(SEQS, L, D), (1, 0, 2))
    return (finals_out, logits_all.reshape(SEQS, CLASSES), grads_out, grad_qkv, grad_out, grad_up, grad_down, grad_pool, grad_class, grad_gains, grad_biases, grad_up_bias, grad_class_bias)
```

```python
import functools

import jax
import jax.numpy as jnp
from jax import lax
from jax.experimental import pallas as pl
from jax.experimental.pallas import tpu as pltpu
from jax.sharding import PartitionSpec as P

HEAD_DIM = 64
PAIR = 2 * HEAD_DIM
REC = 8

eps = 1e-12
neg_big = -1e30
highest = lax.Precision.HIGHEST
f32 = jnp.float32
bf16 = jnp.bfloat16
MIB = 1 << 20

ERF_P = 0.3275911
ERF_A = (0.254829592, -0.284496736, 1.421413741, -1.453152027, 1.061405429)


def nn(left, right):
    return lax.dot_general(left, right, (((1,), (0,)), ((), ())), preferred_element_type=f32)


def nt(left, right):
    return lax.dot_general(left, right, (((1,), (1,)), ((), ())), preferred_element_type=f32)


def tn(left, right):
    return lax.dot_general(left, right, (((0,), (0,)), ((), ())), preferred_element_type=f32)


def params(limit=56):
    return pltpu.CompilerParams(vmem_limit_bytes=limit * MIB)


def cost(flops, nbytes, trans=0):
    return pl.CostEstimate(flops=int(flops), bytes_accessed=int(nbytes), transcendentals=int(trans))


def smem():
    return pl.BlockSpec(memory_space=pltpu.SMEM)


def whole(shape):
    return pl.BlockSpec(shape, lambda *_: (0,) * len(shape))


def three_parts(value):
    hi = value.astype(bf16)
    rest = value - hi.astype(f32)
    mid = rest.astype(bf16)
    low = (rest - mid.astype(f32)).astype(bf16)
    return jnp.concatenate([hi, mid, low], axis=0)


def fine_dot(dot, value, weight):
    rows = value.shape[0]
    parts = dot(jnp.concatenate([three_parts(value)], axis=0), weight)
    return parts[:rows] + parts[rows : 2 * rows] + parts[2 * rows :]


def split_kernel(info, rows, *outs):
    chunks = len(outs)
    per, span, _ = outs[0].shape
    group = chunks * per
    block = 16 * group
    own = info[0]
    dest = lax.broadcasted_iota(jnp.int32, (block, block), 0)
    source = lax.broadcasted_iota(jnp.int32, (block, block), 1)
    chunk = dest // (16 * per)
    wanted = (dest % 16) * group + per * (chunk ^ own) + (dest // 16) % per
    perm = jnp.where(source == wanted, 1.0, 0.0).astype(bf16)
    for b in range(span // 16):
        moved = nn(perm, rows[b * block : (b + 1) * block, :]).astype(bf16)
        for c in range(chunks):
            for q in range(per):
                at = (c * per + q) * 16
                outs[c][q, b * 16 : (b + 1) * 16, :] = moved[at : at + 16]


def split_rows(info, rows, positions, group, chunks):
    width = rows.shape[1]
    per = group // chunks
    steps = 4
    span = positions // steps
    return pl.pallas_call(
        split_kernel,
        grid=(steps,),
        in_specs=[smem(), pl.BlockSpec((span * group, width), lambda i: (i, 0))],
        out_specs=[pl.BlockSpec((per, span, width), lambda i: (0, i, 0))] * chunks,
        out_shape=[jax.ShapeDtypeStruct((per, positions, width), bf16)] * chunks,
        compiler_params=params(),
        cost_estimate=cost(2 * rows.size * 16 * group, 4 * rows.size),
        name="split_rows",
    )(info, rows)


def merge_kernel(info, *refs):
    ins, out = refs[:-1], refs[-1]
    chunks = len(ins)
    per, span, _ = ins[0].shape
    group = chunks * per
    block = 16 * group
    own = info[0]
    dest = lax.broadcasted_iota(jnp.int32, (block, block), 0)
    source = lax.broadcasted_iota(jnp.int32, (block, block), 1)
    seq = dest % group
    wanted = (((seq // per) ^ own) * per + seq % per) * 16 + dest // group
    perm = jnp.where(source == wanted, 1.0, 0.0).astype(bf16)
    for b in range(span // 16):
        rows = jnp.concatenate(
            [ins[c][q, b * 16 : (b + 1) * 16, :] for c in range(chunks) for q in range(per)], axis=0
        )
        out[b * block : (b + 1) * block, :] = nn(perm, rows).astype(out.dtype)


def merge_rows(info, parts, dtype):
    chunks = len(parts)
    per, positions, width = parts[0].shape
    group = per * chunks
    steps = 4
    span = positions // steps
    return pl.pallas_call(
        merge_kernel,
        grid=(steps,),
        in_specs=[smem()] + [pl.BlockSpec((per, span, width), lambda i: (0, i, 0))] * chunks,
        out_specs=pl.BlockSpec((span * group, width), lambda i: (i, 0)),
        out_shape=jax.ShapeDtypeStruct((positions * group, width), dtype),
        compiler_params=params(),
        cost_estimate=cost(2 * positions * group * width * 16 * group, 6 * positions * group * width),
        name="merge_rows",
    )(info, *parts)


def exchange(parts):
    size = lax.axis_size("seq")
    return [parts[0]] + [
        lax.ppermute(parts[c], "seq", [(i, i ^ c) for i in range(size)]) for c in range(1, size)
    ]


def row_stats(resid):
    mean = jnp.mean(resid, axis=-1, keepdims=True)
    centred = resid - mean
    scale = lax.rsqrt(jnp.mean(centred * centred, axis=-1, keepdims=True) + eps)
    return centred * scale, scale


def attend_kernel(info, *refs):
    chunks = len(refs) - 10
    parts = refs[:chunks]
    qkv_w, out_w, biases, x_out, qkv, context, lse, normed, scale, stats = refs[chunks:]
    width = out_w.shape[0]
    span = parts[0].shape[1]
    length = chunks * span
    pairs = width // PAIR
    own = info[0]
    live_len = info[1 + pl.program_id(0)]
    x_out[...] = jnp.concatenate([part[0] for part in parts], axis=0)
    for third in range(3):
        cols = slice(third * width, (third + 1) * width)
        block = nn(x_out[...], qkv_w[:, cols])
        if third == 0:
            block = block + biases[0:1, :]
        elif third == 2:
            block = block + biases[1:2, :]
        qkv[:, cols] = block.astype(bf16)
    lane = lax.broadcasted_iota(jnp.int32, (length, PAIR), 1)
    row = lax.broadcasted_iota(jnp.int32, (length, PAIR), 0)
    pos = ((row // span) ^ own) * span + row % span
    key_ext = jnp.where((lane == 0) & (pos >= live_len), neg_big, 0.0).astype(bf16)
    query_ext = jnp.where(lane == 0, 1.0, 0.0).astype(bf16)
    low_half = lane < HEAD_DIM
    masks = [jnp.where(low_half, 1.0, 0.0).astype(bf16), jnp.where(low_half, 0.0, 1.0).astype(bf16)]
    stats[...] = jnp.zeros_like(stats)

    def one_pair(i, carry):
        start = pl.multiple_of(i * PAIR, PAIR)
        queries = qkv[:, pl.ds(start, PAIR)] * bf16(HEAD_DIM**-0.5)
        keys = jnp.concatenate([qkv[:, pl.ds(start + width, PAIR)], key_ext], axis=1)
        values = qkv[:, pl.ds(start + 2 * width, PAIR)]
        total = None
        tops = []
        for head in range(2):
            scores = nt(jnp.concatenate([queries * masks[head], query_ext], axis=1), keys)
            top = jnp.max(scores, axis=1, keepdims=True)
            weights = jnp.exp(scores - top).astype(bf16)
            part = nn(weights, jnp.concatenate([values * masks[head], masks[head]], axis=1))
            total = part if total is None else total + part
            tops.append(top)
        row_total = total[:, PAIR:]
        context[:, pl.ds(start, PAIR)] = (total[:, :PAIR] / row_total).astype(bf16)
        log_total = jnp.where(low_half, tops[0], tops[1]) + jnp.log(row_total)
        swapped = pltpu.roll(log_total, HEAD_DIM, 1)
        stats[...] = jnp.where(
            lane == 2 * i, log_total, jnp.where(lane == 2 * i + 1, swapped, stats[...])
        )
        return carry

    lax.fori_loop(0, pairs, one_pair, 0)
    lse[0] = jnp.transpose(stats[...])[: lse.shape[1], :]
    resid = x_out[...].astype(f32) + (nn(context[...], out_w[...]) + biases[2:3, :])
    n_one, q_one = row_stats(resid)
    normed[...] = n_one
    scale[...] = q_one


def attend(info, parts, qkv_w, out_w, biases):
    chunks = len(parts)
    per, span, width = parts[0].shape
    length = chunks * span
    rows = per * length
    heads = width // HEAD_DIM
    head_rows = -(-heads // 8) * 8
    by_seq = lambda i: (i, 0)
    return pl.pallas_call(
        attend_kernel,
        grid=(per,),
        in_specs=[smem()]
        + [pl.BlockSpec((1, span, width), lambda i: (i, 0, 0))] * chunks
        + [whole(qkv_w.shape), whole(out_w.shape), whole(biases.shape)],
        out_specs=[
            pl.BlockSpec((length, width), by_seq),
            pl.BlockSpec((length, 3 * width), by_seq),
            pl.BlockSpec((length, width), by_seq),
            pl.BlockSpec((1, head_rows, length), lambda i: (i, 0, 0)),
            pl.BlockSpec((length, width), by_seq),
            pl.BlockSpec((length, 1), by_seq),
        ],
        out_shape=[
            jax.ShapeDtypeStruct((rows, width), bf16),
            jax.ShapeDtypeStruct((rows, 3 * width), bf16),
            jax.ShapeDtypeStruct((rows, width), bf16),
            jax.ShapeDtypeStruct((per, head_rows, length), f32),
            jax.ShapeDtypeStruct((rows, width), f32),
            jax.ShapeDtypeStruct((rows, 1), f32),
        ],
        scratch_shapes=[pltpu.VMEM((length, PAIR), f32)],
        compiler_params=params(),
        cost_estimate=cost(
            8 * rows * width * width + 8 * rows * length * width, 20 * rows * width + 8 * width * width,
            rows * length * heads,
        ),
        name="attend",
    )(info, *parts, qkv_w, out_w, biases)


def gelu_pair(x):
    size = jnp.abs(x)
    denom = 1.0 + (ERF_P * 2**-0.5) * size
    t = 1.0 / denom
    bell = jnp.exp(-0.5 * (x * x))
    poly = ERF_A[4]
    for coef in ERF_A[3::-1]:
        poly = poly * t + coef
    tail = (0.5 * poly) * t * bell
    cdf = jnp.where(x >= 0.0, 1.0 - tail, tail)
    return x * cdf, cdf + x * bell * (0.5 / jnp.pi) ** 0.5


def feed_kernel(info, normed, up_w, up_b, down_w, gains, biases, pool_w, class_w, class_b, *outs):
    middle_out, act, slope, normed_two, scale_two, record = outs[:6]
    finals = outs[6:]
    chunks = len(finals)
    span = finals[0].shape[1]
    own = info[0]
    middle = normed[...] * gains[0:1, :] + biases[3:4, :]
    middle_out[...] = middle.astype(bf16)
    hidden = up_w.shape[1]
    tile = 256
    for j in range(hidden // tile):
        cols = slice(j * tile, (j + 1) * tile)
        pre = nn(middle_out[...], up_w[:, cols]) + up_b[:, cols]
        value, grad = gelu_pair(pre)
        act[:, cols] = value.astype(bf16)
        slope[:, cols] = grad.astype(bf16)
    branch = nn(act[...], down_w[...]) + biases[4:5, :]
    middle = normed[...] * gains[0:1, :] + biases[3:4, :]
    n_two, q_two = row_stats(middle + branch)
    normed_two[...] = n_two
    scale_two[...] = q_two
    for c in range(chunks):
        rows = slice(c * span, (c + 1) * span)
        finals[c][0] = (normed_two[rows, :] * gains[1:2, :] + biases[5:6, :]).astype(bf16)
    label = info[1 + pl.num_programs(0) + pl.program_id(0)]
    start = pl.multiple_of(own * span, 8)
    first = (normed_two[pl.ds(start, REC), :] * gains[1:2, :] + biases[5:6, :]).astype(bf16)
    pooled = jnp.tanh(nn(first, pool_w[...]) + biases[6:7, :])
    logits = fine_dot(nt, pooled, class_w[...]) + class_b[...]
    expo = jnp.exp(logits - jnp.max(logits, axis=1, keepdims=True))
    lane = lax.broadcasted_iota(jnp.int32, logits.shape, 1)
    g_logits = expo / jnp.sum(expo, axis=1, keepdims=True) - jnp.where(lane == label, 1.0, 0.0)
    g_pre = fine_dot(nn, g_logits, class_w[...]) * (1.0 - pooled * pooled)
    g_first = fine_dot(nt, g_pre, pool_w[...])
    record[...] = jnp.zeros_like(record)
    record[0:1, :] = first.astype(f32)[0:1, :]
    record[1:2, :] = g_pre[0:1, :]
    record[2:3, :] = pooled[0:1, :]
    record[3:4, :] = g_first[0:1, :]
    lanes = logits.shape[1]
    record[4:5, :lanes] = logits[0:1, :]
    record[5:6, :lanes] = g_logits[0:1, :]


def feed(info, normed, up_w, up_b, down_w, gains, biases, pool_w, class_w, class_b, per, chunks):
    rows, width = normed.shape
    length = rows // per
    span = length // chunks
    hidden = up_w.shape[1]
    by_seq = lambda i: (i, 0)
    consts = (up_w, up_b, down_w, gains, biases, pool_w, class_w, class_b)
    return pl.pallas_call(
        feed_kernel,
        grid=(per,),
        in_specs=[smem(), pl.BlockSpec((length, width), by_seq)] + [whole(a.shape) for a in consts],
        out_specs=[
            pl.BlockSpec((length, width), by_seq),
            pl.BlockSpec((length, hidden), by_seq),
            pl.BlockSpec((length, hidden), by_seq),
            pl.BlockSpec((length, width), by_seq),
            pl.BlockSpec((length, 1), by_seq),
            pl.BlockSpec((REC, width), by_seq),
        ]
        + [pl.BlockSpec((1, span, width), lambda i: (i, 0, 0))] * chunks,
        out_shape=[
            jax.ShapeDtypeStruct((rows, width), bf16),
            jax.ShapeDtypeStruct((rows, hidden), bf16),
            jax.ShapeDtypeStruct((rows, hidden), bf16),
            jax.ShapeDtypeStruct((rows, width), f32),
            jax.ShapeDtypeStruct((rows, 1), f32),
            jax.ShapeDtypeStruct((per * REC, width), f32),
        ]
        + [jax.ShapeDtypeStruct((per, span, width), bf16)] * chunks,
        compiler_params=params(),
        cost_estimate=cost(4 * rows * width * hidden, 4 * rows * hidden + 4 * width * hidden + 12 * rows * width),
        name="feed",
    )(info, normed, *consts)


def norm_back(upper, normed, scale, gain):
    scaled = upper * gain
    mean_part = jnp.mean(scaled, axis=-1, keepdims=True)
    proj_part = jnp.mean(scaled * normed, axis=-1, keepdims=True)
    return scale * (scaled - mean_part - normed * proj_part)


def col_sum(values):
    return jnp.sum(values, axis=0, keepdims=True)


def feed_back_kernel(info, *refs):
    chunks = len(refs) - 17
    cots = refs[:chunks]
    record, n_two, q_two, slope, down_w, up_w, out_w, n_one, q_one, gains = refs[chunks : chunks + 10]
    branch_grad, pre_grad, grad_one, mix_grad, context_grad, sums, up_sums = refs[chunks + 10 :]
    span = cots[0].shape[1]
    length = chunks * span
    own = info[0]

    @pl.when(pl.program_id(0) == 0)
    def _():
        sums[...] = jnp.zeros_like(sums)
        up_sums[...] = jnp.zeros_like(up_sums)

    cot = jnp.concatenate([part[0] for part in cots], axis=0).astype(f32)
    row = lax.broadcasted_iota(jnp.int32, (length, 1), 0)
    g_final = cot + jnp.where(row == own * span, record[3:4, :], 0.0)
    normed = n_two[...]
    sums[0:1, :] += col_sum(g_final * normed)
    sums[2:3, :] += col_sum(g_final)
    g_two = norm_back(g_final, normed, q_two[...], gains[1:2, :])
    branch_grad[...] = g_two.astype(bf16)
    sums[1:2, :] += col_sum(branch_grad[...].astype(f32))
    grad_one[...] = g_two
    hidden = up_w.shape[1]
    tile = 256
    for j in range(hidden // tile):
        cols = slice(j * tile, (j + 1) * tile)
        pre = nt(branch_grad[...], down_w[cols, :]) * slope[:, cols].astype(f32)
        low = pre.astype(bf16)
        pre_grad[:, cols] = low
        up_sums[:, cols] += col_sum(low.astype(f32))
    g_middle = grad_one[...] + nt(pre_grad[...], up_w[...])
    normed = n_one[...]
    sums[3:4, :] += col_sum(g_middle * normed)
    sums[5:6, :] += col_sum(g_middle)
    g_one = norm_back(g_middle, normed, q_one[...], gains[0:1, :])
    grad_one[...] = g_one
    mix_grad[...] = g_one.astype(bf16)
    sums[4:5, :] += col_sum(mix_grad[...].astype(f32))
    context_grad[...] = nt(mix_grad[...], out_w[...]).astype(bf16)


def feed_back(info, cots, record, n_two, q_two, slope, down_w, up_w, out_w, n_one, q_one, gains):
    chunks = len(cots)
    per, span, width = cots[0].shape
    rows, hidden = slope.shape
    length = rows // per
    by_seq = lambda i: (i, 0)
    row_block = pl.BlockSpec((length, width), by_seq)
    wide_block = pl.BlockSpec((length, hidden), by_seq)
    thin_block = pl.BlockSpec((length, 1), by_seq)
    return pl.pallas_call(
        feed_back_kernel,
        grid=(per,),
        in_specs=[smem()]
        + [pl.BlockSpec((1, span, width), lambda i: (i, 0, 0))] * chunks
        + [
            pl.BlockSpec((REC, width), by_seq),
            row_block,
            thin_block,
            wide_block,
            whole(down_w.shape),
            whole(up_w.shape),
            whole(out_w.shape),
            row_block,
            thin_block,
            whole(gains.shape),
        ],
        out_specs=[row_block, wide_block, row_block, row_block, row_block, whole((8, width)), whole((1, hidden))],
        out_shape=[
            jax.ShapeDtypeStruct((rows, width), bf16),
            jax.ShapeDtypeStruct((rows, hidden), bf16),
            jax.ShapeDtypeStruct((rows, width), f32),
            jax.ShapeDtypeStruct((rows, width), bf16),
            jax.ShapeDtypeStruct((rows, width), bf16),
            jax.ShapeDtypeStruct((8, width), f32),
            jax.ShapeDtypeStruct((1, hidden), f32),
        ],
        compiler_params=params(),
        cost_estimate=cost(
            4 * rows * width * hidden + 2 * rows * width * width,
            4 * rows * hidden + 4 * width * hidden + 20 * rows * width,
        ),
        name="feed_back",
    )(info, *cots, record, n_two, q_two, slope, down_w, up_w, out_w, n_one, q_one, gains)


def attend_back_kernel(info, queries_in, keys_in, values_in, context_grad, context, lse, grads, sums, *, chunks):
    length = queries_in.shape[0]
    span = length // chunks
    own = info[0]
    i = pl.program_id(0)
    live_len = info[1 + pl.program_id(1)]
    factor = HEAD_DIM**-0.5
    lane = lax.broadcasted_iota(jnp.int32, (length, PAIR), 1)
    row = lax.broadcasted_iota(jnp.int32, (length, PAIR), 0)
    pos = ((row // span) ^ own) * span + row % span
    key_ext = jnp.where((lane == 0) & (pos >= live_len), neg_big, 0.0).astype(bf16)
    query_ext = jnp.where(lane == 0, 1.0, 0.0).astype(bf16)
    low_half = lane < HEAD_DIM
    masks = [jnp.where(low_half, 1.0, 0.0).astype(bf16), jnp.where(low_half, 0.0, 1.0).astype(bf16)]
    queries = queries_in[...] * bf16(factor)
    keys = jnp.concatenate([keys_in[...], key_ext], axis=1)
    values = values_in[...]
    ctx_grad = context_grad[...]
    product = ctx_grad.astype(f32) * context[...].astype(f32)
    picks = jnp.where(
        lax.broadcasted_iota(jnp.int32, (8, PAIR), 1) // HEAD_DIM
        == lax.broadcasted_iota(jnp.int32, (8, PAIR), 0),
        1.0,
        0.0,
    ).astype(bf16)
    high = product.astype(bf16)
    low = (product - high.astype(f32)).astype(bf16)
    row_dots = nt(picks, high) + nt(picks, low)
    block = length // 2
    g_queries = None
    g_keys = [None, None]
    g_values = [None, None]
    for head in range(2):
        masked_q = queries * masks[head]
        long_q = jnp.concatenate([masked_q, query_ext], axis=1)
        masked_g = ctx_grad * masks[head]
        log_total = lse[0, pl.ds(2 * i + head, 1), :]
        row_dot = row_dots[head : head + 1, :]
        for c in range(2):
            rows = slice(c * block, (c + 1) * block)
            weights = jnp.exp(nt(keys[rows], long_q) - log_total)
            part = nn(weights.astype(bf16), masked_g)
            g_values[c] = part if g_values[c] is None else g_values[c] + part
            g_scores = (weights * (nt(values[rows], masked_g) - row_dot)).astype(bf16)
            part = nn(g_scores, masked_q)
            g_keys[c] = part if g_keys[c] is None else g_keys[c] + part
            part = tn(g_scores, keys_in[rows, :] * masks[head][rows])
            g_queries = part if g_queries is None else g_queries + part
    grads[0] = (g_queries * factor).astype(bf16)
    for c in range(2):
        rows = slice(c * block, (c + 1) * block)
        grads[1, rows, :] = g_keys[c].astype(bf16)
        grads[2, rows, :] = g_values[c].astype(bf16)

    @pl.when(pl.program_id(1) == 0)
    def _():
        sums[...] = jnp.zeros_like(sums)

    sums[0:1, :] += col_sum(grads[0].astype(f32))
    sums[1:2, :] += col_sum(grads[2].astype(f32))


def attend_back(info, qkv, context_grad, context, lse, chunks):
    rows, width = context.shape
    per, head_rows, length = lse.shape
    pairs = width // PAIR
    spec = lambda third: pl.BlockSpec((length, PAIR), lambda i, q: (q, third * pairs + i))
    return pl.pallas_call(
        functools.partial(attend_back_kernel, chunks=chunks),
        grid=(pairs, per),
        in_specs=[
            smem(),
            spec(0),
            spec(1),
            spec(2),
            spec(0),
            spec(0),
            pl.BlockSpec((1, head_rows, length), lambda i, q: (q, 0, 0)),
        ],
        out_specs=[
            pl.BlockSpec((3, length, PAIR), lambda i, q: (0, q, i)),
            pl.BlockSpec((8, PAIR), lambda i, q: (0, i)),
        ],
        out_shape=[jax.ShapeDtypeStruct((3, rows, width), bf16), jax.ShapeDtypeStruct((8, width), f32)],
        compiler_params=params(),
        cost_estimate=cost(20 * rows * length * width, 16 * rows * width, rows * length * width // HEAD_DIM),
        name="attend_back",
    )(info, qkv, qkv, qkv, context_grad, context, lse)


def input_grad_kernel(grads, qkv_w, grad_one, *outs):
    width = grad_one.shape[1]
    total = grad_one[...]
    for third in range(3):
        total = total + nt(grads[third], qkv_w[:, third * width : (third + 1) * width])
    span = outs[0].shape[1]
    for c, out in enumerate(outs):
        out[0] = total[c * span : (c + 1) * span].astype(bf16)


def input_grad(grads, qkv_w, grad_one, per, chunks):
    _, rows, width = grads.shape
    length = rows // per
    span = length // chunks
    return pl.pallas_call(
        input_grad_kernel,
        grid=(per,),
        in_specs=[
            pl.BlockSpec((3, length, width), lambda i: (0, i, 0)),
            whole(qkv_w.shape),
            pl.BlockSpec((length, width), lambda i: (i, 0)),
        ],
        out_specs=[pl.BlockSpec((1, span, width), lambda i: (i, 0, 0))] * chunks,
        out_shape=[jax.ShapeDtypeStruct((per, span, width), bf16)] * chunks,
        compiler_params=params(),
        cost_estimate=cost(6 * rows * width * width, 12 * rows * width + 6 * width * width),
        name="input_grad",
    )(grads, qkv_w, grad_one)


def weight_grad_kernel(info, left, right, keep, send, left_t, total, *, order, chunk):
    @pl.when(pl.program_id(0) == 0)
    def _():
        left_t[...] = jnp.transpose(left[...])

    rights = right[0] if len(right.shape) == 3 else right[...]
    total[...] = nn(left_t[...], rights)
    me = info[0]
    half = len(order) // 2
    for at in range(0, len(order), 2):
        rows = jnp.concatenate(
            [total[pl.ds(pl.multiple_of((me ^ order[at + k]) * chunk, 8), chunk), :] for k in range(2)], axis=0
        )
        target = keep if at < half else send
        row = (at % half) * chunk
        target[row : row + 2 * chunk, :] = rows.astype(bf16)


def weight_grad(me, left, right, order, tile):
    rows, depth = left.shape
    parts = right.shape[0] if right.ndim == 3 else 1
    width = right.shape[-1]
    chunk = depth // len(order)
    each = width // tile
    if right.ndim == 3:
        spec = pl.BlockSpec((1, rows, tile), lambda j: (j // each, 0, j % each))
    else:
        spec = pl.BlockSpec((rows, tile), lambda j: (0, j))
    return pl.pallas_call(
        functools.partial(weight_grad_kernel, order=order, chunk=chunk),
        grid=(parts * each,),
        in_specs=[smem(), pl.BlockSpec((rows, depth), lambda j: (0, 0)), spec],
        out_specs=[pl.BlockSpec((depth // 2, tile), lambda j: (0, j))] * 2,
        out_shape=[jax.ShapeDtypeStruct((depth // 2, parts * width), bf16)] * 2,
        scratch_shapes=[pltpu.VMEM((depth, rows), bf16), pltpu.VMEM((depth, tile), f32)],
        compiler_params=params(),
        cost_estimate=cost(
            2 * rows * depth * parts * width, 2 * rows * (depth + parts * width) + 2 * depth * parts * width
        ),
        name="weight_grad",
    )(me, left, right)


def halving_order(stages, n_seq):
    bits = [bit * (n_seq if axis == "dp" else 1) for axis, bit in stages]
    count = len(bits)
    return [
        sum(bit for at, bit in enumerate(bits) if (place >> (count - 1 - at)) & 1) for place in range(1 << count)
    ]


def halving_sum(keep, send, stages):
    for at, (axis, bit) in enumerate(stages):
        size = lax.axis_size(axis)
        got = lax.ppermute(send, axis, [(i, i ^ bit) for i in range(size)])
        if at == len(stages) - 1:
            return keep.astype(f32) + got.astype(f32)
        half = keep.shape[0] // 2
        send = (keep[half:].astype(f32) + got[half:].astype(f32)).astype(bf16)
        keep = (keep[:half].astype(f32) + got[:half].astype(f32)).astype(bf16)


def summed_grad(me, left, right, stages, tile):
    n_seq = lax.axis_size("seq")
    n_all = lax.axis_size("dp") * n_seq
    if left.shape[1] % (8 * n_all):
        wide = jnp.concatenate(list(right), axis=1) if right.ndim == 3 else right
        return lax.psum_scatter(tn(left, wide), ("dp", "seq"), scatter_dimension=0, tiled=True)
    keep, send = weight_grad(me, left, right, halving_order(stages, n_seq), tile)
    return halving_sum(keep, send, stages)


def bits_of(size):
    return [1 << k for k in range(size.bit_length() - 1)]


def shards(
    hidden_in,
    lengths,
    labels,
    out_cotangent,
    qkv_weight,
    out_weight,
    up_weight,
    down_weight,
    pool_weight,
    class_weight,
    norm_gains,
    biases,
    up_bias,
    class_bias,
):
    positions, group, width = hidden_in.shape
    n_seq = lax.axis_size("seq")
    n_dp = lax.axis_size("dp")
    n_all = n_seq * n_dp
    seq_at = lax.axis_index("seq")
    me = lax.axis_index("dp") * n_seq + seq_at
    per = group // n_seq
    own_lengths = lax.dynamic_slice_in_dim(lengths, seq_at * per, per)
    info = jnp.concatenate([seq_at[None].astype(jnp.int32), own_lengths, labels])
    me_info = me[None].astype(jnp.int32)
    classes = class_weight.shape[1]
    class_rows = jnp.zeros((128, width), bf16).at[:classes].set(class_weight.T)
    class_shift = jnp.full((1, 128), neg_big, f32).at[0, :classes].set(class_bias)

    x_parts = exchange(split_rows(info, hidden_in.reshape(positions * group, width), positions, group, n_seq))
    cots = exchange(split_rows(info, out_cotangent.reshape(positions * group, width), positions, group, n_seq))

    x_rows, qkv, context, lse, n_one, q_one = attend(info, x_parts, qkv_weight, out_weight, biases)
    outs = feed(
        info, n_one, up_weight, up_bias[None, :], down_weight, norm_gains, biases, pool_weight,
        class_rows, class_shift, per, n_seq,
    )
    middle_low, act, slope, n_two, q_two, record = outs[:6]
    hidden_out = merge_rows(info, exchange(outs[6:]), bf16)

    branch_grad, pre_grad, grad_one, mix_grad, context_grad, sums, up_sums = feed_back(
        info, cots, record, n_two, q_two, slope, down_weight, up_weight, out_weight, n_one, q_one, norm_gains
    )
    seq_bits = [("seq", b) for b in bits_of(n_seq)]
    dp_bits = [("dp", b) for b in bits_of(n_dp)]
    by_dp = seq_bits[:1] + dp_bits[:1] + seq_bits[1:] + dp_bits[1:]
    by_seq = seq_bits + dp_bits
    down_sum = summed_grad(me_info, act, branch_grad, by_dp, 256)
    up_sum = summed_grad(me_info, middle_low, pre_grad, by_seq, 512)
    grads, qkv_sums = attend_back(info, qkv, context_grad, context, lse, n_seq)
    out_sum = summed_grad(me_info, context, mix_grad, by_seq, 384)
    qkv_sum = summed_grad(me_info, x_rows, grads, by_dp, 384)
    grad_in = merge_rows(info, exchange(input_grad(grads, qkv_weight, grad_one, per, n_seq)), f32)

    chunk = width // n_all
    vectors = jnp.concatenate([sums[:6], qkv_sums[:2]], axis=0).reshape(8, n_all, chunk)
    vectors = jnp.concatenate(
        [jnp.transpose(vectors, (1, 0, 2)).reshape(n_all, 8 * chunk), up_sums.reshape(n_all, -1)], axis=1
    )
    vector_sum = lax.psum_scatter(vectors, ("dp", "seq"), scatter_dimension=0, tiled=True)[0]
    vec = vector_sum[: 8 * chunk].reshape(8, chunk)
    up_bias_sum = vector_sum[8 * chunk :]

    records = lax.all_gather(record, ("dp", "seq"), axis=0, tiled=True).reshape(n_all * per, REC, width)
    mine = lax.dynamic_slice_in_dim(records, me * chunk, chunk, axis=2)
    g_logits_all = records[:, 5, :classes]
    pool_sum = lax.dot_general(mine[:, 0], records[:, 1], (((0,), (0,)), ((), ())), precision=highest)
    class_sum = lax.dot_general(mine[:, 2], g_logits_all, (((0,), (0,)), ((), ())), precision=highest)
    pool_bias_sum = jnp.sum(mine[:, 1], axis=0)
    class_bias_sum = jnp.sum(g_logits_all, axis=0)
    ramp_logits = record.reshape(per, REC, width)[:, 4, :classes]

    gains_sum = jnp.stack([vec[3], vec[0]])
    biases_sum = jnp.stack([vec[6], vec[7], vec[4], vec[5], vec[1], vec[2], pool_bias_sum])
    return (
        hidden_out.reshape(positions, group, width),
        ramp_logits,
        grad_in.reshape(positions, group, width),
        qkv_sum,
        out_sum,
        up_sum,
        down_sum,
        pool_sum,
        class_sum,
        gains_sum,
        biases_sum,
        up_bias_sum,
        class_bias_sum,
    )


def solution(mesh):
    every = ("dp", "seq")
    rows = P("seq", "dp", None)
    return jax.shard_map(
        shards,
        mesh=mesh,
        in_specs=(rows, P("dp"), P(every), rows) + (P(),) * 10,
        out_specs=(
            rows,
            P(every, None),
            rows,
            P(every, None),
            P(every, None),
            P(every, None),
            P(every, None),
            P(every, None),
            P(every, None),
            P(None, every),
            P(None, every),
            P(every),
            P(),
        ),
        check_vma=False,
    )
```

```python
import functools

import jax
import jax.numpy as jnp
from jax import lax
from jax.experimental import pallas as pl
from jax.experimental.pallas import tpu as pltpu
from jax.sharding import PartitionSpec as P

HEAD_DIM = 64
PAIR = 2 * HEAD_DIM
REC = 8
CLASSES = 3
FEED_PARTS = 2

eps = 1e-12
neg_big = -1e30
highest = lax.Precision.HIGHEST
f32 = jnp.float32
bf16 = jnp.bfloat16
MIB = 1 << 20


def nn(left, right):
    return lax.dot_general(left, right, (((1,), (0,)), ((), ())), preferred_element_type=f32)


def nt(left, right):
    return lax.dot_general(left, right, (((1,), (1,)), ((), ())), preferred_element_type=f32)


def tn(left, right):
    return lax.dot_general(left, right, (((0,), (0,)), ((), ())), preferred_element_type=f32)


def cost(flops, nbytes, trans=0):
    return pl.CostEstimate(flops=1, bytes_accessed=1, transcendentals=0)


def smem():
    return pl.BlockSpec(memory_space=pltpu.SMEM)


def in_vmem():
    return pl.BlockSpec(memory_space=pltpu.VMEM)


def fixed(shape):
    return pl.BlockSpec(shape, lambda *_: (0,) * len(shape))


def run(kernel, after, operands, in_specs, limit, out_shape, aliases=None, loose=(), **kwargs):
    skip = len(after)
    operands = [
        a
        if k in loose or spec.memory_space in (pltpu.VMEM, pltpu.SMEM)
        else pltpu.with_memory_space_constraint(a, pltpu.HBM)
        for k, (a, spec) in enumerate(zip(operands, in_specs, strict=True))
    ]
    after = [pltpu.with_memory_space_constraint(a, pltpu.HBM) for a in after]
    single = not isinstance(out_shape, list)
    shapes = [pltpu.HBM(a.shape, a.dtype) for a in ([out_shape] if single else out_shape)]

    def body(*refs):
        kernel(*refs[skip:])

    return pl.pallas_call(
        body,
        in_specs=[pl.BlockSpec(memory_space=pl.ANY)] * skip + list(in_specs),
        out_shape=shapes[0] if single else shapes,
        input_output_aliases={k + skip: v for k, v in (aliases or {}).items()},
        compiler_params=pltpu.CompilerParams(vmem_limit_bytes=limit * MIB),
        **kwargs,
    )(*after, *operands)


def three_parts(value):
    hi = value.astype(bf16)
    rest = value - hi.astype(f32)
    mid = rest.astype(bf16)
    low = (rest - mid.astype(f32)).astype(bf16)
    return jnp.concatenate([hi, mid, low], axis=0)


def fine_dot(dot, value, weight):
    rows = value.shape[0]
    parts = dot(jnp.concatenate([three_parts(value)], axis=0), weight)
    return parts[:rows] + parts[rows : 2 * rows] + parts[2 * rows :]


def split_kernel(info, rows, *outs):
    chunks = len(outs)
    per, span, _ = outs[0].shape
    group = chunks * per
    block = 16 * group
    own = info[0]
    dest = lax.broadcasted_iota(jnp.int32, (block, block), 0)
    source = lax.broadcasted_iota(jnp.int32, (block, block), 1)
    chunk = dest // (16 * per)
    wanted = (dest % 16) * group + per * (chunk ^ own) + (dest // 16) % per
    perm = jnp.where(source == wanted, 1.0, 0.0).astype(bf16)
    for b in range(span // 16):
        moved = nn(perm, rows[b * block : (b + 1) * block, :]).astype(bf16)
        for c in range(chunks):
            for q in range(per):
                at = (c * per + q) * 16
                outs[c][q, b * 16 : (b + 1) * 16, :] = moved[at : at + 16]


def split_rows(info, rows, positions, group, chunks, after=()):
    width = rows.shape[1]
    per = group // chunks
    steps = 2
    span = positions // steps
    return run(
        split_kernel,
        after,
        (info, rows),
        [smem(), pl.BlockSpec((span * group, width), lambda i: (i, 0))],
        16,
        grid=(steps,),
        out_specs=[pl.BlockSpec((per, span, width), lambda i: (0, i, 0))] * chunks,
        out_shape=[jax.ShapeDtypeStruct((per, positions, width), bf16)] * chunks,
        cost_estimate=cost(2 * rows.size * 16 * group, 4 * rows.size),
        name="split_rows",
    )


def merge_kernel(info, *refs):
    ins, out = refs[:-1], refs[-1]
    chunks = len(ins)
    per, span, _ = ins[0].shape
    group = chunks * per
    block = 16 * group
    own = info[0]
    dest = lax.broadcasted_iota(jnp.int32, (block, block), 0)
    source = lax.broadcasted_iota(jnp.int32, (block, block), 1)
    seq = dest % group
    wanted = (((seq // per) ^ own) * per + seq % per) * 16 + dest // group
    perm = jnp.where(source == wanted, 1.0, 0.0).astype(bf16)
    for b in range(span // 16):
        rows = jnp.concatenate(
            [ins[c][q, b * 16 : (b + 1) * 16, :] for c in range(chunks) for q in range(per)], axis=0
        )
        out[b * block : (b + 1) * block, :] = nn(perm, rows).astype(out.dtype)


def merge_rows(info, parts, dtype, after=()):
    chunks = len(parts)
    per, positions, width = parts[0].shape
    group = per * chunks
    steps = 2
    span = positions // steps
    return run(
        merge_kernel,
        after,
        (info, *parts),
        [smem()] + [pl.BlockSpec((per, span, width), lambda i: (0, i, 0))] * chunks,
        16,
        grid=(steps,),
        out_specs=pl.BlockSpec((span * group, width), lambda i: (i, 0)),
        out_shape=jax.ShapeDtypeStruct((positions * group, width), dtype),
        cost_estimate=cost(2 * positions * group * width * 16 * group, 6 * positions * group * width),
        name="merge_rows",
    )


def exchange(parts):
    size = lax.axis_size("seq")
    return [parts[0]] + [
        lax.ppermute(parts[c], "seq", [(i, i ^ c) for i in range(size)]) for c in range(1, size)
    ]


def row_stats(resid):
    mean = jnp.mean(resid, axis=-1, keepdims=True)
    centred = resid - mean
    scale = lax.rsqrt(jnp.mean(centred * centred, axis=-1, keepdims=True) + eps)
    return centred * scale, scale


def attend_kernel(info, lengths, *refs):
    chunks = len(refs) - 10
    parts = refs[:chunks]
    qkv_w, out_w, biases, x_out, qkv, context, lse, normed, scale, stats = refs[chunks:]
    width = out_w.shape[0]
    span = parts[0].shape[1]
    length = chunks * span
    pairs = width // PAIR
    own = info[0]
    live_len = lengths[own * pl.num_programs(0) + pl.program_id(0)]
    x_out[...] = jnp.concatenate([part[0] for part in parts], axis=0)
    for third in range(3):
        cols = slice(third * width, (third + 1) * width)
        block = nn(x_out[...], qkv_w[:, cols])
        if third == 0:
            block = block + biases[0:1, :]
        elif third == 2:
            block = block + biases[1:2, :]
        qkv[:, cols] = block.astype(bf16)
    lane = lax.broadcasted_iota(jnp.int32, (length, PAIR), 1)
    row = lax.broadcasted_iota(jnp.int32, (length, PAIR), 0)
    pos = ((row // span) ^ own) * span + row % span
    key_ext = jnp.where((lane == 0) & (pos >= live_len), neg_big, 0.0).astype(bf16)
    query_ext = jnp.where(lane == 0, 1.0, 0.0).astype(bf16)
    low_half = lane < HEAD_DIM
    masks = [jnp.where(low_half, 1.0, 0.0).astype(bf16), jnp.where(low_half, 0.0, 1.0).astype(bf16)]
    stats[...] = jnp.zeros_like(stats)

    def one_pair(i, carry):
        start = pl.multiple_of(i * PAIR, PAIR)
        queries = qkv[:, pl.ds(start, PAIR)] * bf16(HEAD_DIM**-0.5)
        keys = jnp.concatenate([qkv[:, pl.ds(start + width, PAIR)], key_ext], axis=1)
        values = qkv[:, pl.ds(start + 2 * width, PAIR)]
        total = None
        tops = []
        for head in range(2):
            scores = nt(jnp.concatenate([queries * masks[head], query_ext], axis=1), keys)
            top = jnp.max(scores, axis=1, keepdims=True)
            weights = jnp.exp(scores - top).astype(bf16)
            part = nn(weights, jnp.concatenate([values * masks[head], masks[head]], axis=1))
            total = part if total is None else total + part
            tops.append(top)
        row_total = total[:, PAIR:]
        context[:, pl.ds(start, PAIR)] = (total[:, :PAIR] / row_total).astype(bf16)
        log_total = jnp.where(low_half, tops[0], tops[1]) + jnp.log(row_total)
        swapped = pltpu.roll(log_total, HEAD_DIM, 1)
        stats[...] = jnp.where(
            lane == 2 * i, log_total, jnp.where(lane == 2 * i + 1, swapped, stats[...])
        )
        return carry

    lax.fori_loop(0, pairs, one_pair, 0, unroll=pairs)
    lse[0] = jnp.transpose(stats[...])[: lse.shape[1], :]
    resid = x_out[...].astype(f32) + (nn(context[...], out_w[...]) + biases[2:3, :])
    n_one, q_one = row_stats(resid)
    normed[...] = n_one
    scale[...] = q_one


def attend(info, lengths, parts, qkv_w, out_w, biases, after=()):
    chunks = len(parts)
    per, span, width = parts[0].shape
    length = chunks * span
    rows = per * length
    heads = width // HEAD_DIM
    head_rows = -(-heads // 8) * 8
    by_seq = lambda i: (i, 0)
    return run(
        attend_kernel,
        after,
        (info, lengths, *parts, qkv_w, out_w, biases),
        [smem()] * 2
        + [pl.BlockSpec((1, span, width), lambda i: (i, 0, 0))] * chunks
        + [in_vmem()] * 3,
        40,
        grid=(per,),
        out_specs=[
            pl.BlockSpec((length, width), by_seq),
            pl.BlockSpec((length, 3 * width), by_seq),
            pl.BlockSpec((length, width), by_seq),
            pl.BlockSpec((1, head_rows, length), lambda i: (i, 0, 0)),
            pl.BlockSpec((length, width), by_seq),
            pl.BlockSpec((length, 1), by_seq),
        ],
        out_shape=[
            jax.ShapeDtypeStruct((rows, width), bf16),
            jax.ShapeDtypeStruct((rows, 3 * width), bf16),
            jax.ShapeDtypeStruct((rows, width), bf16),
            jax.ShapeDtypeStruct((per, head_rows, length), f32),
            jax.ShapeDtypeStruct((rows, width), f32),
            jax.ShapeDtypeStruct((rows, 1), f32),
        ],
        scratch_shapes=[pltpu.VMEM((length, PAIR), f32)],
        cost_estimate=cost(
            8 * rows * width * width + 8 * rows * length * width, 20 * rows * width + 8 * width * width,
            rows * length * heads,
        ),
        name="attend",
    )


def gelu_pair(x):
    cdf = 0.5 + 0.5 * lax.erf(x * 0.5**0.5)
    bell = jnp.exp(-0.5 * (x * x))
    return x * cdf, cdf + x * bell * (0.5 / jnp.pi) ** 0.5


def norm_back(upper, normed, scale, gain):
    scaled = upper * gain
    mean_part = jnp.mean(scaled, axis=-1, keepdims=True)
    proj_part = jnp.mean(scaled * normed, axis=-1, keepdims=True)
    return scale * (scaled - mean_part - normed * proj_part)


def col_sum(values):
    return jnp.sum(values, axis=0, keepdims=True)


def feed_kernel(info, labels, *refs):
    chunks = (len(refs) - 20) // 2
    cots = refs[:chunks]
    normed, up_w, up_b, down_w, gains, biases, pool_w, class_w, class_b = refs[chunks : chunks + 9]
    middle_out, act, slope, grad_two, branch_grad = refs[chunks + 9 : chunks + 14]
    ramp_first, ramp_pre, ramp_out, sums, ramp_sums = refs[chunks + 14 : chunks + 19]
    finals = refs[chunks + 19 : -1]
    n_two = refs[-1]
    span = finals[0].shape[1]
    own = info[0]

    @pl.when(pl.program_id(0) == 0)
    def _():
        sums[...] = jnp.zeros_like(sums)
        ramp_sums[...] = jnp.zeros_like(ramp_sums)

    hidden = up_w.shape[1]
    tile = 256
    length = chunks * span
    block = length // FEED_PARTS
    scales = []
    for part in range(FEED_PARTS):
        rows = slice(part * block, (part + 1) * block)
        middle = normed[rows, :] * gains[0:1, :] + biases[3:4, :]
        middle_out[rows, :] = middle.astype(bf16)
        for j in range(hidden // tile):
            cols = slice(j * tile, (j + 1) * tile)
            pre = nn(middle_out[rows, :], up_w[:, cols]) + up_b[:, cols]
            value, grad = gelu_pair(pre)
            act[rows, cols] = value.astype(bf16)
            slope[rows, cols] = grad.astype(bf16)
        branch = nn(act[rows, :], down_w[...]) + biases[4:5, :]
        middle = normed[rows, :] * gains[0:1, :] + biases[3:4, :]
        normed_two, q_two = row_stats(middle + branch)
        n_two[rows, :] = normed_two
        scales.append(q_two)
    for c in range(chunks):
        rows = slice(c * span, (c + 1) * span)
        finals[c][0] = (n_two[rows, :] * gains[1:2, :] + biases[5:6, :]).astype(bf16)
    label = labels[pl.program_id(0)]
    start = pl.multiple_of(own * span, 8)
    first = (n_two[pl.ds(start, REC), :] * gains[1:2, :] + biases[5:6, :]).astype(bf16)
    pooled = jnp.tanh(nn(first, pool_w[...]) + biases[6:7, :])
    logits = fine_dot(nt, pooled, class_w[...]) + class_b[...]
    expo = jnp.exp(logits - jnp.max(logits, axis=1, keepdims=True))
    lane = lax.broadcasted_iota(jnp.int32, logits.shape, 1)
    g_logits = expo / jnp.sum(expo, axis=1, keepdims=True) - jnp.where(lane == label, 1.0, 0.0)
    g_pre = fine_dot(nn, g_logits, class_w[...]) * (1.0 - pooled * pooled)
    g_first = fine_dot(nt, g_pre, pool_w[...])
    first_row = lax.broadcasted_iota(jnp.int32, (REC, 1), 0) == 0
    ramp_first[...] = jnp.where(first_row, first.astype(f32), 0.0)
    ramp_pre[...] = jnp.where(first_row, g_pre, 0.0)
    ramp_out[...] = logits
    ramp_sums[1:2, :] += g_pre[0:1, :]
    for c in range(CLASSES):
        at_class = jnp.sum(jnp.where(lane == c, g_logits, 0.0), axis=1, keepdims=True)[0:1, :]
        ramp_sums[2 + c : 3 + c, :] += at_class * pooled[0:1, :]
        ramp_sums[2 + CLASSES + c : 3 + CLASSES + c, :] += at_class + jnp.zeros_like(pooled[0:1, :])
    sum_rows = [0.0, 0.0, 0.0]
    for part in range(FEED_PARTS):
        rows = slice(part * block, (part + 1) * block)
        here = cots[part * chunks // FEED_PARTS : (part + 1) * chunks // FEED_PARTS]
        cot = jnp.concatenate([chunk[0] for chunk in here], axis=0).astype(f32)
        row = part * block + lax.broadcasted_iota(jnp.int32, (block, 1), 0)
        g_final = cot + jnp.where(row == own * span, g_first[0:1, :], 0.0)
        normed_two = n_two[rows, :]
        g_two = norm_back(g_final, normed_two, scales[part], gains[1:2, :])
        grad_two[rows, :] = g_two
        low = g_two.astype(bf16)
        branch_grad[rows, :] = low
        for k, values in enumerate((g_final * normed_two, low.astype(f32), g_final)):
            sum_rows[k] = sum_rows[k] + col_sum(values)
    for k in range(3):
        sums[k : k + 1, :] += sum_rows[k]


def feed(info, labels, cots, normed, up_w, up_b, down_w, gains, biases, pool_w, class_w, class_b, after=()):
    chunks = len(cots)
    per, span, _ = cots[0].shape
    rows, width = normed.shape
    length = rows // per
    hidden = up_w.shape[1]
    by_seq = lambda i: (i, 0)
    row_block = pl.BlockSpec((length, width), by_seq)
    wide_block = pl.BlockSpec((length, hidden), by_seq)
    part = pl.BlockSpec((1, span, width), lambda i: (i, 0, 0))
    consts = (up_w, up_b, down_w, gains, biases, pool_w, class_w, class_b)
    return run(
        feed_kernel,
        after,
        (info, labels, *cots, normed, *consts),
        [smem()] * 2 + [part] * chunks + [row_block] + [in_vmem()] * len(consts),
        40,
        grid=(per,),
        out_specs=[
            row_block, wide_block, wide_block, row_block, row_block,
            pl.BlockSpec((REC, width), by_seq), pl.BlockSpec((REC, width), by_seq),
            pl.BlockSpec((REC, class_b.shape[1]), by_seq), fixed((8, width)), fixed((8, width)),
        ]
        + [part] * chunks,
        out_shape=[
            jax.ShapeDtypeStruct((rows, width), bf16),
            jax.ShapeDtypeStruct((rows, hidden), bf16),
            jax.ShapeDtypeStruct((rows, hidden), bf16),
            jax.ShapeDtypeStruct((rows, width), f32),
            jax.ShapeDtypeStruct((rows, width), bf16),
            jax.ShapeDtypeStruct((per * REC, width), f32),
            jax.ShapeDtypeStruct((per * REC, width), f32),
            jax.ShapeDtypeStruct((per * REC, class_b.shape[1]), f32),
            jax.ShapeDtypeStruct((8, width), f32),
            jax.ShapeDtypeStruct((8, width), f32),
        ]
        + [jax.ShapeDtypeStruct((per, span, width), bf16)] * chunks,
        scratch_shapes=[pltpu.VMEM((length, width), f32)],
        cost_estimate=cost(4 * rows * width * hidden, 4 * rows * hidden + 4 * width * hidden + 12 * rows * width),
        name="feed",
    )


def feed_back_kernel(*refs, carried):
    grad_two, branch_grad, slope, n_one, q_one, down_w, up_w, out_w, gains = refs[:9]
    pre_grad, grad_one, mix_grad, context_grad, sums, up_sums = refs[9 + carried :]

    @pl.when(pl.program_id(0) == 0)
    def _():
        sums[...] = jnp.zeros_like(sums)
        up_sums[...] = jnp.zeros_like(up_sums)

    hidden = up_w.shape[1]
    tile = 256
    for j in range(hidden // tile):
        cols = slice(j * tile, (j + 1) * tile)
        pre = nt(branch_grad[...], down_w[cols, :]) * slope[:, cols].astype(f32)
        low = pre.astype(bf16)
        pre_grad[:, cols] = low
        up_sums[:, cols] += col_sum(low.astype(f32))
    g_middle = grad_two[...] + nt(pre_grad[...], up_w[...])
    normed = n_one[...]
    sums[0:1, :] += col_sum(g_middle * normed)
    sums[2:3, :] += col_sum(g_middle)
    g_one = norm_back(g_middle, normed, q_one[...], gains[0:1, :])
    grad_one[...] = g_one
    mix_grad[...] = g_one.astype(bf16)
    sums[1:2, :] += col_sum(mix_grad[...].astype(f32))
    context_grad[...] = nt(mix_grad[...], out_w[...]).astype(bf16)


def feed_back(at, per, grad_two, branch_grad, slope, n_one, q_one, down_w, up_w, out_w, gains, before, after=()):
    rows, width = grad_two.shape
    hidden = slope.shape[1]
    steps = 2
    block = rows // per // steps
    by_row = lambda i: (at * steps + i, 0)
    row_block = pl.BlockSpec((block, width), by_row)
    wide_block = pl.BlockSpec((block, hidden), by_row)
    thin_block = pl.BlockSpec((block, 1), by_row)
    return run(
        functools.partial(feed_back_kernel, carried=len(before)),
        after,
        (grad_two, branch_grad, slope, n_one, q_one, down_w, up_w, out_w, gains, *before),
        [row_block, row_block, wide_block, row_block, thin_block]
        + [in_vmem()] * 4
        + [pl.BlockSpec(memory_space=pl.ANY)] * len(before),
        32,
        aliases={9 + k: k for k in range(len(before))},
        grid=(steps,),
        out_specs=[wide_block, row_block, row_block, row_block, fixed((8, width)), fixed((1, hidden))],
        out_shape=[
            jax.ShapeDtypeStruct((rows, hidden), bf16),
            jax.ShapeDtypeStruct((rows, width), f32),
            jax.ShapeDtypeStruct((rows, width), bf16),
            jax.ShapeDtypeStruct((rows, width), bf16),
            jax.ShapeDtypeStruct((8, width), f32),
            jax.ShapeDtypeStruct((1, hidden), f32),
        ],
        cost_estimate=cost(
            (4 * rows * width * hidden + 2 * rows * width * width) // per,
            4 * rows * hidden + 4 * width * hidden + 20 * rows * width,
        ),
        name="feed_back",
    )


def attend_back_kernel(info, lengths, queries_in, keys_in, values_in, context_grad, context, lse, grads, sums, *, chunks, first):
    length, cols = queries_in.shape
    span = length // chunks
    own = info[0]
    live_len = lengths[own * pl.num_programs(0) + pl.program_id(0)]
    factor = HEAD_DIM**-0.5
    lane = lax.broadcasted_iota(jnp.int32, (length, PAIR), 1)
    row = lax.broadcasted_iota(jnp.int32, (length, PAIR), 0)
    pos = ((row // span) ^ own) * span + row % span
    key_ext = jnp.where((lane == 0) & (pos >= live_len), neg_big, 0.0).astype(bf16)
    query_ext = jnp.where(lane == 0, 1.0, 0.0).astype(bf16)
    low_half = lane < HEAD_DIM
    masks = [jnp.where(low_half, 1.0, 0.0).astype(bf16), jnp.where(low_half, 0.0, 1.0).astype(bf16)]
    picks = jnp.where(
        lax.broadcasted_iota(jnp.int32, (8, PAIR), 1) // HEAD_DIM
        == lax.broadcasted_iota(jnp.int32, (8, PAIR), 0),
        1.0,
        0.0,
    ).astype(bf16)
    parts = 1
    block = length // parts

    @pl.when(pl.program_id(0) == 0)
    def _():
        sums[...] = jnp.zeros_like(sums)

    for pair in range(cols // PAIR):
        at = slice(pair * PAIR, (pair + 1) * PAIR)
        queries = queries_in[:, at] * bf16(factor)
        keys = jnp.concatenate([keys_in[:, at], key_ext], axis=1)
        values = values_in[:, at]
        ctx_grad = context_grad[:, at]
        product = ctx_grad.astype(f32) * context[:, at].astype(f32)
        high = product.astype(bf16)
        low = (product - high.astype(f32)).astype(bf16)
        row_dots = nt(picks, high) + nt(picks, low)
        g_queries = None
        g_keys = [None] * parts
        g_values = [None] * parts
        for head in range(2):
            masked_q = queries * masks[head]
            long_q = jnp.concatenate([masked_q, query_ext], axis=1)
            masked_g = ctx_grad * masks[head]
            masked_k = keys_in[:, at] * masks[head]
            log_total = lse[0, 2 * (first + pair) + head : 2 * (first + pair) + head + 1, :]
            row_dot = row_dots[head : head + 1, :]
            for c in range(parts):
                rows = slice(c * block, (c + 1) * block)
                weights = jnp.exp(nt(keys[rows], long_q) - log_total)
                part = nn(weights.astype(bf16), masked_g)
                g_values[c] = part if g_values[c] is None else g_values[c] + part
                g_scores = (weights * (nt(values[rows], masked_g) - row_dot)).astype(bf16)
                part = nn(g_scores, masked_q)
                g_keys[c] = part if g_keys[c] is None else g_keys[c] + part
                part = tn(g_scores, masked_k[rows])
                g_queries = part if g_queries is None else g_queries + part
        grads[0, :, at] = (g_queries * factor).astype(bf16)
        for c in range(parts):
            rows = slice(c * block, (c + 1) * block)
            grads[1, rows, at] = g_keys[c].astype(bf16)
            grads[2, rows, at] = g_values[c].astype(bf16)
        sums[0:1, at] += col_sum(grads[0, :, at].astype(f32))
        sums[1:2, at] += col_sum(grads[2, :, at].astype(f32))


def attend_back(info, lengths, qkv, context_grad, context, lse, chunks, first, count, after=()):
    rows, width = context.shape
    per, head_rows, length = lse.shape
    cols = count * PAIR
    blocks = width // cols
    spec = lambda third: pl.BlockSpec((length, cols), lambda q: (q, third * blocks + first // count))
    return run(
        functools.partial(attend_back_kernel, chunks=chunks, first=first),
        after,
        (info, lengths, qkv, qkv, qkv, context_grad, context, lse),
        [
            smem(),
            smem(),
            spec(0),
            spec(1),
            spec(2),
            spec(0),
            spec(0),
            pl.BlockSpec((1, head_rows, length), lambda q: (q, 0, 0)),
        ],
        40,
        grid=(per,),
        out_specs=[
            pl.BlockSpec((3, length, cols), lambda q: (0, q, 0)),
            fixed((8, cols)),
        ],
        out_shape=[
            jax.ShapeDtypeStruct((3, rows, cols), bf16),
            jax.ShapeDtypeStruct((8, cols), f32),
        ],
        cost_estimate=cost(0, 0),
        name="attend_back",
    )


def input_grad_kernel(*refs, groups):
    grads = refs[:groups]
    qkv_w, grad_one = refs[groups : groups + 2]
    outs = refs[groups + 2 :]
    width = grad_one.shape[1]
    each = width // groups
    total = grad_one[...]
    for g in range(groups):
        for third in range(3):
            start = third * width + g * each
            total = total + nt(grads[g][third], qkv_w[:, start : start + each])
    span = outs[0].shape[1]
    for c, out in enumerate(outs):
        out[0] = total[c * span : (c + 1) * span].astype(bf16)


def input_grad(grads, qkv_w, grad_one, per, chunks, after=()):
    groups = len(grads)
    _, rows, each = grads[0].shape
    width = groups * each
    length = rows // per
    span = length // chunks
    return run(
        functools.partial(input_grad_kernel, groups=groups),
        after,
        (*grads, qkv_w, grad_one),
        [pl.BlockSpec((3, length, each), lambda i: (0, i, 0))] * groups
        + [in_vmem(), pl.BlockSpec((length, width), lambda i: (i, 0))],
        32,
        grid=(per,),
        out_specs=[pl.BlockSpec((1, span, width), lambda i: (i, 0, 0))] * chunks,
        out_shape=[jax.ShapeDtypeStruct((per, span, width), bf16)] * chunks,
        cost_estimate=cost(6 * rows * width * width, 12 * rows * width + 6 * width * width),
        name="input_grad",
    )


def chunk_at(me, relative, chunk):
    return pl.ds(pl.multiple_of((me ^ relative) * chunk, 8), chunk)


def tall_grad_kernel(info, left, right, keep, send, total, *, bits, chunk):
    total[...] = tn(left[...], right[...])
    here = left.shape[1] // chunk
    me = info[0]
    for target, other in ((keep, 0), (send, 1)):
        for k in range(0, here, 2):
            source = k + ((me % 2) ^ other)
            relative = (pl.program_id(0) * here + source) ^ me
            place = 0
            for at, bit in enumerate(bits[1:]):
                place = place + ((relative // bit) % 2) * (1 << (len(bits) - 2 - at))
            rows = total[pl.ds(pl.multiple_of(source * chunk, 8), chunk), :]
            target[pl.ds(pl.multiple_of(place * chunk, 16), chunk), :] = rows.astype(bf16)


def tall_grad(me, left, right, bits, after=()):
    rows, depth = left.shape
    width = right.shape[1]
    chunk = depth >> len(bits)
    block = 8 * chunk
    return run(
        functools.partial(tall_grad_kernel, bits=bits, chunk=chunk),
        after,
        (me, left, right),
        [smem(), pl.BlockSpec((rows, block), lambda j: (0, j)), fixed((rows, width))],
        40,
        grid=(depth // block,),
        out_specs=[fixed((depth // 2, width))] * 2,
        out_shape=[jax.ShapeDtypeStruct((depth // 2, width), bf16)] * 2,
        scratch_shapes=[pltpu.VMEM((block, width), f32)],
        cost_estimate=cost(0, 0),
        name="tall_grad",
    )


def wide_grad_kernel(info, left, right, keep, send, left_t, total, *, order, chunk):
    @pl.when(pl.program_id(0) == 0)
    def _():
        left_t[...] = jnp.transpose(left[...])

    me = info[0]
    half = len(order) // 2
    parts, _, tile = total.shape
    for part in range(parts):
        cols = slice(part * tile, (part + 1) * tile)
        total[part] = nn(left_t[...], right[:, cols])
        for at in range(0, len(order), 2):
            rows = jnp.concatenate([total[part, chunk_at(me, order[at + k], chunk), :] for k in range(2)], axis=0)
            target = keep if at < half else send
            row = (at % half) * chunk
            target[row : row + 2 * chunk, cols] = rows.astype(bf16)


def wide_grad(me, left, right, order, tile, after=()):
    rows, depth = left.shape
    width = right.shape[1]
    return run(
        functools.partial(wide_grad_kernel, order=order, chunk=depth // len(order)),
        after,
        (me, left, right),
        [smem(), fixed((rows, depth)), pl.BlockSpec((rows, tile), lambda j: (0, j))],
        32,
        grid=(width // tile,),
        out_specs=[pl.BlockSpec((depth // 2, tile), lambda j: (0, j))] * 2,
        out_shape=[jax.ShapeDtypeStruct((depth // 2, width), bf16)] * 2,
        scratch_shapes=[pltpu.VMEM((depth, rows), bf16), pltpu.VMEM((tile // 256, depth, 256), f32)],
        cost_estimate=cost(2 * rows * depth * width, 2 * rows * (depth + width) + 2 * depth * width),
        name="wide_grad",
    )


def fill_table(table, near, vectors, counts, chunk):
    per, groups = counts
    sums_two, ramp_sums = vectors[:2]
    sums_one = vectors[2 : 2 + per]
    up_sums = vectors[2 + per : 2 + 2 * per]
    qkv_sums = vectors[2 + 2 * per :]
    near[0:3, :] = sums_two[0:3, :]
    near[3:6, :] = sum(ref[0:3, :] for ref in sums_one)
    each = near.shape[1] // groups
    for g in range(groups):
        near[6:8, g * each : (g + 1) * each] = qkv_sums[g][0:2, :]
    ups = sum(ref[...] for ref in up_sums)
    owners = table.shape[0]
    wide = ups.shape[1] // owners
    table[...] = jnp.zeros_like(table)
    for k in range(owners):
        cols = slice(k * chunk, (k + 1) * chunk)
        table[k, :, 0:chunk] = near[:, cols]
        table[k, :, 128 : 128 + chunk] = ramp_sums[:, cols]
        table[k, 0:1, 128 : 128 + wide] = ups[:, k * wide : (k + 1) * wide]


def group_grad_kernel(info, *refs, order, chunk, jobs, counts):
    extra = counts is not None
    scratch = 3 if extra else 1
    keep, send = refs[-2 - scratch : -scratch]
    total = refs[-scratch]
    at_ref = 0
    column = 0
    for thirds in jobs:
        left, right = refs[at_ref : at_ref + 2]
        at_ref += 2
        if left.shape[0] < 128:
            high = right[...].astype(bf16)
            low = (right[...] - high.astype(f32)).astype(bf16)
            lefts = left[...].astype(bf16)
            product = tn(jnp.concatenate([lefts, lefts], axis=0), jnp.concatenate([high, low], axis=0))
            total[:, column : column + high.shape[1]] = product
            column += high.shape[1]
            continue
        left_t = jnp.transpose(left[...])
        for third in range(thirds or 1):
            block = right[third] if thirds else right[...]
            total[:, column : column + block.shape[1]] = nn(left_t, block)
            column += block.shape[1]
    me = info[0]
    half = len(order) // 2
    tall = chunk + (8 if extra else 0)
    if extra:
        table, near = refs[-2:]
        fill_table(table, near, refs[at_ref : at_ref + 2 + 2 * counts[0] + counts[1]], counts, chunk)
    for at in range(0, len(order), 2):
        pieces = []
        for k in range(2):
            pieces.append(total[chunk_at(me, order[at + k], chunk), :])
            if extra:
                vector = table[me ^ order[at + k]]
                high = vector.astype(bf16).astype(f32)
                fill = jnp.zeros((8, column - 2 * vector.shape[1]), f32)
                pieces.append(jnp.concatenate([high, vector - high, fill], axis=1))
        rows = jnp.concatenate(pieces, axis=0)
        target = keep if at < half else send
        row = (at % half) * tall
        target[row : row + 2 * tall, :] = rows.astype(bf16)


def group_grad(me, pairs, vectors, counts, order, after=()):
    rows, depth = pairs[0][0].shape
    jobs = tuple(right.shape[0] if right.ndim == 3 else 0 for _, right in pairs)
    width = sum((right.shape[0] if right.ndim == 3 else 1) * right.shape[-1] for _, right in pairs)
    chunk = depth // len(order)
    extra = counts is not None
    tall = (chunk + (8 if extra else 0)) * len(order) // 2
    operands = [a for pair in pairs for a in pair] + list(vectors)
    scratch = [pltpu.VMEM((depth, width), f32)]
    if extra:
        scratch += [pltpu.VMEM((len(order), 8, 256), f32), pltpu.VMEM((8, depth), f32)]
    return run(
        functools.partial(group_grad_kernel, order=order, chunk=chunk, jobs=jobs, counts=counts),
        after,
        (me, *operands),
        [smem()] + [fixed(a.shape) for a in operands],
        48,
        grid=(1,),
        out_specs=[fixed((tall, width))] * 2,
        out_shape=[jax.ShapeDtypeStruct((tall, width), bf16)] * 2,
        scratch_shapes=scratch,
        cost_estimate=cost(0, 0),
        name="group_grad",
    )


def halving_order(stages, n_seq):
    bits = [bit * (n_seq if axis == "dp" else 1) for axis, bit in stages]
    count = len(bits)
    return [
        sum(bit for at, bit in enumerate(bits) if (place >> (count - 1 - at)) & 1) for place in range(1 << count)
    ]


def add_kernel(*refs, plans):
    count = sum(1 + gots for gots, _, _ in plans)
    ins, outs = list(refs[:count]), list(refs[count:])
    for gots, parts, fine in plans:
        terms = [ins.pop(0) for _ in range(1 + gots)]
        part_rows = terms[0].shape[0] // parts
        if part_rows % 16:
            total = sum(term[...].astype(f32) for term in terms[1:]) + terms[0][...].astype(f32)
        for part in range(parts):
            out = outs.pop(0)
            rows = slice(part * part_rows, (part + 1) * part_rows)
            if part_rows % 16:
                out[...] = total[rows].astype(out.dtype)
                continue
            values = sum(term[rows, :].astype(f32) for term in terms[1:]) + terms[0][rows, :].astype(f32)
            out[...] = values.astype(out.dtype)
            if fine:
                vector = values[:, :256] + values[:, 256:512]
                row = lax.broadcasted_iota(jnp.int32, (part_rows, 256), 0)
                here = (row % 32 >= 24) & (pl.program_id(0) == 0)
                if out.dtype == bf16:
                    high = vector.astype(bf16).astype(f32)
                    out[:, :256] = jnp.where(here, high, values[:, :256]).astype(bf16)
                    out[:, 256:512] = jnp.where(here, vector - high, values[:, 256:512]).astype(bf16)
                else:
                    out[:, :256] = jnp.where(here, vector, values[:, :256])


class Halving:
    def __init__(self, halves, stages, fine=False):
        self.keep, *self.sends = halves
        self.stages = stages
        self.fine = fine
        self.gots = None

    def post(self):
        stage = self.stages[0]
        self.stages = self.stages[1:]
        self.gots = []
        for part, send in enumerate(self.sends, 1):
            masks = {}
            for at, (axis, bit) in enumerate(stage):
                if (part >> (len(stage) - 1 - at)) & 1:
                    masks[axis] = masks.get(axis, 0) ^ bit
            axes = tuple(masks)
            if len(axes) == 1:
                size, mask, name = lax.axis_size(axes[0]), masks[axes[0]], axes[0]
            else:
                n_seq = lax.axis_size("seq")
                size = lax.axis_size("dp") * n_seq
                mask, name = masks["dp"] * n_seq + masks["seq"], ("dp", "seq")
            self.gots.append(lax.ppermute(send, name, [(i, i ^ mask) for i in range(size)]))


def advance(streams, passed, after, hold=()):
    adding = [stream for stream in streams if stream.gots is not None]
    fresh = [stream for stream in streams if stream.gots is None]
    passed = list(passed) + [send for stream in fresh for send in stream.sends]
    steps = 3 if max([stream.keep.size for stream in adding], default=0) > 1 << 17 else 1
    operands, in_specs, out_specs, shapes, plans, loose = [], [], [], [], [], []
    for stream in adding:
        rows, width = stream.keep.shape
        tile = width // steps
        loose += [len(operands) + 1 + k for k in range(len(stream.gots))]
        operands += [stream.keep, *stream.gots]
        in_specs += [pl.BlockSpec((rows, tile), lambda j: (0, j))] * (1 + len(stream.gots))
        parts = 1 << len(stream.stages[0]) if stream.stages else 1
        plans.append((len(stream.gots), parts, stream.fine))
        new = [jax.ShapeDtypeStruct((rows // parts, width), bf16 if stream.stages else f32)] * parts
        shapes += new
        out_specs += [pl.BlockSpec((rows // parts, tile), lambda j: (0, j))] * parts
    first_in, first_out = len(operands), len(shapes)

    def body(*refs):
        add_kernel(*refs[:first_in], *refs[first_in + len(passed) :][:first_out], plans=plans)

    outs = run(
        body,
        after,
        operands + passed,
        in_specs + [pl.BlockSpec(memory_space=pl.ANY)] * len(passed),
        40,
        aliases={first_in + k: first_out + k for k in range(len(passed))},
        loose=loose,
        grid=(steps,),
        out_specs=out_specs + [pl.BlockSpec(memory_space=pl.ANY)] * len(passed),
        out_shape=shapes + [jax.ShapeDtypeStruct(a.shape, a.dtype) for a in passed],
        cost_estimate=cost(0, 0),
        name="add",
    )
    done = (outs[0],)
    outs = list(outs)
    for stream, (_, parts, _) in zip(adding, plans, strict=True):
        new = [outs.pop(0) for _ in range(parts)]
        if stream.stages:
            stream.keep, *stream.sends = new
            if stream in hold:
                stream.gots = None
            else:
                stream.post()
        else:
            stream.total = new[0]
    others = len(outs) - sum(len(stream.sends) for stream in fresh)
    others, outs = outs[:others], outs[others:]
    for stream in fresh:
        stream.sends = [outs.pop(0) for _ in stream.sends]
        stream.post()
    return done, others


def bits_of(size):
    return [1 << k for k in range(size.bit_length() - 1)]


def shards(
    hidden_in,
    lengths,
    labels,
    out_cotangent,
    qkv_weight,
    out_weight,
    up_weight,
    down_weight,
    pool_weight,
    class_weight,
    norm_gains,
    biases,
    up_bias,
    class_bias,
):
    positions, group, width = hidden_in.shape
    n_seq = lax.axis_size("seq")
    n_dp = lax.axis_size("dp")
    n_all = n_seq * n_dp
    seq_at = lax.axis_index("seq")
    me = lax.axis_index("dp") * n_seq + seq_at
    per = group // n_seq
    info = seq_at[None].astype(jnp.int32)
    me_info = me[None].astype(jnp.int32)
    classes = class_weight.shape[1]
    class_rows = jnp.zeros((128, width), bf16).at[:classes].set(class_weight.T)
    class_shift = jnp.full((1, 128), neg_big, f32).at[0, :classes].set(class_bias)

    seq_bits = [("seq", b) for b in bits_of(n_seq)]
    dp_bits = [("dp", b) for b in bits_of(n_dp)]
    chunk = width // n_all
    halved = chunk % 8 == 0

    x_send = split_rows(info, hidden_in.reshape(positions * group, width), positions, group, n_seq)
    x_parts = exchange(x_send)
    cot_send = split_rows(
        info, out_cotangent.reshape(positions * group, width), positions, group, n_seq, after=(x_send[0],)
    )
    cots = exchange(cot_send)
    x_rows, qkv, context, lse, n_one, q_one = attend(
        info, lengths, x_parts, qkv_weight, out_weight, biases, after=(cot_send[0],)
    )
    outs = feed(
        info, labels, cots, n_one, up_weight, up_bias[None, :], down_weight, norm_gains, biases, pool_weight,
        class_rows, class_shift,
    )
    middle_low, act, slope, grad_two, branch_grad, ramp_first, ramp_pre, ramp_out, sums_two, ramp_sums = outs[:10]
    final_parts = outs[10:]

    near = [seq_bits[:1], dp_bits[:1], seq_bits[1:]]
    one_way = [[entry] for entry in seq_bits[:1] + dp_bits[:1] + seq_bits[1:] + dp_bits[1:]]
    two_way = near[:1] + [near[1] + near[2]] + [[entry] for entry in dp_bits[1:]]
    flat = [entry for stage in one_way for entry in stage]
    places = halving_order(flat, n_seq)
    bits = tuple(bit * (n_seq if axis == "dp" else 1) for axis, bit in flat)
    streams = {}
    done = (branch_grad,)

    def stage(*names, passed=(), hold=()):
        nonlocal done
        if halved:
            done, passed = advance(
                [streams[name] for name in names], passed, done, [streams[name] for name in hold]
            )
        return passed

    def start(name, halves, stages, fine=False):
        nonlocal done
        streams[name] = Halving(halves, stages, fine)
        done = (halves[0],)

    if halved:
        start("down", tall_grad(me_info, act, branch_grad, bits, after=done), one_way)
    stage("down")
    filled = ()
    sums_one, up_sums = [], []
    for at in range(per):
        filled = feed_back(
            at, per, grad_two, branch_grad, slope, n_one, q_one, down_weight, up_weight, out_weight,
            norm_gains, filled, after=done,
        )
        sums_one.append(filled[4])
        up_sums.append(filled[5])
        filled = filled[:4]
        done = (sums_one[-1],)
        if at == 0:
            final_parts = exchange([final_parts[0], *stage("down", passed=final_parts[1:])])
    pre_grad, grad_one, mix_grad, context_grad = filled
    if halved:
        start("up", wide_grad(me_info, middle_low, pre_grad, places, 1024, after=done), two_way)
    hidden_out = merge_rows(info, final_parts, bf16, after=done)
    done = (hidden_out,)
    stage("down", "up")

    groups = 3 if (width // PAIR) % 3 == 0 else 1
    count = width // PAIR // groups
    grads, qkv_sums = [], []
    for g in range(groups):
        grad, qkv_sum = attend_back(
            info, lengths, qkv, context_grad, context, lse, n_seq, g * count, count, after=done
        )
        grads.append(grad)
        qkv_sums.append(qkv_sum)
        done = (qkv_sum,)
        if g == 0:
            if halved:
                pairs = [(x_rows, grad), (context, mix_grad), (ramp_first, ramp_pre)]
                start("most", group_grad(me_info, pairs, (), None, places, after=done), one_way)
            stage("down", "up", "most")
    back = input_grad(grads, qkv_weight, grad_one, per, n_seq, after=done)
    done = (back[0],)
    if halved:
        pairs = [(x_rows, grad) for grad in grads[1:]]
        vectors = (sums_two, ramp_sums, *sums_one, *up_sums, *qkv_sums)
        start("last", group_grad(me_info, pairs, vectors, (per, groups), places, after=done), one_way, fine=True)
    back_parts = exchange(
        [back[0], *stage("down", "up", "most", "last", passed=back[1:], hold=("down", "up"))]
    )
    grad_in = merge_rows(info, back_parts, f32, after=done)
    done = (grad_in,)
    stage("down", "up", "most", "last")
    stage("down", "up", "most", "last")
    stage("up", "most", "last")
    stage("most", "last")
    stage("last")
    if halved:
        each = width // groups
        most, last = streams["most"].total, streams["last"].total
        parts = [most[:, :width]] + [last[:chunk, g * width : (g + 1) * width] for g in range(groups - 1)]
        qkv_total = jnp.concatenate(
            [parts[g][:, t * each : (t + 1) * each] for t in range(3) for g in range(groups)], axis=1
        )
        out_total = most[:, width : 2 * width]
        pool_total = most[:, 2 * width :]
        up_total = streams["up"].total
        down_total = streams["down"].total
        vec = last[chunk:, :chunk]
        ramp_vec = last[chunk:, 128 : 128 + chunk]
        up_bias_sum = last[chunk, 128 : 128 + up_weight.shape[1] // n_all]
    else:

        def scatter(value):
            return lax.psum_scatter(value, ("dp", "seq"), scatter_dimension=0, tiled=True)

        wide = jnp.concatenate([grads[g][t] for t in range(3) for g in range(groups)], axis=1)
        qkv_total = scatter(tn(x_rows, wide))
        out_total = scatter(tn(context, mix_grad))
        up_total = scatter(tn(middle_low, pre_grad))
        down_total = scatter(tn(act, branch_grad))
        pool_total = scatter(
            lax.dot_general(ramp_first, ramp_pre, (((0,), (0,)), ((), ())), precision=highest)
        )
        table = jnp.concatenate(
            [sums_two[:3], sum(sums_one)[:3], jnp.concatenate(qkv_sums, axis=1)[:2], ramp_sums], axis=0
        )
        table = jnp.transpose(table.reshape(16, n_all, chunk), (1, 0, 2)).reshape(n_all, 16 * chunk)
        table = scatter(jnp.concatenate([table, sum(up_sums).reshape(n_all, -1)], axis=1))[0]
        vec = table[: 8 * chunk].reshape(8, chunk)
        ramp_vec = table[8 * chunk : 16 * chunk].reshape(8, chunk)
        up_bias_sum = table[16 * chunk :]

    gains_sum = jnp.stack([vec[3], vec[0]])
    biases_sum = jnp.stack([vec[6], vec[7], vec[4], vec[5], vec[1], vec[2], ramp_vec[1]])
    class_sum = jnp.transpose(ramp_vec[2 : 2 + classes])
    class_bias_sum = ramp_vec[2 + classes : 2 + 2 * classes, 0]
    ramp_logits = ramp_out.reshape(per, REC, -1)[:, 0, :classes]
    return (
        hidden_out.reshape(positions, group, width),
        ramp_logits,
        grad_in.reshape(positions, group, width),
        qkv_total,
        out_total,
        up_total,
        down_total,
        pool_total,
        class_sum,
        gains_sum,
        biases_sum,
        up_bias_sum,
        class_bias_sum,
    )


def solution(mesh):
    every = ("dp", "seq")
    rows = P("seq", "dp", None)
    return jax.shard_map(
        shards,
        mesh=mesh,
        in_specs=(rows, P("dp"), P(every), rows) + (P(),) * 10,
        out_specs=(
            rows,
            P(every, None),
            rows,
            P(every, None),
            P(every, None),
            P(every, None),
            P(every, None),
            P(every, None),
            P(every, None),
            P(None, every),
            P(None, every),
            P(every),
            P(),
        ),
        check_vma=False,
    )
```

```python
import functools

import jax
import jax.numpy as jnp
from jax import lax
from jax.experimental import pallas as pl
from jax.experimental.pallas import tpu as pltpu
from jax.sharding import PartitionSpec as P

HEAD_DIM = 64
PAIR = 2 * HEAD_DIM
REC = 8
CLASSES = 3
FEED_PARTS = 2

eps = 1e-12
neg_big = -1e30
highest = lax.Precision.HIGHEST
f32 = jnp.float32
bf16 = jnp.bfloat16
MIB = 1 << 20


def nn(left, right):
    return lax.dot_general(left, right, (((1,), (0,)), ((), ())), preferred_element_type=f32)


def nt(left, right):
    return lax.dot_general(left, right, (((1,), (1,)), ((), ())), preferred_element_type=f32)


def tn(left, right):
    return lax.dot_general(left, right, (((0,), (0,)), ((), ())), preferred_element_type=f32)


def cost(flops, nbytes, trans=0):
    return pl.CostEstimate(flops=1, bytes_accessed=1, transcendentals=0)


def smem():
    return pl.BlockSpec(memory_space=pltpu.SMEM)


def in_vmem():
    return pl.BlockSpec(memory_space=pltpu.VMEM)


def fixed(shape):
    return pl.BlockSpec(shape, lambda *_: (0,) * len(shape))


def run(kernel, after, operands, in_specs, limit, out_shape, aliases=None, loose=(), **kwargs):
    skip = len(after)
    operands = [
        a
        if k in loose or spec.memory_space in (pltpu.VMEM, pltpu.SMEM)
        else pltpu.with_memory_space_constraint(a, pltpu.HBM)
        for k, (a, spec) in enumerate(zip(operands, in_specs, strict=True))
    ]
    after = [pltpu.with_memory_space_constraint(a, pltpu.HBM) for a in after]
    single = not isinstance(out_shape, list)
    shapes = [pltpu.HBM(a.shape, a.dtype) for a in ([out_shape] if single else out_shape)]

    def body(*refs):
        kernel(*refs[skip:])

    return pl.pallas_call(
        body,
        in_specs=[pl.BlockSpec(memory_space=pl.ANY)] * skip + list(in_specs),
        out_shape=shapes[0] if single else shapes,
        input_output_aliases={k + skip: v for k, v in (aliases or {}).items()},
        compiler_params=pltpu.CompilerParams(vmem_limit_bytes=limit * MIB),
        **kwargs,
    )(*after, *operands)


def three_parts(value):
    hi = value.astype(bf16)
    rest = value - hi.astype(f32)
    mid = rest.astype(bf16)
    low = (rest - mid.astype(f32)).astype(bf16)
    return jnp.concatenate([hi, mid, low], axis=0)


def fine_dot(dot, value, weight):
    rows = value.shape[0]
    parts = dot(jnp.concatenate([three_parts(value)], axis=0), weight)
    return parts[:rows] + parts[rows : 2 * rows] + parts[2 * rows :]


def split_kernel(info, rows, *outs):
    chunks = len(outs)
    per, span, _ = outs[0].shape
    group = chunks * per
    block = 16 * group
    own = info[0]
    dest = lax.broadcasted_iota(jnp.int32, (block, block), 0)
    source = lax.broadcasted_iota(jnp.int32, (block, block), 1)
    chunk = dest // (16 * per)
    wanted = (dest % 16) * group + per * (chunk ^ own) + (dest // 16) % per
    perm = jnp.where(source == wanted, 1.0, 0.0).astype(bf16)
    for b in range(span // 16):
        moved = nn(perm, rows[b * block : (b + 1) * block, :]).astype(bf16)
        for c in range(chunks):
            for q in range(per):
                at = (c * per + q) * 16
                outs[c][q, b * 16 : (b + 1) * 16, :] = moved[at : at + 16]


def split_rows(info, rows, positions, group, chunks, after=()):
    width = rows.shape[1]
    per = group // chunks
    steps = 2
    span = positions // steps
    return run(
        split_kernel,
        after,
        (info, rows),
        [smem(), pl.BlockSpec((span * group, width), lambda i: (i, 0))],
        16,
        grid=(steps,),
        out_specs=[pl.BlockSpec((per, span, width), lambda i: (0, i, 0))] * chunks,
        out_shape=[jax.ShapeDtypeStruct((per, positions, width), bf16)] * chunks,
        cost_estimate=cost(2 * rows.size * 16 * group, 4 * rows.size),
        name="split_rows",
    )


def merge_kernel(info, *refs):
    ins, out = refs[:-1], refs[-1]
    chunks = len(ins)
    per, span, _ = ins[0].shape
    group = chunks * per
    block = 16 * group
    own = info[0]
    dest = lax.broadcasted_iota(jnp.int32, (block, block), 0)
    source = lax.broadcasted_iota(jnp.int32, (block, block), 1)
    seq = dest % group
    wanted = (((seq // per) ^ own) * per + seq % per) * 16 + dest // group
    perm = jnp.where(source == wanted, 1.0, 0.0).astype(bf16)
    for b in range(span // 16):
        rows = jnp.concatenate(
            [ins[c][q, b * 16 : (b + 1) * 16, :] for c in range(chunks) for q in range(per)], axis=0
        )
        out[b * block : (b + 1) * block, :] = nn(perm, rows).astype(out.dtype)


def merge_rows(info, parts, dtype, after=()):
    chunks = len(parts)
    per, positions, width = parts[0].shape
    group = per * chunks
    steps = 2
    span = positions // steps
    return run(
        merge_kernel,
        after,
        (info, *parts),
        [smem()] + [pl.BlockSpec((per, span, width), lambda i: (0, i, 0))] * chunks,
        16,
        grid=(steps,),
        out_specs=pl.BlockSpec((span * group, width), lambda i: (i, 0)),
        out_shape=jax.ShapeDtypeStruct((positions * group, width), dtype),
        cost_estimate=cost(2 * positions * group * width * 16 * group, 6 * positions * group * width),
        name="merge_rows",
    )


def exchange(parts):
    size = lax.axis_size("seq")
    return [parts[0]] + [
        lax.ppermute(parts[c], "seq", [(i, i ^ c) for i in range(size)]) for c in range(1, size)
    ]


def row_stats(resid):
    mean = jnp.mean(resid, axis=-1, keepdims=True)
    centred = resid - mean
    scale = lax.rsqrt(jnp.mean(centred * centred, axis=-1, keepdims=True) + eps)
    return centred * scale, scale


def attend_kernel(info, lengths, *refs):
    chunks = len(refs) - 10
    parts = refs[:chunks]
    qkv_w, out_w, biases, x_out, qkv, context, lse, normed, scale, stats = refs[chunks:]
    width = out_w.shape[0]
    span = parts[0].shape[1]
    length = chunks * span
    pairs = width // PAIR
    own = info[0]
    live_len = lengths[own * pl.num_programs(0) + pl.program_id(0)]
    x_out[...] = jnp.concatenate([part[0] for part in parts], axis=0)
    for third in range(3):
        cols = slice(third * width, (third + 1) * width)
        block = nn(x_out[...], qkv_w[:, cols])
        if third == 0:
            block = block + biases[0:1, :]
        elif third == 2:
            block = block + biases[1:2, :]
        qkv[:, cols] = block.astype(bf16)
    lane = lax.broadcasted_iota(jnp.int32, (length, PAIR), 1)
    row = lax.broadcasted_iota(jnp.int32, (length, PAIR), 0)
    pos = ((row // span) ^ own) * span + row % span
    key_ext = jnp.where((lane == 0) & (pos >= live_len), neg_big, 0.0).astype(bf16)
    query_ext = jnp.where(lane == 0, 1.0, 0.0).astype(bf16)
    low_half = lane < HEAD_DIM
    masks = [jnp.where(low_half, 1.0, 0.0).astype(bf16), jnp.where(low_half, 0.0, 1.0).astype(bf16)]
    stats[...] = jnp.zeros_like(stats)

    def one_pair(i, carry):
        start = pl.multiple_of(i * PAIR, PAIR)
        queries = qkv[:, pl.ds(start, PAIR)] * bf16(HEAD_DIM**-0.5)
        keys = jnp.concatenate([qkv[:, pl.ds(start + width, PAIR)], key_ext], axis=1)
        values = qkv[:, pl.ds(start + 2 * width, PAIR)]
        total = None
        tops = []
        for head in range(2):
            scores = nt(jnp.concatenate([queries * masks[head], query_ext], axis=1), keys)
            top = jnp.max(scores, axis=1, keepdims=True)
            weights = jnp.exp(scores - top).astype(bf16)
            part = nn(weights, jnp.concatenate([values * masks[head], masks[head]], axis=1))
            total = part if total is None else total + part
            tops.append(top)
        row_total = total[:, PAIR:]
        context[:, pl.ds(start, PAIR)] = (total[:, :PAIR] / row_total).astype(bf16)
        log_total = jnp.where(low_half, tops[0], tops[1]) + jnp.log(row_total)
        swapped = pltpu.roll(log_total, HEAD_DIM, 1)
        stats[...] = jnp.where(
            lane == 2 * i, log_total, jnp.where(lane == 2 * i + 1, swapped, stats[...])
        )
        return carry

    lax.fori_loop(0, pairs, one_pair, 0, unroll=pairs)
    lse[0] = jnp.transpose(stats[...])[: lse.shape[1], :]
    resid = x_out[...].astype(f32) + (nn(context[...], out_w[...]) + biases[2:3, :])
    n_one, q_one = row_stats(resid)
    normed[...] = n_one
    scale[...] = q_one


def attend(info, lengths, parts, qkv_w, out_w, biases, after=()):
    chunks = len(parts)
    per, span, width = parts[0].shape
    length = chunks * span
    rows = per * length
    heads = width // HEAD_DIM
    head_rows = -(-heads // 8) * 8
    by_seq = lambda i: (i, 0)
    return run(
        attend_kernel,
        after,
        (info, lengths, *parts, qkv_w, out_w, biases),
        [smem()] * 2
        + [pl.BlockSpec((1, span, width), lambda i: (i, 0, 0))] * chunks
        + [in_vmem()] * 3,
        40,
        grid=(per,),
        out_specs=[
            pl.BlockSpec((length, width), by_seq),
            pl.BlockSpec((length, 3 * width), by_seq),
            pl.BlockSpec((length, width), by_seq),
            pl.BlockSpec((1, head_rows, length), lambda i: (i, 0, 0)),
            pl.BlockSpec((length, width), by_seq),
            pl.BlockSpec((length, 1), by_seq),
        ],
        out_shape=[
            jax.ShapeDtypeStruct((rows, width), bf16),
            jax.ShapeDtypeStruct((rows, 3 * width), bf16),
            jax.ShapeDtypeStruct((rows, width), bf16),
            jax.ShapeDtypeStruct((per, head_rows, length), f32),
            jax.ShapeDtypeStruct((rows, width), f32),
            jax.ShapeDtypeStruct((rows, 1), f32),
        ],
        scratch_shapes=[pltpu.VMEM((length, PAIR), f32)],
        cost_estimate=cost(
            8 * rows * width * width + 8 * rows * length * width, 20 * rows * width + 8 * width * width,
            rows * length * heads,
        ),
        name="attend",
    )


def gelu_pair(x):
    cdf = 0.5 + 0.5 * lax.erf(x * 0.5**0.5)
    bell = jnp.exp(-0.5 * (x * x))
    return x * cdf, cdf + x * bell * (0.5 / jnp.pi) ** 0.5


def norm_back(upper, normed, scale, gain):
    scaled = upper * gain
    mean_part = jnp.mean(scaled, axis=-1, keepdims=True)
    proj_part = jnp.mean(scaled * normed, axis=-1, keepdims=True)
    return scale * (scaled - mean_part - normed * proj_part)


def col_sum(values):
    return jnp.sum(values, axis=0, keepdims=True)


def feed_kernel(info, labels, *refs):
    chunks = (len(refs) - 20) // 2
    cots = refs[:chunks]
    normed, up_w, up_b, down_w, gains, biases, pool_w, class_w, class_b = refs[chunks : chunks + 9]
    middle_out, act, slope, grad_two, branch_grad = refs[chunks + 9 : chunks + 14]
    ramp_first, ramp_pre, ramp_out, sums, ramp_sums = refs[chunks + 14 : chunks + 19]
    finals = refs[chunks + 19 : -1]
    n_two = refs[-1]
    span = finals[0].shape[1]
    own = info[0]

    @pl.when(pl.program_id(0) == 0)
    def _():
        sums[...] = jnp.zeros_like(sums)
        ramp_sums[...] = jnp.zeros_like(ramp_sums)

    hidden = up_w.shape[1]
    tile = 256
    length = chunks * span
    block = length // FEED_PARTS
    scales = []
    for part in range(FEED_PARTS):
        rows = slice(part * block, (part + 1) * block)
        middle = normed[rows, :] * gains[0:1, :] + biases[3:4, :]
        middle_out[rows, :] = middle.astype(bf16)
        for j in range(hidden // tile):
            cols = slice(j * tile, (j + 1) * tile)
            pre = nn(middle_out[rows, :], up_w[:, cols]) + up_b[:, cols]
            value, grad = gelu_pair(pre)
            act[rows, cols] = value.astype(bf16)
            slope[rows, cols] = grad.astype(bf16)
        branch = nn(act[rows, :], down_w[...]) + biases[4:5, :]
        middle = normed[rows, :] * gains[0:1, :] + biases[3:4, :]
        normed_two, q_two = row_stats(middle + branch)
        n_two[rows, :] = normed_two
        scales.append(q_two)
    for c in range(chunks):
        rows = slice(c * span, (c + 1) * span)
        finals[c][0] = (n_two[rows, :] * gains[1:2, :] + biases[5:6, :]).astype(bf16)
    label = labels[pl.program_id(0)]
    start = pl.multiple_of(own * span, 8)
    first = (n_two[pl.ds(start, REC), :] * gains[1:2, :] + biases[5:6, :]).astype(bf16)
    pooled = jnp.tanh(nn(first, pool_w[...]) + biases[6:7, :])
    logits = fine_dot(nt, pooled, class_w[...]) + class_b[...]
    expo = jnp.exp(logits - jnp.max(logits, axis=1, keepdims=True))
    lane = lax.broadcasted_iota(jnp.int32, logits.shape, 1)
    g_logits = expo / jnp.sum(expo, axis=1, keepdims=True) - jnp.where(lane == label, 1.0, 0.0)
    g_pre = fine_dot(nn, g_logits, class_w[...]) * (1.0 - pooled * pooled)
    g_first = fine_dot(nt, g_pre, pool_w[...])
    first_row = lax.broadcasted_iota(jnp.int32, (REC, 1), 0) == 0
    ramp_first[...] = jnp.where(first_row, first.astype(f32), 0.0)
    ramp_pre[...] = jnp.where(first_row, g_pre, 0.0)
    ramp_out[...] = logits
    ramp_sums[1:2, :] += g_pre[0:1, :]
    for c in range(CLASSES):
        at_class = jnp.sum(jnp.where(lane == c, g_logits, 0.0), axis=1, keepdims=True)[0:1, :]
        ramp_sums[2 + c : 3 + c, :] += at_class * pooled[0:1, :]
        ramp_sums[2 + CLASSES + c : 3 + CLASSES + c, :] += at_class + jnp.zeros_like(pooled[0:1, :])
    sum_rows = [0.0, 0.0, 0.0]
    for part in range(FEED_PARTS):
        rows = slice(part * block, (part + 1) * block)
        here = cots[part * chunks // FEED_PARTS : (part + 1) * chunks // FEED_PARTS]
        cot = jnp.concatenate([chunk[0] for chunk in here], axis=0).astype(f32)
        row = part * block + lax.broadcasted_iota(jnp.int32, (block, 1), 0)
        g_final = cot + jnp.where(row == own * span, g_first[0:1, :], 0.0)
        normed_two = n_two[rows, :]
        g_two = norm_back(g_final, normed_two, scales[part], gains[1:2, :])
        grad_two[rows, :] = g_two
        low = g_two.astype(bf16)
        branch_grad[rows, :] = low
        for k, values in enumerate((g_final * normed_two, low.astype(f32), g_final)):
            sum_rows[k] = sum_rows[k] + col_sum(values)
    for k in range(3):
        sums[k : k + 1, :] += sum_rows[k]


def feed(info, labels, cots, normed, up_w, up_b, down_w, gains, biases, pool_w, class_w, class_b, after=()):
    chunks = len(cots)
    per, span, _ = cots[0].shape
    rows, width = normed.shape
    length = rows // per
    hidden = up_w.shape[1]
    by_seq = lambda i: (i, 0)
    row_block = pl.BlockSpec((length, width), by_seq)
    wide_block = pl.BlockSpec((length, hidden), by_seq)
    part = pl.BlockSpec((1, span, width), lambda i: (i, 0, 0))
    consts = (up_w, up_b, down_w, gains, biases, pool_w, class_w, class_b)
    return run(
        feed_kernel,
        after,
        (info, labels, *cots, normed, *consts),
        [smem()] * 2 + [part] * chunks + [row_block] + [in_vmem()] * len(consts),
        40,
        grid=(per,),
        out_specs=[
            row_block, wide_block, wide_block, row_block, row_block,
            pl.BlockSpec((REC, width), by_seq), pl.BlockSpec((REC, width), by_seq),
            pl.BlockSpec((REC, class_b.shape[1]), by_seq), fixed((8, width)), fixed((8, width)),
        ]
        + [part] * chunks,
        out_shape=[
            jax.ShapeDtypeStruct((rows, width), bf16),
            jax.ShapeDtypeStruct((rows, hidden), bf16),
            jax.ShapeDtypeStruct((rows, hidden), bf16),
            jax.ShapeDtypeStruct((rows, width), f32),
            jax.ShapeDtypeStruct((rows, width), bf16),
            jax.ShapeDtypeStruct((per * REC, width), f32),
            jax.ShapeDtypeStruct((per * REC, width), f32),
            jax.ShapeDtypeStruct((per * REC, class_b.shape[1]), f32),
            jax.ShapeDtypeStruct((8, width), f32),
            jax.ShapeDtypeStruct((8, width), f32),
        ]
        + [jax.ShapeDtypeStruct((per, span, width), bf16)] * chunks,
        scratch_shapes=[pltpu.VMEM((length, width), f32)],
        cost_estimate=cost(4 * rows * width * hidden, 4 * rows * hidden + 4 * width * hidden + 12 * rows * width),
        name="feed",
    )


def feed_back_kernel(*refs, carried):
    grad_two, branch_grad, slope, n_one, q_one, down_w, up_w, out_w, gains = refs[:9]
    pre_grad, grad_one, mix_grad, context_grad, sums, up_sums = refs[9 + carried :]

    @pl.when(pl.program_id(0) == 0)
    def _():
        sums[...] = jnp.zeros_like(sums)
        up_sums[...] = jnp.zeros_like(up_sums)

    hidden = up_w.shape[1]
    tile = 256
    for j in range(hidden // tile):
        cols = slice(j * tile, (j + 1) * tile)
        pre = nt(branch_grad[...], down_w[cols, :]) * slope[:, cols].astype(f32)
        low = pre.astype(bf16)
        pre_grad[:, cols] = low
        up_sums[:, cols] += col_sum(low.astype(f32))
    g_middle = grad_two[...] + nt(pre_grad[...], up_w[...])
    normed = n_one[...]
    sums[0:1, :] += col_sum(g_middle * normed)
    sums[2:3, :] += col_sum(g_middle)
    g_one = norm_back(g_middle, normed, q_one[...], gains[0:1, :])
    grad_one[...] = g_one
    mix_grad[...] = g_one.astype(bf16)
    sums[1:2, :] += col_sum(mix_grad[...].astype(f32))
    context_grad[...] = nt(mix_grad[...], out_w[...]).astype(bf16)


def feed_back(at, per, grad_two, branch_grad, slope, n_one, q_one, down_w, up_w, out_w, gains, before, after=()):
    rows, width = grad_two.shape
    hidden = slope.shape[1]
    steps = 2
    block = rows // per // steps
    by_row = lambda i: (at * steps + i, 0)
    row_block = pl.BlockSpec((block, width), by_row)
    wide_block = pl.BlockSpec((block, hidden), by_row)
    thin_block = pl.BlockSpec((block, 1), by_row)
    return run(
        functools.partial(feed_back_kernel, carried=len(before)),
        after,
        (grad_two, branch_grad, slope, n_one, q_one, down_w, up_w, out_w, gains, *before),
        [row_block, row_block, wide_block, row_block, thin_block]
        + [in_vmem()] * 4
        + [pl.BlockSpec(memory_space=pl.ANY)] * len(before),
        32,
        aliases={9 + k: k for k in range(len(before))},
        grid=(steps,),
        out_specs=[wide_block, row_block, row_block, row_block, fixed((8, width)), fixed((1, hidden))],
        out_shape=[
            jax.ShapeDtypeStruct((rows, hidden), bf16),
            jax.ShapeDtypeStruct((rows, width), f32),
            jax.ShapeDtypeStruct((rows, width), bf16),
            jax.ShapeDtypeStruct((rows, width), bf16),
            jax.ShapeDtypeStruct((8, width), f32),
            jax.ShapeDtypeStruct((1, hidden), f32),
        ],
        cost_estimate=cost(
            (4 * rows * width * hidden + 2 * rows * width * width) // per,
            4 * rows * hidden + 4 * width * hidden + 20 * rows * width,
        ),
        name="feed_back",
    )


def attend_back_kernel(info, lengths, queries_in, keys_in, values_in, context_grad, context, lse, grads, sums, *, chunks, first):
    length, cols = queries_in.shape
    span = length // chunks
    own = info[0]
    live_len = lengths[own * pl.num_programs(0) + pl.program_id(0)]
    factor = HEAD_DIM**-0.5
    lane = lax.broadcasted_iota(jnp.int32, (length, PAIR), 1)
    row = lax.broadcasted_iota(jnp.int32, (length, PAIR), 0)
    pos = ((row // span) ^ own) * span + row % span
    key_ext = jnp.where((lane == 0) & (pos >= live_len), neg_big, 0.0).astype(bf16)
    query_ext = jnp.where(lane == 0, 1.0, 0.0).astype(bf16)
    low_half = lane < HEAD_DIM
    masks = [jnp.where(low_half, 1.0, 0.0).astype(bf16), jnp.where(low_half, 0.0, 1.0).astype(bf16)]
    picks = jnp.where(
        lax.broadcasted_iota(jnp.int32, (8, PAIR), 1) // HEAD_DIM
        == lax.broadcasted_iota(jnp.int32, (8, PAIR), 0),
        1.0,
        0.0,
    ).astype(bf16)
    parts = 1
    block = length // parts

    @pl.when(pl.program_id(0) == 0)
    def _():
        sums[...] = jnp.zeros_like(sums)

    for pair in range(cols // PAIR):
        at = slice(pair * PAIR, (pair + 1) * PAIR)
        queries = queries_in[:, at] * bf16(factor)
        keys = jnp.concatenate([keys_in[:, at], key_ext], axis=1)
        values = values_in[:, at]
        ctx_grad = context_grad[:, at]
        product = ctx_grad.astype(f32) * context[:, at].astype(f32)
        high = product.astype(bf16)
        low = (product - high.astype(f32)).astype(bf16)
        row_dots = nt(picks, high) + nt(picks, low)
        g_queries = None
        g_keys = [None] * parts
        g_values = [None] * parts
        for head in range(2):
            masked_q = queries * masks[head]
            long_q = jnp.concatenate([masked_q, query_ext], axis=1)
            masked_g = ctx_grad * masks[head]
            masked_k = keys_in[:, at] * masks[head]
            log_total = lse[0, 2 * (first + pair) + head : 2 * (first + pair) + head + 1, :]
            row_dot = row_dots[head : head + 1, :]
            for c in range(parts):
                rows = slice(c * block, (c + 1) * block)
                weights = jnp.exp(nt(keys[rows], long_q) - log_total)
                part = nn(weights.astype(bf16), masked_g)
                g_values[c] = part if g_values[c] is None else g_values[c] + part
                g_scores = (weights * (nt(values[rows], masked_g) - row_dot)).astype(bf16)
                part = nn(g_scores, masked_q)
                g_keys[c] = part if g_keys[c] is None else g_keys[c] + part
                part = tn(g_scores, masked_k[rows])
                g_queries = part if g_queries is None else g_queries + part
        grads[0, :, at] = (g_queries * factor).astype(bf16)
        for c in range(parts):
            rows = slice(c * block, (c + 1) * block)
            grads[1, rows, at] = g_keys[c].astype(bf16)
            grads[2, rows, at] = g_values[c].astype(bf16)
        sums[0:1, at] += col_sum(grads[0, :, at].astype(f32))
        sums[1:2, at] += col_sum(grads[2, :, at].astype(f32))


def attend_back(info, lengths, qkv, context_grad, context, lse, chunks, first, count, after=()):
    rows, width = context.shape
    per, head_rows, length = lse.shape
    cols = count * PAIR
    blocks = width // cols
    spec = lambda third: pl.BlockSpec((length, cols), lambda q: (q, third * blocks + first // count))
    return run(
        functools.partial(attend_back_kernel, chunks=chunks, first=first),
        after,
        (info, lengths, qkv, qkv, qkv, context_grad, context, lse),
        [
            smem(),
            smem(),
            spec(0),
            spec(1),
            spec(2),
            spec(0),
            spec(0),
            pl.BlockSpec((1, head_rows, length), lambda q: (q, 0, 0)),
        ],
        40,
        grid=(per,),
        out_specs=[
            pl.BlockSpec((3, length, cols), lambda q: (0, q, 0)),
            fixed((8, cols)),
        ],
        out_shape=[
            jax.ShapeDtypeStruct((3, rows, cols), bf16),
            jax.ShapeDtypeStruct((8, cols), f32),
        ],
        cost_estimate=cost(0, 0),
        name="attend_back",
    )


def input_grad_kernel(*refs, groups):
    grads = refs[:groups]
    qkv_w, grad_one = refs[groups : groups + 2]
    outs = refs[groups + 2 :]
    width = grad_one.shape[1]
    each = width // groups
    total = grad_one[...]
    for g in range(groups):
        for third in range(3):
            start = third * width + g * each
            total = total + nt(grads[g][third], qkv_w[:, start : start + each])
    span = outs[0].shape[1]
    for c, out in enumerate(outs):
        out[0] = total[c * span : (c + 1) * span].astype(bf16)


def input_grad(grads, qkv_w, grad_one, per, chunks, after=()):
    groups = len(grads)
    _, rows, each = grads[0].shape
    width = groups * each
    length = rows // per
    span = length // chunks
    return run(
        functools.partial(input_grad_kernel, groups=groups),
        after,
        (*grads, qkv_w, grad_one),
        [pl.BlockSpec((3, length, each), lambda i: (0, i, 0))] * groups
        + [in_vmem(), pl.BlockSpec((length, width), lambda i: (i, 0))],
        32,
        grid=(per,),
        out_specs=[pl.BlockSpec((1, span, width), lambda i: (i, 0, 0))] * chunks,
        out_shape=[jax.ShapeDtypeStruct((per, span, width), bf16)] * chunks,
        cost_estimate=cost(6 * rows * width * width, 12 * rows * width + 6 * width * width),
        name="input_grad",
    )


def chunk_at(me, relative, chunk):
    return pl.ds(pl.multiple_of((me ^ relative) * chunk, 8), chunk)


def tall_grad_kernel(info, left, right, keep, send, total, *, bits, chunk):
    total[...] = tn(left[...], right[...])
    here = left.shape[1] // chunk
    me = info[0]
    for target, other in ((keep, 0), (send, 1)):
        for k in range(0, here, 2):
            source = k + ((me % 2) ^ other)
            relative = (pl.program_id(0) * here + source) ^ me
            place = 0
            for at, bit in enumerate(bits[1:]):
                place = place + ((relative // bit) % 2) * (1 << (len(bits) - 2 - at))
            rows = total[pl.ds(pl.multiple_of(source * chunk, 8), chunk), :]
            target[pl.ds(pl.multiple_of(place * chunk, 16), chunk), :] = rows.astype(bf16)


def tall_grad(me, left, right, bits, after=()):
    rows, depth = left.shape
    width = right.shape[1]
    chunk = depth >> len(bits)
    block = 8 * chunk
    return run(
        functools.partial(tall_grad_kernel, bits=bits, chunk=chunk),
        after,
        (me, left, right),
        [smem(), pl.BlockSpec((rows, block), lambda j: (0, j)), fixed((rows, width))],
        40,
        grid=(depth // block,),
        out_specs=[fixed((depth // 2, width))] * 2,
        out_shape=[jax.ShapeDtypeStruct((depth // 2, width), bf16)] * 2,
        scratch_shapes=[pltpu.VMEM((block, width), f32)],
        cost_estimate=cost(0, 0),
        name="tall_grad",
    )


def wide_grad_kernel(info, left, right, keep, send, left_t, total, *, order, chunk):
    @pl.when(pl.program_id(0) == 0)
    def _():
        left_t[...] = jnp.transpose(left[...])

    me = info[0]
    half = len(order) // 2
    parts, _, tile = total.shape
    for part in range(parts):
        cols = slice(part * tile, (part + 1) * tile)
        total[part] = nn(left_t[...], right[:, cols])
        for at in range(0, len(order), 2):
            rows = jnp.concatenate([total[part, chunk_at(me, order[at + k], chunk), :] for k in range(2)], axis=0)
            target = keep if at < half else send
            row = (at % half) * chunk
            target[row : row + 2 * chunk, cols] = rows.astype(bf16)


def wide_grad(me, left, right, order, tile, after=()):
    rows, depth = left.shape
    width = right.shape[1]
    return run(
        functools.partial(wide_grad_kernel, order=order, chunk=depth // len(order)),
        after,
        (me, left, right),
        [smem(), fixed((rows, depth)), pl.BlockSpec((rows, tile), lambda j: (0, j))],
        32,
        grid=(width // tile,),
        out_specs=[pl.BlockSpec((depth // 2, tile), lambda j: (0, j))] * 2,
        out_shape=[jax.ShapeDtypeStruct((depth // 2, width), bf16)] * 2,
        scratch_shapes=[pltpu.VMEM((depth, rows), bf16), pltpu.VMEM((tile // 256, depth, 256), f32)],
        cost_estimate=cost(2 * rows * depth * width, 2 * rows * (depth + width) + 2 * depth * width),
        name="wide_grad",
    )


def fill_table(table, near, vectors, counts, chunk):
    per, groups = counts
    sums_two, ramp_sums = vectors[:2]
    sums_one = vectors[2 : 2 + per]
    up_sums = vectors[2 + per : 2 + 2 * per]
    qkv_sums = vectors[2 + 2 * per :]
    near[0:3, :] = sums_two[0:3, :]
    near[3:6, :] = sum(ref[0:3, :] for ref in sums_one)
    each = near.shape[1] // groups
    for g in range(groups):
        near[6:8, g * each : (g + 1) * each] = qkv_sums[g][0:2, :]
    ups = sum(ref[...] for ref in up_sums)
    owners = table.shape[0]
    wide = ups.shape[1] // owners
    table[...] = jnp.zeros_like(table)
    for k in range(owners):
        cols = slice(k * chunk, (k + 1) * chunk)
        table[k, :, 0:chunk] = near[:, cols]
        table[k, :, 128 : 128 + chunk] = ramp_sums[:, cols]
        table[k, 0:1, 128 : 128 + wide] = ups[:, k * wide : (k + 1) * wide]


def group_grad_kernel(info, *refs, order, chunk, jobs, counts):
    extra = counts is not None
    scratch = 3 if extra else 1
    keep, send = refs[-2 - scratch : -scratch]
    total = refs[-scratch]
    at_ref = 0
    column = 0
    for thirds in jobs:
        left, right = refs[at_ref : at_ref + 2]
        at_ref += 2
        if left.shape[0] < 128:
            high = right[...].astype(bf16)
            low = (right[...] - high.astype(f32)).astype(bf16)
            lefts = left[...].astype(bf16)
            product = tn(jnp.concatenate([lefts, lefts], axis=0), jnp.concatenate([high, low], axis=0))
            total[:, column : column + high.shape[1]] = product
            column += high.shape[1]
            continue
        left_t = jnp.transpose(left[...])
        for third in range(thirds or 1):
            block = right[third] if thirds else right[...]
            total[:, column : column + block.shape[1]] = nn(left_t, block)
            column += block.shape[1]
    me = info[0]
    half = len(order) // 2
    tall = chunk + (8 if extra else 0)
    if extra:
        table, near = refs[-2:]
        fill_table(table, near, refs[at_ref : at_ref + 2 + 2 * counts[0] + counts[1]], counts, chunk)
    for at in range(0, len(order), 2):
        pieces = []
        for k in range(2):
            pieces.append(total[chunk_at(me, order[at + k], chunk), :])
            if extra:
                vector = table[me ^ order[at + k]]
                high = vector.astype(bf16).astype(f32)
                fill = jnp.zeros((8, column - 2 * vector.shape[1]), f32)
                pieces.append(jnp.concatenate([high, vector - high, fill], axis=1))
        rows = jnp.concatenate(pieces, axis=0)
        target = keep if at < half else send
        row = (at % half) * tall
        target[row : row + 2 * tall, :] = rows.astype(bf16)


def group_grad(me, pairs, vectors, counts, order, after=()):
    rows, depth = pairs[0][0].shape
    jobs = tuple(right.shape[0] if right.ndim == 3 else 0 for _, right in pairs)
    width = sum((right.shape[0] if right.ndim == 3 else 1) * right.shape[-1] for _, right in pairs)
    chunk = depth // len(order)
    extra = counts is not None
    tall = (chunk + (8 if extra else 0)) * len(order) // 2
    operands = [a for pair in pairs for a in pair] + list(vectors)
    scratch = [pltpu.VMEM((depth, width), f32)]
    if extra:
        scratch += [pltpu.VMEM((len(order), 8, 256), f32), pltpu.VMEM((8, depth), f32)]
    return run(
        functools.partial(group_grad_kernel, order=order, chunk=chunk, jobs=jobs, counts=counts),
        after,
        (me, *operands),
        [smem()] + [fixed(a.shape) for a in operands],
        48,
        grid=(1,),
        out_specs=[fixed((tall, width))] * 2,
        out_shape=[jax.ShapeDtypeStruct((tall, width), bf16)] * 2,
        scratch_shapes=scratch,
        cost_estimate=cost(0, 0),
        name="group_grad",
    )


def halving_order(stages, n_seq):
    bits = [bit * (n_seq if axis == "dp" else 1) for axis, bit in stages]
    count = len(bits)
    return [
        sum(bit for at, bit in enumerate(bits) if (place >> (count - 1 - at)) & 1) for place in range(1 << count)
    ]


def add_kernel(*refs, plans):
    count = sum(1 + gots for gots, _, _ in plans)
    ins, outs = list(refs[:count]), list(refs[count:])
    for gots, parts, fine in plans:
        terms = [ins.pop(0) for _ in range(1 + gots)]
        part_rows = terms[0].shape[0] // parts
        if part_rows % 16:
            total = sum(term[...].astype(f32) for term in terms[1:]) + terms[0][...].astype(f32)
        for part in range(parts):
            out = outs.pop(0)
            rows = slice(part * part_rows, (part + 1) * part_rows)
            if part_rows % 16:
                out[...] = total[rows].astype(out.dtype)
                continue
            values = sum(term[rows, :].astype(f32) for term in terms[1:]) + terms[0][rows, :].astype(f32)
            out[...] = values.astype(out.dtype)
            if fine:
                vector = values[:, :256] + values[:, 256:512]
                row = lax.broadcasted_iota(jnp.int32, (part_rows, 256), 0)
                here = (row % 32 >= 24) & (pl.program_id(0) == 0)
                if out.dtype == bf16:
                    high = vector.astype(bf16).astype(f32)
                    out[:, :256] = jnp.where(here, high, values[:, :256]).astype(bf16)
                    out[:, 256:512] = jnp.where(here, vector - high, values[:, 256:512]).astype(bf16)
                else:
                    out[:, :256] = jnp.where(here, vector, values[:, :256])


class Halving:
    def __init__(self, halves, stages, fine=False):
        self.keep, *self.sends = halves
        self.stages = stages
        self.fine = fine
        self.gots = None

    def post(self):
        stage = self.stages[0]
        self.stages = self.stages[1:]
        self.gots = []
        for part, send in enumerate(self.sends, 1):
            masks = {}
            for at, (axis, bit) in enumerate(stage):
                if (part >> (len(stage) - 1 - at)) & 1:
                    masks[axis] = masks.get(axis, 0) ^ bit
            axes = tuple(masks)
            if len(axes) == 1:
                size, mask, name = lax.axis_size(axes[0]), masks[axes[0]], axes[0]
            else:
                n_seq = lax.axis_size("seq")
                size = lax.axis_size("dp") * n_seq
                mask, name = masks["dp"] * n_seq + masks["seq"], ("dp", "seq")
            self.gots.append(lax.ppermute(send, name, [(i, i ^ mask) for i in range(size)]))


def advance(streams, passed, after, hold=()):
    adding = [stream for stream in streams if stream.gots is not None]
    fresh = [stream for stream in streams if stream.gots is None]
    passed = list(passed) + [send for stream in fresh for send in stream.sends]
    steps = 2 if sum(stream.keep.size for stream in adding) > 3 << 18 else 1
    operands, in_specs, out_specs, shapes, plans, loose = [], [], [], [], [], []
    for stream in adding:
        rows, width = stream.keep.shape
        tile = width // steps
        loose += [len(operands) + 1 + k for k in range(len(stream.gots))]
        operands += [stream.keep, *stream.gots]
        in_specs += [pl.BlockSpec((rows, tile), lambda j: (0, j))] * (1 + len(stream.gots))
        parts = 1 << len(stream.stages[0]) if stream.stages else 1
        plans.append((len(stream.gots), parts, stream.fine))
        new = [jax.ShapeDtypeStruct((rows // parts, width), bf16 if stream.stages else f32)] * parts
        shapes += new
        out_specs += [pl.BlockSpec((rows // parts, tile), lambda j: (0, j))] * parts
    first_in, first_out = len(operands), len(shapes)

    def body(*refs):
        add_kernel(*refs[:first_in], *refs[first_in + len(passed) :][:first_out], plans=plans)

    outs = run(
        body,
        after,
        operands + passed,
        in_specs + [pl.BlockSpec(memory_space=pl.ANY)] * len(passed),
        40,
        aliases={first_in + k: first_out + k for k in range(len(passed))},
        loose=loose,
        grid=(steps,),
        out_specs=out_specs + [pl.BlockSpec(memory_space=pl.ANY)] * len(passed),
        out_shape=shapes + [jax.ShapeDtypeStruct(a.shape, a.dtype) for a in passed],
        cost_estimate=cost(0, 0),
        name="add",
    )
    done = (outs[0],)
    outs = list(outs)
    for stream, (_, parts, _) in zip(adding, plans, strict=True):
        new = [outs.pop(0) for _ in range(parts)]
        if stream.stages:
            stream.keep, *stream.sends = new
            if stream in hold:
                stream.gots = None
            else:
                stream.post()
        else:
            stream.total = new[0]
    others = len(outs) - sum(len(stream.sends) for stream in fresh)
    others, outs = outs[:others], outs[others:]
    for stream in fresh:
        stream.sends = [outs.pop(0) for _ in stream.sends]
        stream.post()
    return done, others


def finish_kernel(most, keep, got, qkv_out, out_out, pool_out, gains, biases, up_bias, classes, class_bias, *, groups):
    chunk, width = out_out.shape
    total = keep[...].astype(f32) + got[...].astype(f32)
    each = width // groups
    for g in range(groups):
        for third in range(3):
            cols = slice(third * width + g * each, third * width + (g + 1) * each)
            if g == 0:
                qkv_out[:, cols] = most[:, third * each : (third + 1) * each]
            else:
                start = (g - 1) * width + third * each
                qkv_out[:, cols] = total[:chunk, start : start + each]
    out_out[...] = most[:, width : 2 * width]
    pool_out[...] = most[:, 2 * width : 3 * width]
    vector = total[chunk:, :256] + total[chunk:, 256:512]
    for row, source in enumerate((3, 0)):
        gains[row : row + 1, :] = vector[source : source + 1, :chunk]
    for row, source in enumerate((6, 7, 4, 5, 1, 2)):
        biases[row : row + 1, :] = vector[source : source + 1, :chunk]
    ramp = vector[:, 128:256]
    biases[6:7, :] = ramp[1:2, :chunk]
    up_bias[...] = ramp[0:1, : up_bias.shape[1]]
    classes[...] = ramp[2 : 2 + CLASSES, :chunk]
    class_bias[...] = jnp.transpose(ramp)[0:1, 2 + CLASSES : 2 + 2 * CLASSES]


def finish(most, last, groups, up_size, after):
    chunk, wide = most.shape
    width = wide // 3
    sizes = [(chunk, wide), (chunk, width), (chunk, width), (2, chunk), (7, chunk), (1, up_size), (CLASSES, chunk)]
    sizes.append((1, CLASSES))
    operands = (most, last.keep, last.gots[0])
    return run(
        functools.partial(finish_kernel, groups=groups),
        after,
        operands,
        [fixed(a.shape) for a in operands],
        16,
        loose=(2,),
        grid=(1,),
        out_specs=[fixed(size) for size in sizes],
        out_shape=[jax.ShapeDtypeStruct(size, f32) for size in sizes],
        cost_estimate=cost(0, 0),
        name="finish",
    )


def bits_of(size):
    return [1 << k for k in range(size.bit_length() - 1)]


def shards(
    hidden_in,
    lengths,
    labels,
    out_cotangent,
    qkv_weight,
    out_weight,
    up_weight,
    down_weight,
    pool_weight,
    class_weight,
    norm_gains,
    biases,
    up_bias,
    class_bias,
):
    positions, group, width = hidden_in.shape
    n_seq = lax.axis_size("seq")
    n_dp = lax.axis_size("dp")
    n_all = n_seq * n_dp
    seq_at = lax.axis_index("seq")
    me = lax.axis_index("dp") * n_seq + seq_at
    per = group // n_seq
    info = seq_at[None].astype(jnp.int32)
    me_info = me[None].astype(jnp.int32)
    classes = class_weight.shape[1]
    class_rows = jnp.zeros((128, width), bf16).at[:classes].set(class_weight.T)
    class_shift = jnp.full((1, 128), neg_big, f32).at[0, :classes].set(class_bias)

    seq_bits = [("seq", b) for b in bits_of(n_seq)]
    dp_bits = [("dp", b) for b in bits_of(n_dp)]
    chunk = width // n_all
    halved = chunk % 8 == 0

    x_send = split_rows(info, hidden_in.reshape(positions * group, width), positions, group, n_seq)
    x_parts = exchange(x_send)
    cot_send = split_rows(
        info, out_cotangent.reshape(positions * group, width), positions, group, n_seq, after=(x_send[0],)
    )
    cots = exchange(cot_send)
    x_rows, qkv, context, lse, n_one, q_one = attend(
        info, lengths, x_parts, qkv_weight, out_weight, biases, after=(cot_send[0],)
    )
    outs = feed(
        info, labels, cots, n_one, up_weight, up_bias[None, :], down_weight, norm_gains, biases, pool_weight,
        class_rows, class_shift,
    )
    middle_low, act, slope, grad_two, branch_grad, ramp_first, ramp_pre, ramp_out, sums_two, ramp_sums = outs[:10]
    final_parts = outs[10:]

    near = [seq_bits[:1], dp_bits[:1], seq_bits[1:]]
    one_way = [[entry] for entry in seq_bits[:1] + dp_bits[:1] + seq_bits[1:] + dp_bits[1:]]
    two_way = near[:1] + [near[1] + near[2]] + [[entry] for entry in dp_bits[1:]]
    flat = [entry for stage in one_way for entry in stage]
    places = halving_order(flat, n_seq)
    bits = tuple(bit * (n_seq if axis == "dp" else 1) for axis, bit in flat)
    streams = {}
    done = (branch_grad,)

    def stage(*names, passed=(), hold=()):
        nonlocal done
        if halved:
            done, passed = advance(
                [streams[name] for name in names], passed, done, [streams[name] for name in hold]
            )
        return passed

    def start(name, halves, stages, fine=False):
        nonlocal done
        streams[name] = Halving(halves, stages, fine)
        done = (halves[0],)

    if halved:
        start("down", tall_grad(me_info, act, branch_grad, bits, after=done), two_way)
    stage("down")
    filled = ()
    sums_one, up_sums = [], []
    for at in range(per):
        filled = feed_back(
            at, per, grad_two, branch_grad, slope, n_one, q_one, down_weight, up_weight, out_weight,
            norm_gains, filled, after=done,
        )
        sums_one.append(filled[4])
        up_sums.append(filled[5])
        filled = filled[:4]
        done = (sums_one[-1],)
        if at == 0:
            stage("down")
    pre_grad, grad_one, mix_grad, context_grad = filled
    if halved:
        start("up", wide_grad(me_info, middle_low, pre_grad, places, 1024, after=done), two_way)
    final_parts = exchange([final_parts[0], *stage("down", "up", passed=final_parts[1:])])

    groups = 3 if (width // PAIR) % 3 == 0 else 1
    count = width // PAIR // groups
    grads, qkv_sums = [], []
    for g in range(groups):
        grad, qkv_sum = attend_back(
            info, lengths, qkv, context_grad, context, lse, n_seq, g * count, count, after=done
        )
        grads.append(grad)
        qkv_sums.append(qkv_sum)
        done = (qkv_sum,)
        if g == 0:
            if halved:
                pairs = [(x_rows, grad), (context, mix_grad), (ramp_first, ramp_pre)]
                start("most", group_grad(me_info, pairs, (), None, places, after=done), one_way)
            final_parts = [final_parts[0], *stage("down", "up", "most", passed=final_parts[1:])]
    back = input_grad(grads, qkv_weight, grad_one, per, n_seq, after=done)
    done = (back[0],)
    if halved:
        pairs = [(x_rows, grad) for grad in grads[1:]]
        vectors = (sums_two, ramp_sums, *sums_one, *up_sums, *qkv_sums)
        start("last", group_grad(me_info, pairs, vectors, (per, groups), places, after=done), one_way, fine=True)
    back_parts = exchange(
        [back[0], *stage("down", "up", "most", "last", passed=back[1:], hold=("up",))]
    )
    hidden_out = merge_rows(info, final_parts, bf16, after=done)
    done = (hidden_out,)
    back_parts = [back[0], *stage("up", "most", "last", passed=back_parts[1:])]
    grad_in = merge_rows(info, back_parts, f32, after=done)
    done = (grad_in,)
    stage("up", "most", "last")
    stage("up", "most", "last")
    stage("most", "last")
    if halved:
        qkv_total, out_total, pool_total, gains_sum, biases_sum, up_bias_sum, class_sum, class_bias_sum = finish(
            streams["most"].total, streams["last"], groups, up_weight.shape[1] // n_all, done
        )
        up_bias_sum = up_bias_sum[0]
        class_sum = jnp.transpose(class_sum)
        class_bias_sum = class_bias_sum[0]
        up_total = streams["up"].total
        down_total = streams["down"].total
    else:

        def scatter(value):
            return lax.psum_scatter(value, ("dp", "seq"), scatter_dimension=0, tiled=True)

        wide = jnp.concatenate([grads[g][t] for t in range(3) for g in range(groups)], axis=1)
        qkv_total = scatter(tn(x_rows, wide))
        out_total = scatter(tn(context, mix_grad))
        up_total = scatter(tn(middle_low, pre_grad))
        down_total = scatter(tn(act, branch_grad))
        pool_total = scatter(
            lax.dot_general(ramp_first, ramp_pre, (((0,), (0,)), ((), ())), precision=highest)
        )
        table = jnp.concatenate(
            [sums_two[:3], sum(sums_one)[:3], jnp.concatenate(qkv_sums, axis=1)[:2], ramp_sums], axis=0
        )
        table = jnp.transpose(table.reshape(16, n_all, chunk), (1, 0, 2)).reshape(n_all, 16 * chunk)
        table = scatter(jnp.concatenate([table, sum(up_sums).reshape(n_all, -1)], axis=1))[0]
        vec = table[: 8 * chunk].reshape(8, chunk)
        ramp_vec = table[8 * chunk : 16 * chunk].reshape(8, chunk)
        up_bias_sum = table[16 * chunk :]
        gains_sum = jnp.stack([vec[3], vec[0]])
        biases_sum = jnp.stack([vec[6], vec[7], vec[4], vec[5], vec[1], vec[2], ramp_vec[1]])
        class_sum = jnp.transpose(ramp_vec[2 : 2 + classes])
        class_bias_sum = ramp_vec[2 + classes : 2 + 2 * classes, 0]
    ramp_logits = ramp_out.reshape(per, REC, -1)[:, 0, :classes]
    return (
        hidden_out.reshape(positions, group, width),
        ramp_logits,
        grad_in.reshape(positions, group, width),
        qkv_total,
        out_total,
        up_total,
        down_total,
        pool_total,
        class_sum,
        gains_sum,
        biases_sum,
        up_bias_sum,
        class_bias_sum,
    )


def solution(mesh):
    every = ("dp", "seq")
    rows = P("seq", "dp", None)
    return jax.shard_map(
        shards,
        mesh=mesh,
        in_specs=(rows, P("dp"), P(every), rows) + (P(),) * 10,
        out_specs=(
            rows,
            P(every, None),
            rows,
            P(every, None),
            P(every, None),
            P(every, None),
            P(every, None),
            P(every, None),
            P(every, None),
            P(None, every),
            P(None, every),
            P(every),
            P(),
        ),
        check_vma=False,
    )
```

```python
import functools

import jax
import jax.numpy as jnp
from jax import lax
from jax.experimental import pallas as pl
from jax.experimental.pallas import tpu as pltpu
from jax.sharding import PartitionSpec as P

HEAD_DIM = 64
PAIR = 2 * HEAD_DIM
REC = 8
CLASSES = 3
FEED_PARTS = 2

eps = 1e-12
neg_big = -1e30
highest = lax.Precision.HIGHEST
f32 = jnp.float32
bf16 = jnp.bfloat16
MIB = 1 << 20


def nn(left, right):
    return lax.dot_general(left, right, (((1,), (0,)), ((), ())), preferred_element_type=f32)


def nt(left, right):
    return lax.dot_general(left, right, (((1,), (1,)), ((), ())), preferred_element_type=f32)


def tn(left, right):
    return lax.dot_general(left, right, (((0,), (0,)), ((), ())), preferred_element_type=f32)


def cost(flops, nbytes, trans=0):
    return pl.CostEstimate(flops=1, bytes_accessed=1, transcendentals=0)


def smem():
    return pl.BlockSpec(memory_space=pltpu.SMEM)


def in_vmem():
    return pl.BlockSpec(memory_space=pltpu.VMEM)


def fixed(shape):
    return pl.BlockSpec(shape, lambda *_: (0,) * len(shape))


def once(shape):
    return pl.BlockSpec(shape, lambda *_: (0,) * len(shape), pipeline_mode=pl.Buffered(1))


def run(kernel, after, operands, in_specs, limit, out_shape, aliases=None, loose=(), **kwargs):
    skip = len(after)
    operands = [
        a
        if k in loose or spec.memory_space in (pltpu.VMEM, pltpu.SMEM)
        else pltpu.with_memory_space_constraint(a, pltpu.HBM)
        for k, (a, spec) in enumerate(zip(operands, in_specs, strict=True))
    ]
    after = [pltpu.with_memory_space_constraint(a, pltpu.HBM) for a in after]
    single = not isinstance(out_shape, list)
    shapes = [pltpu.HBM(a.shape, a.dtype) for a in ([out_shape] if single else out_shape)]

    def body(*refs):
        kernel(*refs[skip:])

    return pl.pallas_call(
        body,
        in_specs=[pl.BlockSpec(memory_space=pl.ANY)] * skip + list(in_specs),
        out_shape=shapes[0] if single else shapes,
        input_output_aliases={k + skip: v for k, v in (aliases or {}).items()},
        compiler_params=pltpu.CompilerParams(vmem_limit_bytes=limit * MIB),
        **kwargs,
    )(*after, *operands)


def three_parts(value):
    hi = value.astype(bf16)
    rest = value - hi.astype(f32)
    mid = rest.astype(bf16)
    low = (rest - mid.astype(f32)).astype(bf16)
    return jnp.concatenate([hi, mid, low], axis=0)


def fine_dot(dot, value, weight):
    rows = value.shape[0]
    parts = dot(jnp.concatenate([three_parts(value)], axis=0), weight)
    return parts[:rows] + parts[rows : 2 * rows] + parts[2 * rows :]


def split_kernel(info, rows, *outs):
    chunks = len(outs)
    per, span, _ = outs[0].shape
    group = chunks * per
    block = 16 * group
    own = info[0]
    dest = lax.broadcasted_iota(jnp.int32, (block, block), 0)
    source = lax.broadcasted_iota(jnp.int32, (block, block), 1)
    chunk = dest // (16 * per)
    wanted = (dest % 16) * group + per * (chunk ^ own) + (dest // 16) % per
    perm = jnp.where(source == wanted, 1.0, 0.0).astype(bf16)
    for b in range(span // 16):
        moved = nn(perm, rows[b * block : (b + 1) * block, :]).astype(bf16)
        for c in range(chunks):
            for q in range(per):
                at = (c * per + q) * 16
                outs[c][q, b * 16 : (b + 1) * 16, :] = moved[at : at + 16]


def split_rows(info, rows, positions, group, chunks, after=()):
    width = rows.shape[1]
    per = group // chunks
    steps = 2
    span = positions // steps
    return run(
        split_kernel,
        after,
        (info, rows),
        [smem(), pl.BlockSpec((span * group, width), lambda i: (i, 0))],
        16,
        grid=(steps,),
        out_specs=[pl.BlockSpec((per, span, width), lambda i: (0, i, 0))] * chunks,
        out_shape=[jax.ShapeDtypeStruct((per, positions, width), bf16)] * chunks,
        cost_estimate=cost(2 * rows.size * 16 * group, 4 * rows.size),
        name="split_rows",
    )


def merge_kernel(info, *refs):
    ins, out = refs[:-1], refs[-1]
    chunks = len(ins)
    per, span, _ = ins[0].shape
    group = chunks * per
    block = 16 * group
    own = info[0]
    dest = lax.broadcasted_iota(jnp.int32, (block, block), 0)
    source = lax.broadcasted_iota(jnp.int32, (block, block), 1)
    seq = dest % group
    wanted = (((seq // per) ^ own) * per + seq % per) * 16 + dest // group
    perm = jnp.where(source == wanted, 1.0, 0.0).astype(bf16)
    for b in range(span // 16):
        rows = jnp.concatenate(
            [ins[c][q, b * 16 : (b + 1) * 16, :] for c in range(chunks) for q in range(per)], axis=0
        )
        out[b * block : (b + 1) * block, :] = nn(perm, rows).astype(out.dtype)


def merge_rows(info, parts, dtype, after=()):
    chunks = len(parts)
    per, positions, width = parts[0].shape
    group = per * chunks
    steps = 2
    span = positions // steps
    return run(
        merge_kernel,
        after,
        (info, *parts),
        [smem()] + [pl.BlockSpec((per, span, width), lambda i: (0, i, 0))] * chunks,
        16,
        grid=(steps,),
        out_specs=pl.BlockSpec((span * group, width), lambda i: (i, 0)),
        out_shape=jax.ShapeDtypeStruct((positions * group, width), dtype),
        cost_estimate=cost(2 * positions * group * width * 16 * group, 6 * positions * group * width),
        name="merge_rows",
    )


def exchange(parts):
    size = lax.axis_size("seq")
    return [parts[0]] + [
        lax.ppermute(parts[c], "seq", [(i, i ^ c) for i in range(size)]) for c in range(1, size)
    ]


def row_stats(resid):
    mean = jnp.mean(resid, axis=-1, keepdims=True)
    centred = resid - mean
    scale = lax.rsqrt(jnp.mean(centred * centred, axis=-1, keepdims=True) + eps)
    return centred * scale, scale


def attend_kernel(info, lengths, *refs):
    chunks = len(refs) - 10
    parts = refs[:chunks]
    qkv_w, out_w, biases, x_out, qkv, context, lse, normed, scale, stats = refs[chunks:]
    width = out_w.shape[0]
    span = parts[0].shape[1]
    length = chunks * span
    pairs = width // PAIR
    own = info[0]
    live_len = lengths[own * pl.num_programs(0) + pl.program_id(0)]
    x_out[...] = jnp.concatenate([part[0] for part in parts], axis=0)
    for third in range(3):
        cols = slice(third * width, (third + 1) * width)
        block = nn(x_out[...], qkv_w[:, cols])
        if third == 0:
            block = block + biases[0:1, :]
        elif third == 2:
            block = block + biases[1:2, :]
        qkv[:, cols] = block.astype(bf16)
    lane = lax.broadcasted_iota(jnp.int32, (length, PAIR), 1)
    row = lax.broadcasted_iota(jnp.int32, (length, PAIR), 0)
    pos = ((row // span) ^ own) * span + row % span
    key_ext = jnp.where((lane == 0) & (pos >= live_len), neg_big, 0.0).astype(bf16)
    query_ext = jnp.where(lane == 0, 1.0, 0.0).astype(bf16)
    low_half = lane < HEAD_DIM
    masks = [jnp.where(low_half, 1.0, 0.0).astype(bf16), jnp.where(low_half, 0.0, 1.0).astype(bf16)]
    stats[...] = jnp.zeros_like(stats)

    def one_pair(i, carry):
        start = pl.multiple_of(i * PAIR, PAIR)
        queries = qkv[:, pl.ds(start, PAIR)] * bf16(HEAD_DIM**-0.5)
        keys = jnp.concatenate([qkv[:, pl.ds(start + width, PAIR)], key_ext], axis=1)
        values = qkv[:, pl.ds(start + 2 * width, PAIR)]
        total = None
        tops = []
        for head in range(2):
            scores = nt(jnp.concatenate([queries * masks[head], query_ext], axis=1), keys)
            top = jnp.max(scores, axis=1, keepdims=True)
            weights = jnp.exp(scores - top).astype(bf16)
            part = nn(weights, jnp.concatenate([values * masks[head], masks[head]], axis=1))
            total = part if total is None else total + part
            tops.append(top)
        row_total = total[:, PAIR:]
        context[:, pl.ds(start, PAIR)] = (total[:, :PAIR] / row_total).astype(bf16)
        log_total = jnp.where(low_half, tops[0], tops[1]) + jnp.log(row_total)
        swapped = pltpu.roll(log_total, HEAD_DIM, 1)
        stats[...] = jnp.where(
            lane == 2 * i, log_total, jnp.where(lane == 2 * i + 1, swapped, stats[...])
        )
        return carry

    lax.fori_loop(0, pairs, one_pair, 0, unroll=pairs)
    lse[0] = jnp.transpose(stats[...])[: lse.shape[1], :]
    resid = x_out[...].astype(f32) + (nn(context[...], out_w[...]) + biases[2:3, :])
    n_one, q_one = row_stats(resid)
    normed[...] = n_one
    scale[...] = q_one


def attend(info, lengths, parts, qkv_w, out_w, biases, after=()):
    chunks = len(parts)
    per, span, width = parts[0].shape
    length = chunks * span
    rows = per * length
    heads = width // HEAD_DIM
    head_rows = -(-heads // 8) * 8
    by_seq = lambda i: (i, 0)
    return run(
        attend_kernel,
        after,
        (info, lengths, *parts, qkv_w, out_w, biases),
        [smem()] * 2
        + [pl.BlockSpec((1, span, width), lambda i: (i, 0, 0))] * chunks
        + [in_vmem(), once(out_w.shape), once(biases.shape)],
        30,
        grid=(per,),
        out_specs=[
            pl.BlockSpec((length, width), by_seq),
            pl.BlockSpec((length, 3 * width), by_seq),
            pl.BlockSpec((length, width), by_seq),
            pl.BlockSpec((1, head_rows, length), lambda i: (i, 0, 0)),
            pl.BlockSpec((length, width), by_seq),
            pl.BlockSpec((length, 1), by_seq),
        ],
        out_shape=[
            jax.ShapeDtypeStruct((rows, width), bf16),
            jax.ShapeDtypeStruct((rows, 3 * width), bf16),
            jax.ShapeDtypeStruct((rows, width), bf16),
            jax.ShapeDtypeStruct((per, head_rows, length), f32),
            jax.ShapeDtypeStruct((rows, width), f32),
            jax.ShapeDtypeStruct((rows, 1), f32),
        ],
        scratch_shapes=[pltpu.VMEM((length, PAIR), f32)],
        cost_estimate=cost(
            8 * rows * width * width + 8 * rows * length * width, 20 * rows * width + 8 * width * width,
            rows * length * heads,
        ),
        name="attend",
    )


def gelu_pair(x):
    cdf = 0.5 + 0.5 * lax.erf(x * 0.5**0.5)
    bell = jnp.exp(-0.5 * (x * x))
    return x * cdf, cdf + x * bell * (0.5 / jnp.pi) ** 0.5


def norm_back(upper, normed, scale, gain):
    scaled = upper * gain
    mean_part = jnp.mean(scaled, axis=-1, keepdims=True)
    proj_part = jnp.mean(scaled * normed, axis=-1, keepdims=True)
    return scale * (scaled - mean_part - normed * proj_part)


def col_sum(values):
    return jnp.sum(values, axis=0, keepdims=True)


def feed_kernel(info, labels, *refs):
    chunks = (len(refs) - 20) // 2
    cots = refs[:chunks]
    normed, up_w, up_b, down_w, gains, biases, pool_w, class_w, class_b = refs[chunks : chunks + 9]
    middle_out, act, slope, grad_two, branch_grad = refs[chunks + 9 : chunks + 14]
    ramp_first, ramp_pre, ramp_out, sums, ramp_sums = refs[chunks + 14 : chunks + 19]
    finals = refs[chunks + 19 : -1]
    n_two = refs[-1]
    span = finals[0].shape[1]
    own = info[0]

    @pl.when(pl.program_id(0) == 0)
    def _():
        sums[...] = jnp.zeros_like(sums)
        ramp_sums[...] = jnp.zeros_like(ramp_sums)

    hidden = up_w.shape[1]
    tile = 256
    length = chunks * span
    block = length // FEED_PARTS
    scales = []
    for part in range(FEED_PARTS):
        rows = slice(part * block, (part + 1) * block)
        middle = normed[rows, :] * gains[0:1, :] + biases[3:4, :]
        middle_out[rows, :] = middle.astype(bf16)
        for j in range(hidden // tile):
            cols = slice(j * tile, (j + 1) * tile)
            pre = nn(middle_out[rows, :], up_w[:, cols]) + up_b[:, cols]
            value, grad = gelu_pair(pre)
            act[rows, cols] = value.astype(bf16)
            slope[rows, cols] = grad.astype(bf16)
        branch = nn(act[rows, :], down_w[...]) + biases[4:5, :]
        middle = normed[rows, :] * gains[0:1, :] + biases[3:4, :]
        normed_two, q_two = row_stats(middle + branch)
        n_two[rows, :] = normed_two
        scales.append(q_two)
    for c in range(chunks):
        rows = slice(c * span, (c + 1) * span)
        finals[c][0] = (n_two[rows, :] * gains[1:2, :] + biases[5:6, :]).astype(bf16)
    label = labels[pl.program_id(0)]
    start = pl.multiple_of(own * span, 8)
    first = (n_two[pl.ds(start, REC), :] * gains[1:2, :] + biases[5:6, :]).astype(bf16)
    pooled = jnp.tanh(nn(first, pool_w[...]) + biases[6:7, :])
    logits = fine_dot(nt, pooled, class_w[...]) + class_b[...]
    expo = jnp.exp(logits - jnp.max(logits, axis=1, keepdims=True))
    lane = lax.broadcasted_iota(jnp.int32, logits.shape, 1)
    g_logits = expo / jnp.sum(expo, axis=1, keepdims=True) - jnp.where(lane == label, 1.0, 0.0)
    g_pre = fine_dot(nn, g_logits, class_w[...]) * (1.0 - pooled * pooled)
    g_first = fine_dot(nt, g_pre, pool_w[...])
    first_row = lax.broadcasted_iota(jnp.int32, (REC, 1), 0) == 0
    ramp_first[...] = jnp.where(first_row, first.astype(f32), 0.0)
    ramp_pre[...] = jnp.where(first_row, g_pre, 0.0)
    ramp_out[...] = logits
    ramp_sums[1:2, :] += g_pre[0:1, :]
    for c in range(CLASSES):
        at_class = jnp.sum(jnp.where(lane == c, g_logits, 0.0), axis=1, keepdims=True)[0:1, :]
        ramp_sums[2 + c : 3 + c, :] += at_class * pooled[0:1, :]
        ramp_sums[2 + CLASSES + c : 3 + CLASSES + c, :] += at_class + jnp.zeros_like(pooled[0:1, :])
    sum_rows = [0.0, 0.0, 0.0]
    for part in range(FEED_PARTS):
        rows = slice(part * block, (part + 1) * block)
        here = cots[part * chunks // FEED_PARTS : (part + 1) * chunks // FEED_PARTS]
        cot = jnp.concatenate([chunk[0] for chunk in here], axis=0).astype(f32)
        row = part * block + lax.broadcasted_iota(jnp.int32, (block, 1), 0)
        g_final = cot + jnp.where(row == own * span, g_first[0:1, :], 0.0)
        normed_two = n_two[rows, :]
        g_two = norm_back(g_final, normed_two, scales[part], gains[1:2, :])
        grad_two[rows, :] = g_two
        low = g_two.astype(bf16)
        branch_grad[rows, :] = low
        for k, values in enumerate((g_final * normed_two, low.astype(f32), g_final)):
            sum_rows[k] = sum_rows[k] + col_sum(values)
    for k in range(3):
        sums[k : k + 1, :] += sum_rows[k]


def feed(info, labels, cots, normed, up_w, up_b, down_w, gains, biases, pool_w, class_w, class_b, after=()):
    chunks = len(cots)
    per, span, _ = cots[0].shape
    rows, width = normed.shape
    length = rows // per
    hidden = up_w.shape[1]
    by_seq = lambda i: (i, 0)
    row_block = pl.BlockSpec((length, width), by_seq)
    wide_block = pl.BlockSpec((length, hidden), by_seq)
    part = pl.BlockSpec((1, span, width), lambda i: (i, 0, 0))
    consts = (up_w, up_b, down_w, gains, biases, pool_w, class_w, class_b)
    return run(
        feed_kernel,
        after,
        (info, labels, *cots, normed, *consts),
        [smem()] * 2 + [part] * chunks + [row_block, in_vmem()] + [once(a.shape) for a in consts[1:]],
        44,
        grid=(per,),
        out_specs=[
            row_block, wide_block, wide_block, row_block, row_block,
            pl.BlockSpec((REC, width), by_seq), pl.BlockSpec((REC, width), by_seq),
            pl.BlockSpec((REC, class_b.shape[1]), by_seq), fixed((8, width)), fixed((8, width)),
        ]
        + [part] * chunks,
        out_shape=[
            jax.ShapeDtypeStruct((rows, width), bf16),
            jax.ShapeDtypeStruct((rows, hidden), bf16),
            jax.ShapeDtypeStruct((rows, hidden), bf16),
            jax.ShapeDtypeStruct((rows, width), f32),
            jax.ShapeDtypeStruct((rows, width), bf16),
            jax.ShapeDtypeStruct((per * REC, width), f32),
            jax.ShapeDtypeStruct((per * REC, width), f32),
            jax.ShapeDtypeStruct((per * REC, class_b.shape[1]), f32),
            jax.ShapeDtypeStruct((8, width), f32),
            jax.ShapeDtypeStruct((8, width), f32),
        ]
        + [jax.ShapeDtypeStruct((per, span, width), bf16)] * chunks,
        scratch_shapes=[pltpu.VMEM((length, width), f32)],
        cost_estimate=cost(4 * rows * width * hidden, 4 * rows * hidden + 4 * width * hidden + 12 * rows * width),
        name="feed",
    )


def feed_back_kernel(*refs, carried):
    grad_two, branch_grad, slope, n_one, q_one, down_w, up_w, out_w, gains = refs[:9]
    pre_grad, grad_one, mix_grad, context_grad, sums, up_sums = refs[9 + carried :]

    @pl.when(pl.program_id(0) == 0)
    def _():
        sums[...] = jnp.zeros_like(sums)
        up_sums[...] = jnp.zeros_like(up_sums)

    hidden = up_w.shape[1]
    tile = 256
    for j in range(hidden // tile):
        cols = slice(j * tile, (j + 1) * tile)
        pre = nt(branch_grad[...], down_w[cols, :]) * slope[:, cols].astype(f32)
        low = pre.astype(bf16)
        pre_grad[:, cols] = low
        up_sums[:, cols] += col_sum(low.astype(f32))
    g_middle = grad_two[...] + nt(pre_grad[...], up_w[...])
    normed = n_one[...]
    sums[0:1, :] += col_sum(g_middle * normed)
    sums[2:3, :] += col_sum(g_middle)
    g_one = norm_back(g_middle, normed, q_one[...], gains[0:1, :])
    grad_one[...] = g_one
    mix_grad[...] = g_one.astype(bf16)
    sums[1:2, :] += col_sum(mix_grad[...].astype(f32))
    context_grad[...] = nt(mix_grad[...], out_w[...]).astype(bf16)


def feed_back(first, steps, blocks, grad_two, branch_grad, slope, n_one, q_one, down_w, up_w, out_w, gains, before, after=()):
    rows, width = grad_two.shape
    hidden = slope.shape[1]
    block = rows // blocks
    by_row = lambda i: (first + i, 0)
    row_block = pl.BlockSpec((block, width), by_row)
    wide_block = pl.BlockSpec((block, hidden), by_row)
    thin_block = pl.BlockSpec((block, 1), by_row)
    return run(
        functools.partial(feed_back_kernel, carried=len(before)),
        after,
        (grad_two, branch_grad, slope, n_one, q_one, down_w, up_w, out_w, gains, *before),
        [row_block, row_block, wide_block, row_block, thin_block]
        + [in_vmem()] * 2
        + [once(out_w.shape), once(gains.shape)]
        + [pl.BlockSpec(memory_space=pl.ANY)] * len(before),
        32,
        aliases={9 + k: k for k in range(len(before))},
        grid=(steps,),
        out_specs=[wide_block, row_block, row_block, row_block, fixed((8, width)), fixed((1, hidden))],
        out_shape=[
            jax.ShapeDtypeStruct((rows, hidden), bf16),
            jax.ShapeDtypeStruct((rows, width), f32),
            jax.ShapeDtypeStruct((rows, width), bf16),
            jax.ShapeDtypeStruct((rows, width), bf16),
            jax.ShapeDtypeStruct((8, width), f32),
            jax.ShapeDtypeStruct((1, hidden), f32),
        ],
        cost_estimate=cost(0, 0),
        name="feed_back",
    )


def attend_back_kernel(info, lengths, queries_in, keys_in, values_in, context_grad, context, lse, grads, sums, *, chunks, first):
    length, cols = queries_in.shape
    first = first + pl.program_id(0) * (cols // PAIR)
    at_seq = pl.program_id(1)
    span = length // chunks
    own = info[0]
    live_len = lengths[own * pl.num_programs(1) + at_seq]
    factor = HEAD_DIM**-0.5
    lane = lax.broadcasted_iota(jnp.int32, (length, PAIR), 1)
    row = lax.broadcasted_iota(jnp.int32, (length, PAIR), 0)
    pos = ((row // span) ^ own) * span + row % span
    key_ext = jnp.where((lane == 0) & (pos >= live_len), neg_big, 0.0).astype(bf16)
    query_ext = jnp.where(lane == 0, 1.0, 0.0).astype(bf16)
    low_half = lane < HEAD_DIM
    masks = [jnp.where(low_half, 1.0, 0.0).astype(bf16), jnp.where(low_half, 0.0, 1.0).astype(bf16)]
    picks = jnp.where(
        lax.broadcasted_iota(jnp.int32, (8, PAIR), 1) // HEAD_DIM
        == lax.broadcasted_iota(jnp.int32, (8, PAIR), 0),
        1.0,
        0.0,
    ).astype(bf16)
    parts = 1
    block = length // parts

    @pl.when(at_seq == 0)
    def _():
        sums[...] = jnp.zeros_like(sums)

    for pair in range(cols // PAIR):
        at = slice(pair * PAIR, (pair + 1) * PAIR)
        queries = queries_in[:, at] * bf16(factor)
        keys = jnp.concatenate([keys_in[:, at], key_ext], axis=1)
        values = values_in[:, at]
        ctx_grad = context_grad[:, at]
        product = ctx_grad.astype(f32) * context[:, at].astype(f32)
        high = product.astype(bf16)
        low = (product - high.astype(f32)).astype(bf16)
        row_dots = nt(picks, high) + nt(picks, low)
        g_queries = None
        g_keys = [None] * parts
        g_values = [None] * parts
        for head in range(2):
            masked_q = queries * masks[head]
            long_q = jnp.concatenate([masked_q, query_ext], axis=1)
            masked_g = ctx_grad * masks[head]
            masked_k = keys_in[:, at] * masks[head]
            log_total = lse[0, pl.ds(2 * (first + pair) + head, 1), :]
            row_dot = row_dots[head : head + 1, :]
            for c in range(parts):
                rows = slice(c * block, (c + 1) * block)
                weights = jnp.exp(nt(keys[rows], long_q) - log_total)
                part = nn(weights.astype(bf16), masked_g)
                g_values[c] = part if g_values[c] is None else g_values[c] + part
                g_scores = (weights * (nt(values[rows], masked_g) - row_dot)).astype(bf16)
                part = nn(g_scores, masked_q)
                g_keys[c] = part if g_keys[c] is None else g_keys[c] + part
                part = tn(g_scores, masked_k[rows])
                g_queries = part if g_queries is None else g_queries + part
        grads[0, :, at] = (g_queries * factor).astype(bf16)
        for c in range(parts):
            rows = slice(c * block, (c + 1) * block)
            grads[1, rows, at] = g_keys[c].astype(bf16)
            grads[2, rows, at] = g_values[c].astype(bf16)
        sums[0:1, at] += col_sum(grads[0, :, at].astype(f32))
        sums[1:2, at] += col_sum(grads[2, :, at].astype(f32))


def attend_back(info, lengths, qkv, context_grad, context, lse, chunks, first, count, groups, after=()):
    rows, width = context.shape
    per, head_rows, length = lse.shape
    cols = count * PAIR
    blocks = width // cols
    spec = lambda third: pl.BlockSpec((length, cols), lambda g, q: (q, third * blocks + first // count + g))
    return run(
        functools.partial(attend_back_kernel, chunks=chunks, first=first),
        after,
        (info, lengths, qkv, qkv, qkv, context_grad, context, lse),
        [
            smem(),
            smem(),
            spec(0),
            spec(1),
            spec(2),
            spec(0),
            spec(0),
            pl.BlockSpec((1, head_rows, length), lambda g, q: (q, 0, 0)),
        ],
        40,
        grid=(groups, per),
        out_specs=[
            pl.BlockSpec((3, length, cols), lambda g, q: (0, q, g)),
            pl.BlockSpec((8, cols), lambda g, q: (0, g)),
        ],
        out_shape=[
            jax.ShapeDtypeStruct((3, rows, groups * cols), bf16),
            jax.ShapeDtypeStruct((8, groups * cols), f32),
        ],
        cost_estimate=cost(0, 0),
        name="attend_back",
    )


def input_grad_kernel(*refs, groups):
    grads = refs[:groups]
    qkv_w, grad_one = refs[groups : groups + 2]
    outs = refs[groups + 2 :]
    width = grad_one.shape[1]
    total = grad_one[...]
    offset = 0
    for grad in grads:
        each = grad.shape[2]
        for third in range(3):
            start = third * width + offset
            total = total + nt(grad[third], qkv_w[:, start : start + each])
        offset += each
    span = outs[0].shape[1]
    for c, out in enumerate(outs):
        out[0] = total[c * span : (c + 1) * span].astype(bf16)


def input_grad(grads, qkv_w, grad_one, per, chunks, after=()):
    groups = len(grads)
    rows, width = grad_one.shape
    length = rows // per
    span = length // chunks
    return run(
        functools.partial(input_grad_kernel, groups=groups),
        after,
        (*grads, qkv_w, grad_one),
        [pl.BlockSpec((3, length, grad.shape[2]), lambda i: (0, i, 0)) for grad in grads]
        + [in_vmem(), pl.BlockSpec((length, width), lambda i: (i, 0))],
        32,
        grid=(per,),
        out_specs=[pl.BlockSpec((1, span, width), lambda i: (i, 0, 0))] * chunks,
        out_shape=[jax.ShapeDtypeStruct((per, span, width), bf16)] * chunks,
        cost_estimate=cost(6 * rows * width * width, 12 * rows * width + 6 * width * width),
        name="input_grad",
    )


def chunk_at(me, relative, chunk):
    return pl.ds(pl.multiple_of((me ^ relative) * chunk, 8), chunk)


def tall_grad_kernel(info, left, right, keep, send, total, *, bits, chunk):
    total[...] = tn(left[...], right[...])
    here = left.shape[1] // chunk
    me = info[0]
    for target, other in ((keep, 0), (send, 1)):
        for k in range(0, here, 2):
            source = k + ((me % 2) ^ other)
            relative = (pl.program_id(0) * here + source) ^ me
            place = 0
            for at, bit in enumerate(bits[1:]):
                place = place + ((relative // bit) % 2) * (1 << (len(bits) - 2 - at))
            rows = total[pl.ds(pl.multiple_of(source * chunk, 8), chunk), :]
            target[pl.ds(pl.multiple_of(place * chunk, 16), chunk), :] = rows.astype(bf16)


def tall_grad(me, left, right, bits, after=()):
    rows, depth = left.shape
    width = right.shape[1]
    chunk = depth >> len(bits)
    block = 8 * chunk
    return run(
        functools.partial(tall_grad_kernel, bits=bits, chunk=chunk),
        after,
        (me, left, right),
        [smem(), pl.BlockSpec((rows, block), lambda j: (0, j)), fixed((rows, width))],
        24,
        grid=(depth // block,),
        out_specs=[fixed((depth // 2, width))] * 2,
        out_shape=[jax.ShapeDtypeStruct((depth // 2, width), bf16)] * 2,
        scratch_shapes=[pltpu.VMEM((block, width), f32)],
        cost_estimate=cost(0, 0),
        name="tall_grad",
    )


def wide_grad_kernel(info, left, right, keep, send, left_t, total, *, order, chunk):
    @pl.when(pl.program_id(0) == 0)
    def _():
        left_t[...] = jnp.transpose(left[...])

    me = info[0]
    half = len(order) // 2
    parts, _, tile = total.shape
    for part in range(parts):
        cols = slice(part * tile, (part + 1) * tile)
        total[part] = nn(left_t[...], right[:, cols])
        for at in range(0, len(order), 2):
            rows = jnp.concatenate([total[part, chunk_at(me, order[at + k], chunk), :] for k in range(2)], axis=0)
            target = keep if at < half else send
            row = (at % half) * chunk
            target[row : row + 2 * chunk, cols] = rows.astype(bf16)


def wide_grad(me, left, right, order, tile, after=()):
    rows, depth = left.shape
    width = right.shape[1]
    return run(
        functools.partial(wide_grad_kernel, order=order, chunk=depth // len(order)),
        after,
        (me, left, right),
        [smem(), fixed((rows, depth)), pl.BlockSpec((rows, tile), lambda j: (0, j))],
        32,
        grid=(width // tile,),
        out_specs=[pl.BlockSpec((depth // 2, tile), lambda j: (0, j))] * 2,
        out_shape=[jax.ShapeDtypeStruct((depth // 2, width), bf16)] * 2,
        scratch_shapes=[pltpu.VMEM((depth, rows), bf16), pltpu.VMEM((tile // 256, depth, 256), f32)],
        cost_estimate=cost(2 * rows * depth * width, 2 * rows * (depth + width) + 2 * depth * width),
        name="wide_grad",
    )


def fill_table(table, near, vectors, counts, chunk):
    per, groups = counts
    sums_two, ramp_sums = vectors[:2]
    sums_one = vectors[2 : 2 + per]
    up_sums = vectors[2 + per : 2 + 2 * per]
    qkv_sums = vectors[2 + 2 * per :]
    near[0:3, :] = sums_two[0:3, :]
    near[3:6, :] = sum(ref[0:3, :] for ref in sums_one)
    offset = 0
    for ref in qkv_sums:
        near[6:8, offset : offset + ref.shape[1]] = ref[0:2, :]
        offset += ref.shape[1]
    ups = sum(ref[...] for ref in up_sums)
    owners = table.shape[0]
    wide = ups.shape[1] // owners // 2
    table[...] = jnp.zeros_like(table)
    for k in range(owners):
        cols = slice(k * chunk, (k + 1) * chunk)
        table[k, :, 0:chunk] = near[:, cols]
        table[k, :, chunk : 2 * chunk] = ramp_sums[:, cols]
        for row in range(2):
            start = (2 * k + row) * wide
            table[k, row : row + 1, 2 * chunk : 2 * chunk + wide] = ups[:, start : start + wide]


def group_grad_kernel(info, *refs, order, chunk, jobs, counts):
    extra = counts is not None
    scratch = 3 if extra else 1
    keep, send = refs[-2 - scratch : -scratch]
    total = refs[-scratch]
    at_ref = 0
    column = 0
    for thirds in jobs:
        left, right = refs[at_ref : at_ref + 2]
        at_ref += 2
        if left.shape[0] < 128:
            high = right[...].astype(bf16)
            low = (right[...] - high.astype(f32)).astype(bf16)
            lefts = left[...].astype(bf16)
            product = tn(jnp.concatenate([lefts, lefts], axis=0), jnp.concatenate([high, low], axis=0))
            total[:, column : column + high.shape[1]] = product
            column += high.shape[1]
            continue
        left_t = jnp.transpose(left[...])
        for third in range(thirds or 1):
            block = right[third] if thirds else right[...]
            total[:, column : column + block.shape[1]] = nn(left_t, block)
            column += block.shape[1]
    me = info[0]
    half = len(order) // 2
    if extra:
        table, near = refs[-2:]
        fill_table(table, near, refs[at_ref : at_ref + 2 + 2 * counts[0] + counts[1]], counts, chunk)
        for k in range(len(order)):
            high = table[k].astype(bf16).astype(f32)
            total[k * chunk : k * chunk + 8, column:] = high
            total[k * chunk + 8 : k * chunk + 16, column:] = table[k] - high
            total[k * chunk + 16 : (k + 1) * chunk, column:] = jnp.zeros((chunk - 16, high.shape[1]), f32)
    for at in range(0, len(order), 2):
        rows = jnp.concatenate([total[chunk_at(me, order[at + k], chunk), :] for k in range(2)], axis=0)
        target = keep if at < half else send
        row = (at % half) * chunk
        target[row : row + 2 * chunk, :] = rows.astype(bf16)


def group_grad(me, pairs, vectors, counts, order, after=()):
    rows, depth = pairs[0][0].shape
    jobs = tuple(right.shape[0] if right.ndim == 3 else 0 for _, right in pairs)
    width = sum((right.shape[0] if right.ndim == 3 else 1) * right.shape[-1] for _, right in pairs)
    chunk = depth // len(order)
    extra = counts is not None
    width += 128 if extra else 0
    tall = depth // 2
    operands = [a for pair in pairs for a in pair] + list(vectors)
    scratch = [pltpu.VMEM((depth, width), f32)]
    if extra:
        scratch += [pltpu.VMEM((len(order), 8, 128), f32), pltpu.VMEM((8, depth), f32)]
    return run(
        functools.partial(group_grad_kernel, order=order, chunk=chunk, jobs=jobs, counts=counts),
        after,
        (me, *operands),
        [smem()] + [fixed(a.shape) for a in operands],
        48,
        grid=(1,),
        out_specs=[fixed((tall, width))] * 2,
        out_shape=[jax.ShapeDtypeStruct((tall, width), bf16)] * 2,
        scratch_shapes=scratch,
        cost_estimate=cost(0, 0),
        name="group_grad",
    )


def halving_order(stages, n_seq):
    bits = [bit * (n_seq if axis == "dp" else 1) for axis, bit in stages]
    count = len(bits)
    return [
        sum(bit for at, bit in enumerate(bits) if (place >> (count - 1 - at)) & 1) for place in range(1 << count)
    ]


def renew(values, chunk):
    groups = values.reshape(-1, chunk // 8, 8, values.shape[1])
    vector = groups[:, 0] + groups[:, 1]
    high = vector.astype(bf16).astype(f32)
    rest = [groups[:, k] for k in range(2, chunk // 8)]
    return jnp.stack([high, vector - high, *rest], axis=1).reshape(values.shape)


def add_kernel(*refs, plans):
    count = sum(1 + gots for gots, _, _ in plans)
    ins, outs = list(refs[:count]), list(refs[count:])
    for gots, parts, chunk in plans:
        terms = [ins.pop(0) for _ in range(1 + gots)]
        part_rows = terms[0].shape[0] // parts
        whole_rows = part_rows % 16 == 0
        if not whole_rows:
            total = sum(term[...].astype(f32) for term in terms[1:]) + terms[0][...].astype(f32)
        for part in range(parts):
            out = outs.pop(0)
            rows = slice(part * part_rows, (part + 1) * part_rows)
            if whole_rows:
                values = sum(term[rows, :].astype(f32) for term in terms[1:]) + terms[0][rows, :].astype(f32)
            else:
                values = total[rows]
            if chunk:
                out[:, :-128] = values[:, :-128].astype(out.dtype)
                out[:, -128:] = renew(values[:, -128:], chunk).astype(out.dtype)
            else:
                out[...] = values.astype(out.dtype)


class Halving:
    def __init__(self, halves, stages, fine=0):
        self.keep, *self.sends = halves
        self.stages = stages
        self.fine = fine
        self.gots = None

    def post(self):
        stage = self.stages[0]
        self.stages = self.stages[1:]
        self.gots = []
        for part, send in enumerate(self.sends, 1):
            masks = {}
            for at, (axis, bit) in enumerate(stage):
                if (part >> (len(stage) - 1 - at)) & 1:
                    masks[axis] = masks.get(axis, 0) ^ bit
            axes = tuple(masks)
            if len(axes) == 1:
                size, mask, name = lax.axis_size(axes[0]), masks[axes[0]], axes[0]
            else:
                n_seq = lax.axis_size("seq")
                size = lax.axis_size("dp") * n_seq
                mask, name = masks["dp"] * n_seq + masks["seq"], ("dp", "seq")
            self.gots.append(lax.ppermute(send, name, [(i, i ^ mask) for i in range(size)]))


def advance(streams, passed, after, hold=()):
    adding = [stream for stream in streams if stream.gots is not None]
    fresh = [stream for stream in streams if stream.gots is None]
    passed = list(passed) + [send for stream in fresh for send in stream.sends]
    steps = 2 if sum(stream.keep.size for stream in adding) > 3 << 18 and not any(s.fine for s in adding) else 1
    operands, in_specs, out_specs, shapes, plans, loose = [], [], [], [], [], []
    for stream in adding:
        rows, width = stream.keep.shape
        tile = width // steps
        loose += [len(operands) + 1 + k for k in range(len(stream.gots))]
        operands += [stream.keep, *stream.gots]
        in_specs += [pl.BlockSpec((rows, tile), lambda j: (0, j))] * (1 + len(stream.gots))
        parts = 1 << len(stream.stages[0]) if stream.stages else 1
        plans.append((len(stream.gots), parts, stream.fine))
        new = [jax.ShapeDtypeStruct((rows // parts, width), bf16 if stream.stages else f32)] * parts
        shapes += new
        out_specs += [pl.BlockSpec((rows // parts, tile), lambda j: (0, j))] * parts
    first_in, first_out = len(operands), len(shapes)

    def body(*refs):
        add_kernel(*refs[:first_in], *refs[first_in + len(passed) :][:first_out], plans=plans)

    outs = run(
        body,
        after,
        operands + passed,
        in_specs + [pl.BlockSpec(memory_space=pl.ANY)] * len(passed),
        40,
        aliases={first_in + k: first_out + k for k in range(len(passed))},
        loose=loose,
        grid=(steps,),
        out_specs=out_specs + [pl.BlockSpec(memory_space=pl.ANY)] * len(passed),
        out_shape=shapes + [jax.ShapeDtypeStruct(a.shape, a.dtype) for a in passed],
        cost_estimate=cost(0, 0),
        name="add",
    )
    done = (outs[0],)
    outs = list(outs)
    for stream, (_, parts, _) in zip(adding, plans, strict=True):
        new = [outs.pop(0) for _ in range(parts)]
        if stream.stages:
            stream.keep, *stream.sends = new
            if stream in hold:
                stream.gots = None
            else:
                stream.post()
        else:
            stream.total = new[0]
    others = len(outs) - sum(len(stream.sends) for stream in fresh)
    others, outs = outs[:others], outs[others:]
    for stream in fresh:
        stream.sends = [outs.pop(0) for _ in stream.sends]
        stream.post()
    return done, others


def finish_kernel(most, keep, *refs, split, gots):
    qkv_out, out_out, pool_out, gains, biases, up_bias, classes, class_bias = refs[gots:]
    chunk, width = out_out.shape
    total = sum(ref[...].astype(f32) for ref in refs[:gots]) + keep[...].astype(f32)
    for third in range(3):
        start = third * width
        qkv_out[:, start : start + split] = most[:, third * split : (third + 1) * split]
        rest = width - split
        qkv_out[:, start + split : start + width] = total[:, third * rest : (third + 1) * rest]
    out_out[...] = most[:, 3 * split : 3 * split + width]
    pool_out[...] = most[:, 3 * split + width :]
    vector = total[0:8, -128:] + total[8:16, -128:]
    for row, source in enumerate((3, 0)):
        gains[row : row + 1, :] = vector[source : source + 1, :chunk]
    for row, source in enumerate((6, 7, 4, 5, 1, 2)):
        biases[row : row + 1, :] = vector[source : source + 1, :chunk]
    ramp = vector[:, chunk : 2 * chunk]
    biases[6:7, :] = ramp[1:2, :]
    half = up_bias.shape[1] // 2
    for row in range(2):
        up_bias[:, row * half : (row + 1) * half] = vector[row : row + 1, 2 * chunk : 2 * chunk + half]
    classes[...] = ramp[2 : 2 + CLASSES, :]
    class_bias[...] = jnp.transpose(vector)[chunk : chunk + 1, 2 + CLASSES : 2 + 2 * CLASSES]


def finish(most, last, split, width, up_size, after):
    chunk = most.shape[0]
    sizes = [(chunk, 3 * width), (chunk, width), (chunk, width), (2, chunk), (7, chunk), (1, up_size), (CLASSES, chunk)]
    sizes.append((1, CLASSES))
    operands = (most, last.keep, *last.gots)
    return run(
        functools.partial(finish_kernel, split=split, gots=len(last.gots)),
        after,
        operands,
        [fixed(a.shape) for a in operands],
        16,
        loose=range(2, len(operands)),
        grid=(1,),
        out_specs=[fixed(size) for size in sizes],
        out_shape=[jax.ShapeDtypeStruct(size, f32) for size in sizes],
        cost_estimate=cost(0, 0),
        name="finish",
    )


def bits_of(size):
    return [1 << k for k in range(size.bit_length() - 1)]


def shards(
    hidden_in,
    lengths,
    labels,
    out_cotangent,
    qkv_weight,
    out_weight,
    up_weight,
    down_weight,
    pool_weight,
    class_weight,
    norm_gains,
    biases,
    up_bias,
    class_bias,
):
    positions, group, width = hidden_in.shape
    n_seq = lax.axis_size("seq")
    n_dp = lax.axis_size("dp")
    n_all = n_seq * n_dp
    seq_at = lax.axis_index("seq")
    me = lax.axis_index("dp") * n_seq + seq_at
    per = group // n_seq
    info = seq_at[None].astype(jnp.int32)
    me_info = me[None].astype(jnp.int32)
    classes = class_weight.shape[1]
    class_rows = jnp.zeros((128, width), bf16).at[:classes].set(class_weight.T)
    class_shift = jnp.full((1, 128), neg_big, f32).at[0, :classes].set(class_bias)

    seq_bits = [("seq", b) for b in bits_of(n_seq)]
    dp_bits = [("dp", b) for b in bits_of(n_dp)]
    chunk = width // n_all
    halved = chunk % 8 == 0

    x_send = split_rows(info, hidden_in.reshape(positions * group, width), positions, group, n_seq)
    x_parts = exchange(x_send)
    cot_send = split_rows(
        info, out_cotangent.reshape(positions * group, width), positions, group, n_seq, after=(x_send[0],)
    )
    cots = exchange(cot_send)
    x_rows, qkv, context, lse, n_one, q_one = attend(
        info, lengths, x_parts, qkv_weight, out_weight, biases, after=(cot_send[0],)
    )
    outs = feed(
        info, labels, cots, n_one, up_weight, up_bias[None, :], down_weight, norm_gains, biases, pool_weight,
        class_rows, class_shift,
    )
    middle_low, act, slope, grad_two, branch_grad, ramp_first, ramp_pre, ramp_out, sums_two, ramp_sums = outs[:10]
    final_parts = outs[10:]

    near = [seq_bits[:1], dp_bits[:1], seq_bits[1:]]
    one_way = [[entry] for entry in seq_bits[:1] + dp_bits[:1] + seq_bits[1:] + dp_bits[1:]]
    three_way = one_way[:3] + [dp_bits[1:]]
    two_way = near[:1] + [near[1] + near[2]] + [[entry] for entry in dp_bits[1:]]
    flat = [entry for stage in one_way for entry in stage]
    places = halving_order(flat, n_seq)
    bits = tuple(bit * (n_seq if axis == "dp" else 1) for axis, bit in flat)
    streams = {}
    done = (branch_grad,)

    def stage(*names, passed=(), hold=()):
        nonlocal done
        if halved:
            done, passed = advance(
                [streams[name] for name in names], passed, done, [streams[name] for name in hold]
            )
        return passed

    def start(name, halves, stages, fine=0):
        nonlocal done
        streams[name] = Halving(halves, stages, fine)
        done = (halves[0],)

    if halved:
        start("down", tall_grad(me_info, act, branch_grad, bits, after=done), two_way)
    stage("down")
    filled = ()
    sums_one, up_sums = [], []
    blocks = 2 * per
    for first, steps in ((0, 1), (1, blocks - 1)):
        filled = feed_back(
            first, steps, blocks, grad_two, branch_grad, slope, n_one, q_one, down_weight, up_weight, out_weight,
            norm_gains, filled, after=done,
        )
        sums_one.append(filled[4])
        up_sums.append(filled[5])
        filled = filled[:4]
        done = (sums_one[-1],)
        if first == 0:
            stage("down")
    pre_grad, grad_one, mix_grad, context_grad = filled
    if halved:
        start("up", wide_grad(me_info, middle_low, pre_grad, places, 1024, after=done), two_way)
    final_parts = exchange([final_parts[0], *stage("down", "up", passed=final_parts[1:])])

    count = width // PAIR // 3
    grads, qkv_sums = [], []
    for first, groups in ((0, 1), (count, 2)):
        grad, qkv_sum = attend_back(
            info, lengths, qkv, context_grad, context, lse, n_seq, first, count, groups, after=done
        )
        grads.append(grad)
        qkv_sums.append(qkv_sum)
        done = (qkv_sum,)
        if first == 0:
            if halved:
                pairs = [(x_rows, grad), (context, mix_grad), (ramp_first, ramp_pre)]
                start("most", group_grad(me_info, pairs, (), None, places, after=done), one_way)
            final_parts = [final_parts[0], *stage("down", "up", "most", passed=final_parts[1:])]
    back = input_grad(grads, qkv_weight, grad_one, per, n_seq, after=done)
    done = (back[0],)
    if halved:
        pairs = [(x_rows, grad) for grad in grads[1:]]
        vectors = (sums_two, ramp_sums, *sums_one, *up_sums, *qkv_sums)
        start("last", group_grad(me_info, pairs, vectors, (len(sums_one), len(qkv_sums)), places, after=done), three_way, fine=chunk)
    back_parts = exchange(
        [back[0], *stage("down", "up", "most", "last", passed=back[1:], hold=("up",))]
    )
    hidden_out = merge_rows(info, final_parts, bf16, after=done)
    done = (hidden_out,)
    back_parts = [back[0], *stage("up", "most", "last", passed=back_parts[1:])]
    grad_in = merge_rows(info, back_parts, f32, after=done)
    done = (grad_in,)
    stage("up", "most", "last")
    stage("up", "most", "last")
    stage("most")
    if halved:
        qkv_total, out_total, pool_total, gains_sum, biases_sum, up_bias_sum, class_sum, class_bias_sum = finish(
            streams["most"].total, streams["last"], count * PAIR, width, up_weight.shape[1] // n_all, done
        )
        up_bias_sum = up_bias_sum[0]
        class_sum = jnp.transpose(class_sum)
        class_bias_sum = class_bias_sum[0]
        up_total = streams["up"].total
        down_total = streams["down"].total
    else:

        def scatter(value):
            return lax.psum_scatter(value, ("dp", "seq"), scatter_dimension=0, tiled=True)

        wide = jnp.concatenate([grad[t] for t in range(3) for grad in grads], axis=1)
        qkv_total = scatter(tn(x_rows, wide))
        out_total = scatter(tn(context, mix_grad))
        up_total = scatter(tn(middle_low, pre_grad))
        down_total = scatter(tn(act, branch_grad))
        pool_total = scatter(
            lax.dot_general(ramp_first, ramp_pre, (((0,), (0,)), ((), ())), precision=highest)
        )
        table = jnp.concatenate(
            [sums_two[:3], sum(sums_one)[:3], jnp.concatenate(qkv_sums, axis=1)[:2], ramp_sums], axis=0
        )
        table = jnp.transpose(table.reshape(16, n_all, chunk), (1, 0, 2)).reshape(n_all, 16 * chunk)
        table = scatter(jnp.concatenate([table, sum(up_sums).reshape(n_all, -1)], axis=1))[0]
        vec = table[: 8 * chunk].reshape(8, chunk)
        ramp_vec = table[8 * chunk : 16 * chunk].reshape(8, chunk)
        up_bias_sum = table[16 * chunk :]
        gains_sum = jnp.stack([vec[3], vec[0]])
        biases_sum = jnp.stack([vec[6], vec[7], vec[4], vec[5], vec[1], vec[2], ramp_vec[1]])
        class_sum = jnp.transpose(ramp_vec[2 : 2 + classes])
        class_bias_sum = ramp_vec[2 + classes : 2 + 2 * classes, 0]
    ramp_logits = ramp_out.reshape(per, REC, -1)[:, 0, :classes]
    return (
        hidden_out.reshape(positions, group, width),
        ramp_logits,
        grad_in.reshape(positions, group, width),
        qkv_total,
        out_total,
        up_total,
        down_total,
        pool_total,
        class_sum,
        gains_sum,
        biases_sum,
        up_bias_sum,
        class_bias_sum,
    )


def solution(mesh):
    every = ("dp", "seq")
    rows = P("seq", "dp", None)
    return jax.shard_map(
        shards,
        mesh=mesh,
        in_specs=(rows, P("dp"), P(every), rows) + (P(),) * 10,
        out_specs=(
            rows,
            P(every, None),
            rows,
            P(every, None),
            P(every, None),
            P(every, None),
            P(every, None),
            P(every, None),
            P(every, None),
            P(None, every),
            P(None, every),
            P(every),
            P(),
        ),
        check_vma=False,
    )
```

```python
import functools

import jax
import jax.numpy as jnp
from jax import lax
from jax.experimental import pallas as pl
from jax.experimental.pallas import tpu as pltpu
from jax.sharding import PartitionSpec as P

HEAD_DIM = 64
PAIR = 2 * HEAD_DIM
REC = 8
CLASSES = 3
FEED_PARTS = 2

eps = 1e-12
neg_big = -1e30
highest = lax.Precision.HIGHEST
f32 = jnp.float32
bf16 = jnp.bfloat16
MIB = 1 << 20


def nn(left, right):
    return lax.dot_general(left, right, (((1,), (0,)), ((), ())), preferred_element_type=f32)


def nt(left, right):
    return lax.dot_general(left, right, (((1,), (1,)), ((), ())), preferred_element_type=f32)


def tn(left, right):
    return lax.dot_general(left, right, (((0,), (0,)), ((), ())), preferred_element_type=f32)


def cost(flops, nbytes, trans=0):
    return pl.CostEstimate(flops=1, bytes_accessed=1, transcendentals=0)


def smem():
    return pl.BlockSpec(memory_space=pltpu.SMEM)


def in_vmem():
    return pl.BlockSpec(memory_space=pltpu.VMEM)


def fixed(shape):
    return pl.BlockSpec(shape, lambda *_: (0,) * len(shape))


def once(shape):
    return pl.BlockSpec(shape, lambda *_: (0,) * len(shape), pipeline_mode=pl.Buffered(1))


def run(kernel, after, operands, in_specs, limit, out_shape, aliases=None, loose=(), **kwargs):
    skip = len(after)
    operands = [
        a
        if k in loose or spec.memory_space in (pltpu.VMEM, pltpu.SMEM)
        else pltpu.with_memory_space_constraint(a, pltpu.HBM)
        for k, (a, spec) in enumerate(zip(operands, in_specs, strict=True))
    ]
    after = [pltpu.with_memory_space_constraint(a, pltpu.HBM) for a in after]
    single = not isinstance(out_shape, list)
    shapes = [pltpu.HBM(a.shape, a.dtype) for a in ([out_shape] if single else out_shape)]

    def body(*refs):
        kernel(*refs[skip:])

    return pl.pallas_call(
        body,
        in_specs=[pl.BlockSpec(memory_space=pl.ANY)] * skip + list(in_specs),
        out_shape=shapes[0] if single else shapes,
        input_output_aliases={k + skip: v for k, v in (aliases or {}).items()},
        compiler_params=pltpu.CompilerParams(vmem_limit_bytes=limit * MIB),
        **kwargs,
    )(*after, *operands)


def three_parts(value):
    hi = value.astype(bf16)
    rest = value - hi.astype(f32)
    mid = rest.astype(bf16)
    low = (rest - mid.astype(f32)).astype(bf16)
    return jnp.concatenate([hi, mid, low], axis=0)


def fine_dot(dot, value, weight):
    rows = value.shape[0]
    parts = dot(jnp.concatenate([three_parts(value)], axis=0), weight)
    return parts[:rows] + parts[rows : 2 * rows] + parts[2 * rows :]


def split_kernel(info, rows, *outs):
    chunks = len(outs)
    per, span, _ = outs[0].shape
    group = chunks * per
    block = 16 * group
    own = info[0]
    dest = lax.broadcasted_iota(jnp.int32, (block, block), 0)
    source = lax.broadcasted_iota(jnp.int32, (block, block), 1)
    chunk = dest // (16 * per)
    wanted = (dest % 16) * group + per * (chunk ^ own) + (dest // 16) % per
    perm = jnp.where(source == wanted, 1.0, 0.0).astype(bf16)
    for b in range(span // 16):
        moved = nn(perm, rows[b * block : (b + 1) * block, :]).astype(bf16)
        for c in range(chunks):
            for q in range(per):
                at = (c * per + q) * 16
                outs[c][q, b * 16 : (b + 1) * 16, :] = moved[at : at + 16]


def split_rows(info, rows, positions, group, chunks, after=()):
    width = rows.shape[1]
    per = group // chunks
    steps = 2
    span = positions // steps
    return run(
        split_kernel,
        after,
        (info, rows),
        [smem(), pl.BlockSpec((span * group, width), lambda i: (i, 0))],
        16,
        grid=(steps,),
        out_specs=[pl.BlockSpec((per, span, width), lambda i: (0, i, 0))] * chunks,
        out_shape=[jax.ShapeDtypeStruct((per, positions, width), bf16)] * chunks,
        cost_estimate=cost(2 * rows.size * 16 * group, 4 * rows.size),
        name="split_rows",
    )


def merge_kernel(info, *refs):
    ins, out = refs[:-1], refs[-1]
    chunks = len(ins)
    per, span, _ = ins[0].shape
    group = chunks * per
    block = 16 * group
    own = info[0]
    dest = lax.broadcasted_iota(jnp.int32, (block, block), 0)
    source = lax.broadcasted_iota(jnp.int32, (block, block), 1)
    seq = dest % group
    wanted = (((seq // per) ^ own) * per + seq % per) * 16 + dest // group
    perm = jnp.where(source == wanted, 1.0, 0.0).astype(bf16)
    for b in range(span // 16):
        rows = jnp.concatenate(
            [ins[c][q, b * 16 : (b + 1) * 16, :] for c in range(chunks) for q in range(per)], axis=0
        )
        out[b * block : (b + 1) * block, :] = nn(perm, rows).astype(out.dtype)


def merge_rows(info, parts, dtype, after=()):
    chunks = len(parts)
    per, positions, width = parts[0].shape
    group = per * chunks
    steps = 2
    span = positions // steps
    return run(
        merge_kernel,
        after,
        (info, *parts),
        [smem()] + [pl.BlockSpec((per, span, width), lambda i: (0, i, 0))] * chunks,
        16,
        grid=(steps,),
        out_specs=pl.BlockSpec((span * group, width), lambda i: (i, 0)),
        out_shape=jax.ShapeDtypeStruct((positions * group, width), dtype),
        cost_estimate=cost(2 * positions * group * width * 16 * group, 6 * positions * group * width),
        name="merge_rows",
    )


def exchange(parts):
    size = lax.axis_size("seq")
    return [parts[0]] + [
        lax.ppermute(parts[c], "seq", [(i, i ^ c) for i in range(size)]) for c in range(1, size)
    ]


def row_stats(resid):
    mean = jnp.mean(resid, axis=-1, keepdims=True)
    centred = resid - mean
    scale = lax.rsqrt(jnp.mean(centred * centred, axis=-1, keepdims=True) + eps)
    return centred * scale, scale


def attend_kernel(info, lengths, *refs):
    chunks = len(refs) - 10
    parts = refs[:chunks]
    qkv_w, out_w, biases, x_out, qkv, context, lse, normed, scale, stats = refs[chunks:]
    width = out_w.shape[0]
    span = parts[0].shape[1]
    length = chunks * span
    pairs = width // PAIR
    own = info[0]
    live_len = lengths[own * pl.num_programs(0) + pl.program_id(0)]
    x_out[...] = jnp.concatenate([part[0] for part in parts], axis=0)
    for third in range(3):
        cols = slice(third * width, (third + 1) * width)
        block = nn(x_out[...], qkv_w[:, cols])
        if third == 0:
            block = block + biases[0:1, :]
        elif third == 2:
            block = block + biases[1:2, :]
        qkv[:, cols] = block.astype(bf16)
    lane = lax.broadcasted_iota(jnp.int32, (length, PAIR), 1)
    row = lax.broadcasted_iota(jnp.int32, (length, PAIR), 0)
    pos = ((row // span) ^ own) * span + row % span
    key_ext = jnp.where((lane == 0) & (pos >= live_len), neg_big, 0.0).astype(bf16)
    query_ext = jnp.where(lane == 0, 1.0, 0.0).astype(bf16)
    low_half = lane < HEAD_DIM
    masks = [jnp.where(low_half, 1.0, 0.0).astype(bf16), jnp.where(low_half, 0.0, 1.0).astype(bf16)]
    stats[...] = jnp.zeros_like(stats)

    def one_pair(i, carry):
        start = pl.multiple_of(i * PAIR, PAIR)
        queries = qkv[:, pl.ds(start, PAIR)] * bf16(HEAD_DIM**-0.5)
        keys = jnp.concatenate([qkv[:, pl.ds(start + width, PAIR)], key_ext], axis=1)
        values = qkv[:, pl.ds(start + 2 * width, PAIR)]
        total = None
        tops = []
        for head in range(2):
            scores = nt(jnp.concatenate([queries * masks[head], query_ext], axis=1), keys)
            top = jnp.max(scores, axis=1, keepdims=True)
            weights = jnp.exp(scores - top).astype(bf16)
            part = nn(weights, jnp.concatenate([values * masks[head], masks[head]], axis=1))
            total = part if total is None else total + part
            tops.append(top)
        row_total = total[:, PAIR:]
        context[:, pl.ds(start, PAIR)] = (total[:, :PAIR] / row_total).astype(bf16)
        log_total = jnp.where(low_half, tops[0], tops[1]) + jnp.log(row_total)
        swapped = pltpu.roll(log_total, HEAD_DIM, 1)
        stats[...] = jnp.where(
            lane == 2 * i, log_total, jnp.where(lane == 2 * i + 1, swapped, stats[...])
        )
        return carry

    lax.fori_loop(0, pairs, one_pair, 0, unroll=pairs)
    lse[0] = jnp.transpose(stats[...])[: lse.shape[1], :]
    resid = x_out[...].astype(f32) + (nn(context[...], out_w[...]) + biases[2:3, :])
    n_one, q_one = row_stats(resid)
    normed[...] = n_one
    scale[...] = q_one


def attend(info, lengths, parts, qkv_w, out_w, biases, after=()):
    chunks = len(parts)
    per, span, width = parts[0].shape
    length = chunks * span
    rows = per * length
    heads = width // HEAD_DIM
    head_rows = -(-heads // 8) * 8
    by_seq = lambda i: (i, 0)
    return run(
        attend_kernel,
        after,
        (info, lengths, *parts, qkv_w, out_w, biases),
        [smem()] * 2
        + [pl.BlockSpec((1, span, width), lambda i: (i, 0, 0))] * chunks
        + [in_vmem(), once(out_w.shape), once(biases.shape)],
        30,
        grid=(per,),
        out_specs=[
            pl.BlockSpec((length, width), by_seq),
            pl.BlockSpec((length, 3 * width), by_seq),
            pl.BlockSpec((length, width), by_seq),
            pl.BlockSpec((1, head_rows, length), lambda i: (i, 0, 0)),
            pl.BlockSpec((length, width), by_seq),
            pl.BlockSpec((length, 1), by_seq),
        ],
        out_shape=[
            jax.ShapeDtypeStruct((rows, width), bf16),
            jax.ShapeDtypeStruct((rows, 3 * width), bf16),
            jax.ShapeDtypeStruct((rows, width), bf16),
            jax.ShapeDtypeStruct((per, head_rows, length), f32),
            jax.ShapeDtypeStruct((rows, width), f32),
            jax.ShapeDtypeStruct((rows, 1), f32),
        ],
        scratch_shapes=[pltpu.VMEM((length, PAIR), f32)],
        cost_estimate=cost(
            8 * rows * width * width + 8 * rows * length * width, 20 * rows * width + 8 * width * width,
            rows * length * heads,
        ),
        name="attend",
    )


def gelu_pair(x):
    cdf = 0.5 + 0.5 * lax.erf(x * 0.5**0.5)
    bell = jnp.exp(-0.5 * (x * x))
    return x * cdf, cdf + x * bell * (0.5 / jnp.pi) ** 0.5


def norm_back(upper, normed, scale, gain):
    scaled = upper * gain
    mean_part = jnp.mean(scaled, axis=-1, keepdims=True)
    proj_part = jnp.mean(scaled * normed, axis=-1, keepdims=True)
    return scale * (scaled - mean_part - normed * proj_part)


def col_sum(values):
    return jnp.sum(values, axis=0, keepdims=True)


def feed_kernel(info, labels, *refs):
    chunks = (len(refs) - 20) // 2
    cots = refs[:chunks]
    normed, up_w, up_b, down_w, gains, biases, pool_w, class_w, class_b = refs[chunks : chunks + 9]
    middle_out, act, slope, grad_two, branch_grad = refs[chunks + 9 : chunks + 14]
    ramp_first, ramp_pre, ramp_out, sums, ramp_sums = refs[chunks + 14 : chunks + 19]
    finals = refs[chunks + 19 : -1]
    n_two = refs[-1]
    span = finals[0].shape[1]
    own = info[0]

    @pl.when(pl.program_id(0) == 0)
    def _():
        sums[...] = jnp.zeros_like(sums)
        ramp_sums[...] = jnp.zeros_like(ramp_sums)

    hidden = up_w.shape[1]
    tile = 256
    length = chunks * span
    block = length // FEED_PARTS
    scales = []
    for part in range(FEED_PARTS):
        rows = slice(part * block, (part + 1) * block)
        middle = normed[rows, :] * gains[0:1, :] + biases[3:4, :]
        middle_out[rows, :] = middle.astype(bf16)
        for j in range(hidden // tile):
            cols = slice(j * tile, (j + 1) * tile)
            pre = nn(middle_out[rows, :], up_w[:, cols]) + up_b[:, cols]
            value, grad = gelu_pair(pre)
            act[rows, cols] = value.astype(bf16)
            slope[rows, cols] = grad.astype(bf16)
        branch = nn(act[rows, :], down_w[...]) + biases[4:5, :]
        middle = normed[rows, :] * gains[0:1, :] + biases[3:4, :]
        normed_two, q_two = row_stats(middle + branch)
        n_two[rows, :] = normed_two
        scales.append(q_two)
    for c in range(chunks):
        rows = slice(c * span, (c + 1) * span)
        finals[c][0] = (n_two[rows, :] * gains[1:2, :] + biases[5:6, :]).astype(bf16)
    label = labels[pl.program_id(0)]
    start = pl.multiple_of(own * span, 8)
    first = (n_two[pl.ds(start, REC), :] * gains[1:2, :] + biases[5:6, :]).astype(bf16)
    pooled = jnp.tanh(nn(first, pool_w[...]) + biases[6:7, :])
    logits = fine_dot(nt, pooled, class_w[...]) + class_b[...]
    expo = jnp.exp(logits - jnp.max(logits, axis=1, keepdims=True))
    lane = lax.broadcasted_iota(jnp.int32, logits.shape, 1)
    g_logits = expo / jnp.sum(expo, axis=1, keepdims=True) - jnp.where(lane == label, 1.0, 0.0)
    g_pre = fine_dot(nn, g_logits, class_w[...]) * (1.0 - pooled * pooled)
    g_first = fine_dot(nt, g_pre, pool_w[...])
    first_row = lax.broadcasted_iota(jnp.int32, (REC, 1), 0) == 0
    ramp_first[...] = jnp.where(first_row, first.astype(f32), 0.0)
    ramp_pre[...] = jnp.where(first_row, g_pre, 0.0)
    ramp_out[...] = logits
    ramp_sums[1:2, :] += g_pre[0:1, :]
    for c in range(CLASSES):
        at_class = jnp.sum(jnp.where(lane == c, g_logits, 0.0), axis=1, keepdims=True)[0:1, :]
        ramp_sums[2 + c : 3 + c, :] += at_class * pooled[0:1, :]
        ramp_sums[2 + CLASSES + c : 3 + CLASSES + c, :] += at_class + jnp.zeros_like(pooled[0:1, :])
    sum_rows = [0.0, 0.0, 0.0]
    for part in range(FEED_PARTS):
        rows = slice(part * block, (part + 1) * block)
        here = cots[part * chunks // FEED_PARTS : (part + 1) * chunks // FEED_PARTS]
        cot = jnp.concatenate([chunk[0] for chunk in here], axis=0).astype(f32)
        row = part * block + lax.broadcasted_iota(jnp.int32, (block, 1), 0)
        g_final = cot + jnp.where(row == own * span, g_first[0:1, :], 0.0)
        normed_two = n_two[rows, :]
        g_two = norm_back(g_final, normed_two, scales[part], gains[1:2, :])
        grad_two[rows, :] = g_two
        low = g_two.astype(bf16)
        branch_grad[rows, :] = low
        for k, values in enumerate((g_final * normed_two, low.astype(f32), g_final)):
            sum_rows[k] = sum_rows[k] + col_sum(values)
    for k in range(3):
        sums[k : k + 1, :] += sum_rows[k]


def feed(info, labels, cots, normed, up_w, up_b, down_w, gains, biases, pool_w, class_w, class_b, after=()):
    chunks = len(cots)
    per, span, _ = cots[0].shape
    rows, width = normed.shape
    length = rows // per
    hidden = up_w.shape[1]
    by_seq = lambda i: (i, 0)
    row_block = pl.BlockSpec((length, width), by_seq)
    wide_block = pl.BlockSpec((length, hidden), by_seq)
    part = pl.BlockSpec((1, span, width), lambda i: (i, 0, 0))
    consts = (up_w, up_b, down_w, gains, biases, pool_w, class_w, class_b)
    return run(
        feed_kernel,
        after,
        (info, labels, *cots, normed, *consts),
        [smem()] * 2 + [part] * chunks + [row_block, in_vmem()] + [once(a.shape) for a in consts[1:]],
        44,
        grid=(per,),
        out_specs=[
            row_block, wide_block, wide_block, row_block, row_block,
            pl.BlockSpec((REC, width), by_seq), pl.BlockSpec((REC, width), by_seq),
            pl.BlockSpec((REC, class_b.shape[1]), by_seq), fixed((8, width)), fixed((8, width)),
        ]
        + [part] * chunks,
        out_shape=[
            jax.ShapeDtypeStruct((rows, width), bf16),
            jax.ShapeDtypeStruct((rows, hidden), bf16),
            jax.ShapeDtypeStruct((rows, hidden), bf16),
            jax.ShapeDtypeStruct((rows, width), f32),
            jax.ShapeDtypeStruct((rows, width), bf16),
            jax.ShapeDtypeStruct((per * REC, width), f32),
            jax.ShapeDtypeStruct((per * REC, width), f32),
            jax.ShapeDtypeStruct((per * REC, class_b.shape[1]), f32),
            jax.ShapeDtypeStruct((8, width), f32),
            jax.ShapeDtypeStruct((8, width), f32),
        ]
        + [jax.ShapeDtypeStruct((per, span, width), bf16)] * chunks,
        scratch_shapes=[pltpu.VMEM((length, width), f32)],
        cost_estimate=cost(4 * rows * width * hidden, 4 * rows * hidden + 4 * width * hidden + 12 * rows * width),
        name="feed",
    )


def feed_back_kernel(*refs, carried):
    grad_two, branch_grad, slope, n_one, q_one, down_w, up_w, out_w, gains = refs[:9]
    pre_grad, grad_one, mix_grad, context_grad, sums, up_sums = refs[9 + carried :]

    @pl.when(pl.program_id(0) == 0)
    def _():
        sums[...] = jnp.zeros_like(sums)
        up_sums[...] = jnp.zeros_like(up_sums)

    hidden = up_w.shape[1]
    tile = 256
    for j in range(hidden // tile):
        cols = slice(j * tile, (j + 1) * tile)
        pre = nt(branch_grad[...], down_w[cols, :]) * slope[:, cols].astype(f32)
        low = pre.astype(bf16)
        pre_grad[:, cols] = low
        up_sums[:, cols] += col_sum(low.astype(f32))
    g_middle = grad_two[...] + nt(pre_grad[...], up_w[...])
    normed = n_one[...]
    sums[0:1, :] += col_sum(g_middle * normed)
    sums[2:3, :] += col_sum(g_middle)
    g_one = norm_back(g_middle, normed, q_one[...], gains[0:1, :])
    grad_one[...] = g_one
    mix_grad[...] = g_one.astype(bf16)
    sums[1:2, :] += col_sum(mix_grad[...].astype(f32))
    context_grad[...] = nt(mix_grad[...], out_w[...]).astype(bf16)


def feed_back(first, steps, blocks, grad_two, branch_grad, slope, n_one, q_one, down_w, up_w, out_w, gains, before, after=()):
    rows, width = grad_two.shape
    hidden = slope.shape[1]
    block = rows // blocks
    by_row = lambda i: (first + i, 0)
    row_block = pl.BlockSpec((block, width), by_row)
    wide_block = pl.BlockSpec((block, hidden), by_row)
    thin_block = pl.BlockSpec((block, 1), by_row)
    return run(
        functools.partial(feed_back_kernel, carried=len(before)),
        after,
        (grad_two, branch_grad, slope, n_one, q_one, down_w, up_w, out_w, gains, *before),
        [row_block, row_block, wide_block, row_block, thin_block]
        + [in_vmem()] * 2
        + [once(out_w.shape), once(gains.shape)]
        + [pl.BlockSpec(memory_space=pl.ANY)] * len(before),
        32,
        aliases={9 + k: k for k in range(len(before))},
        grid=(steps,),
        out_specs=[wide_block, row_block, row_block, row_block, fixed((8, width)), fixed((1, hidden))],
        out_shape=[
            jax.ShapeDtypeStruct((rows, hidden), bf16),
            jax.ShapeDtypeStruct((rows, width), f32),
            jax.ShapeDtypeStruct((rows, width), bf16),
            jax.ShapeDtypeStruct((rows, width), bf16),
            jax.ShapeDtypeStruct((8, width), f32),
            jax.ShapeDtypeStruct((1, hidden), f32),
        ],
        cost_estimate=cost(0, 0),
        name="feed_back",
    )


def attend_back_kernel(info, lengths, queries_in, keys_in, values_in, context_grad, context, lse, grads, sums, *, chunks, first):
    length, cols = queries_in.shape
    first = first + pl.program_id(0) * (cols // PAIR)
    at_seq = pl.program_id(1)
    span = length // chunks
    own = info[0]
    live_len = lengths[own * pl.num_programs(1) + at_seq]
    factor = HEAD_DIM**-0.5
    lane = lax.broadcasted_iota(jnp.int32, (length, PAIR), 1)
    row = lax.broadcasted_iota(jnp.int32, (length, PAIR), 0)
    pos = ((row // span) ^ own) * span + row % span
    key_ext = jnp.where((lane == 0) & (pos >= live_len), neg_big, 0.0).astype(bf16)
    query_ext = jnp.where(lane == 0, 1.0, 0.0).astype(bf16)
    low_half = lane < HEAD_DIM
    masks = [jnp.where(low_half, 1.0, 0.0).astype(bf16), jnp.where(low_half, 0.0, 1.0).astype(bf16)]
    picks = jnp.where(
        lax.broadcasted_iota(jnp.int32, (8, PAIR), 1) // HEAD_DIM
        == lax.broadcasted_iota(jnp.int32, (8, PAIR), 0),
        1.0,
        0.0,
    ).astype(bf16)
    parts = 1
    block = length // parts

    @pl.when(at_seq == 0)
    def _():
        sums[...] = jnp.zeros_like(sums)

    for pair in range(cols // PAIR):
        at = slice(pair * PAIR, (pair + 1) * PAIR)
        queries = queries_in[:, at] * bf16(factor)
        keys = jnp.concatenate([keys_in[:, at], key_ext], axis=1)
        values = values_in[:, at]
        ctx_grad = context_grad[:, at]
        product = ctx_grad.astype(f32) * context[:, at].astype(f32)
        high = product.astype(bf16)
        low = (product - high.astype(f32)).astype(bf16)
        row_dots = nt(picks, high) + nt(picks, low)
        g_queries = None
        g_keys = [None] * parts
        g_values = [None] * parts
        for head in range(2):
            masked_q = queries * masks[head]
            long_q = jnp.concatenate([masked_q, query_ext], axis=1)
            masked_g = ctx_grad * masks[head]
            masked_k = keys_in[:, at] * masks[head]
            log_total = lse[0, pl.ds(2 * (first + pair) + head, 1), :]
            row_dot = row_dots[head : head + 1, :]
            for c in range(parts):
                rows = slice(c * block, (c + 1) * block)
                weights = jnp.exp(nt(keys[rows], long_q) - log_total)
                part = nn(weights.astype(bf16), masked_g)
                g_values[c] = part if g_values[c] is None else g_values[c] + part
                g_scores = (weights * (nt(values[rows], masked_g) - row_dot)).astype(bf16)
                part = nn(g_scores, masked_q)
                g_keys[c] = part if g_keys[c] is None else g_keys[c] + part
                part = tn(g_scores, masked_k[rows])
                g_queries = part if g_queries is None else g_queries + part
        grads[0, :, at] = (g_queries * factor).astype(bf16)
        for c in range(parts):
            rows = slice(c * block, (c + 1) * block)
            grads[1, rows, at] = g_keys[c].astype(bf16)
            grads[2, rows, at] = g_values[c].astype(bf16)
        sums[0:1, at] += col_sum(grads[0, :, at].astype(f32))
        sums[1:2, at] += col_sum(grads[2, :, at].astype(f32))


def attend_back(info, lengths, qkv, context_grad, context, lse, chunks, first, count, groups, after=()):
    rows, width = context.shape
    per, head_rows, length = lse.shape
    cols = count * PAIR
    blocks = width // cols
    spec = lambda third: pl.BlockSpec((length, cols), lambda g, q: (q, third * blocks + first // count + g))
    return run(
        functools.partial(attend_back_kernel, chunks=chunks, first=first),
        after,
        (info, lengths, qkv, qkv, qkv, context_grad, context, lse),
        [
            smem(),
            smem(),
            spec(0),
            spec(1),
            spec(2),
            spec(0),
            spec(0),
            pl.BlockSpec((1, head_rows, length), lambda g, q: (q, 0, 0)),
        ],
        40,
        grid=(groups, per),
        out_specs=[
            pl.BlockSpec((3, length, cols), lambda g, q: (0, q, g)),
            pl.BlockSpec((8, cols), lambda g, q: (0, g)),
        ],
        out_shape=[
            jax.ShapeDtypeStruct((3, rows, groups * cols), bf16),
            jax.ShapeDtypeStruct((8, groups * cols), f32),
        ],
        cost_estimate=cost(0, 0),
        name="attend_back",
    )


def input_grad_kernel(*refs, groups):
    grads = refs[:groups]
    qkv_w, grad_one = refs[groups : groups + 2]
    outs = refs[groups + 2 :]
    width = grad_one.shape[1]
    total = grad_one[...]
    offset = 0
    for grad in grads:
        each = grad.shape[2]
        for third in range(3):
            start = third * width + offset
            total = total + nt(grad[third], qkv_w[:, start : start + each])
        offset += each
    span = outs[0].shape[1]
    for c, out in enumerate(outs):
        out[0] = total[c * span : (c + 1) * span].astype(bf16)


def input_grad(grads, qkv_w, grad_one, per, chunks, after=()):
    groups = len(grads)
    rows, width = grad_one.shape
    length = rows // per
    span = length // chunks
    return run(
        functools.partial(input_grad_kernel, groups=groups),
        after,
        (*grads, qkv_w, grad_one),
        [pl.BlockSpec((3, length, grad.shape[2]), lambda i: (0, i, 0)) for grad in grads]
        + [in_vmem(), pl.BlockSpec((length, width), lambda i: (i, 0))],
        32,
        grid=(per,),
        out_specs=[pl.BlockSpec((1, span, width), lambda i: (i, 0, 0))] * chunks,
        out_shape=[jax.ShapeDtypeStruct((per, span, width), bf16)] * chunks,
        cost_estimate=cost(6 * rows * width * width, 12 * rows * width + 6 * width * width),
        name="input_grad",
    )


def chunk_at(me, relative, chunk):
    return pl.ds(pl.multiple_of((me ^ relative) * chunk, 8), chunk)


def tall_grad_kernel(info, left, right, keep, send, total, keep_near, send_near, sems, *, bits, chunk):
    total[...] = tn(left[...], right[...])
    here = left.shape[1] // chunk
    me = info[0]

    def copy(other, place, number):
        near, far = ((keep_near, keep), (send_near, send))[other]
        rows = pl.ds(place, chunk)
        return pltpu.make_async_copy(near.at[rows, :], far.at[rows, :], sems.at[other, number])

    for other, near in enumerate((keep_near, send_near)):
        for k in range(0, here, 2):
            source = k + ((me % 2) ^ other)
            relative = (pl.program_id(0) * here + source) ^ me
            place = 0
            for at, bit in enumerate(bits[1:]):
                place = place + ((relative // bit) % 2) * (1 << (len(bits) - 2 - at))
            rows = total[pl.ds(pl.multiple_of(source * chunk, 8), chunk), :]
            start = pl.multiple_of(place * chunk, 16)
            near[pl.ds(start, chunk), :] = rows.astype(bf16)
            copy(other, start, (pl.program_id(0) * here + k) // 2).start()

    @pl.when(pl.program_id(0) == pl.num_programs(0) - 1)
    def _():
        for other in range(2):
            for number in range(1 << (len(bits) - 1)):
                copy(other, 0, number).wait()


def tall_grad(me, left, right, bits, after=()):
    rows, depth = left.shape
    width = right.shape[1]
    chunk = depth >> len(bits)
    block = 8 * chunk
    half = pltpu.VMEM((depth // 2, width), bf16)
    return run(
        functools.partial(tall_grad_kernel, bits=bits, chunk=chunk),
        after,
        (me, left, right),
        [smem(), pl.BlockSpec((rows, block), lambda j: (0, j)), once((rows, width))],
        40,
        grid=(depth // block,),
        out_specs=[pl.BlockSpec(memory_space=pl.ANY)] * 2,
        out_shape=[jax.ShapeDtypeStruct((depth // 2, width), bf16)] * 2,
        scratch_shapes=[
            pltpu.VMEM((block, width), f32), half, half, pltpu.SemaphoreType.DMA((2, 1 << (len(bits) - 1)))
        ],
        cost_estimate=cost(0, 0),
        name="tall_grad",
    )


def wide_grad_kernel(info, left, right, keep, send, left_t, total, *, order, chunk):
    @pl.when(pl.program_id(0) == 0)
    def _():
        left_t[...] = jnp.transpose(left[...])

    me = info[0]
    half = len(order) // 2
    parts, _, tile = total.shape
    for part in range(parts):
        cols = slice(part * tile, (part + 1) * tile)
        total[part] = nn(left_t[...], right[:, cols])
        for at in range(0, len(order), 2):
            rows = jnp.concatenate([total[part, chunk_at(me, order[at + k], chunk), :] for k in range(2)], axis=0)
            target = keep if at < half else send
            row = (at % half) * chunk
            target[row : row + 2 * chunk, cols] = rows.astype(bf16)


def wide_grad(me, left, right, order, tile, after=()):
    rows, depth = left.shape
    width = right.shape[1]
    return run(
        functools.partial(wide_grad_kernel, order=order, chunk=depth // len(order)),
        after,
        (me, left, right),
        [smem(), fixed((rows, depth)), pl.BlockSpec((rows, tile), lambda j: (0, j))],
        32,
        grid=(width // tile,),
        out_specs=[pl.BlockSpec((depth // 2, tile), lambda j: (0, j))] * 2,
        out_shape=[jax.ShapeDtypeStruct((depth // 2, width), bf16)] * 2,
        scratch_shapes=[pltpu.VMEM((depth, rows), bf16), pltpu.VMEM((tile // 256, depth, 256), f32)],
        cost_estimate=cost(2 * rows * depth * width, 2 * rows * (depth + width) + 2 * depth * width),
        name="wide_grad",
    )


def fill_table(table, near, vectors, counts, chunk):
    per, groups = counts
    sums_two, ramp_sums = vectors[:2]
    sums_one = vectors[2 : 2 + per]
    up_sums = vectors[2 + per : 2 + 2 * per]
    qkv_sums = vectors[2 + 2 * per :]
    near[0:3, :] = sums_two[0:3, :]
    near[3:6, :] = sum(ref[0:3, :] for ref in sums_one)
    offset = 0
    for ref in qkv_sums:
        near[6:8, offset : offset + ref.shape[1]] = ref[0:2, :]
        offset += ref.shape[1]
    ups = sum(ref[...] for ref in up_sums)
    owners = table.shape[0]
    wide = ups.shape[1] // owners // 2
    table[...] = jnp.zeros_like(table)
    for k in range(owners):
        cols = slice(k * chunk, (k + 1) * chunk)
        table[k, :, 0:chunk] = near[:, cols]
        table[k, :, chunk : 2 * chunk] = ramp_sums[:, cols]
        for row in range(2):
            start = (2 * k + row) * wide
            table[k, row : row + 1, 2 * chunk : 2 * chunk + wide] = ups[:, start : start + wide]


def group_grad_kernel(info, *refs, order, chunk, jobs, counts):
    extra = counts is not None
    scratch = 3 if extra else 1
    keep, send = refs[-2 - scratch : -scratch]
    total = refs[-scratch]
    at_ref = 0
    column = 0
    for thirds in jobs:
        left, right = refs[at_ref : at_ref + 2]
        at_ref += 2
        if left.shape[0] < 128:
            high = right[...].astype(bf16)
            low = (right[...] - high.astype(f32)).astype(bf16)
            lefts = left[...].astype(bf16)
            product = tn(jnp.concatenate([lefts, lefts], axis=0), jnp.concatenate([high, low], axis=0))
            total[:, column : column + high.shape[1]] = product
            column += high.shape[1]
            continue
        left_t = jnp.transpose(left[...])
        for third in range(thirds or 1):
            block = right[third] if thirds else right[...]
            total[:, column : column + block.shape[1]] = nn(left_t, block)
            column += block.shape[1]
    me = info[0]
    half = len(order) // 2
    if extra:
        table, near = refs[-2:]
        fill_table(table, near, refs[at_ref : at_ref + 2 + 2 * counts[0] + counts[1]], counts, chunk)
        for k in range(len(order)):
            high = table[k].astype(bf16).astype(f32)
            total[k * chunk : k * chunk + 8, column:] = high
            total[k * chunk + 8 : k * chunk + 16, column:] = table[k] - high
            total[k * chunk + 16 : (k + 1) * chunk, column:] = jnp.zeros((chunk - 16, high.shape[1]), f32)
    for at in range(0, len(order), 2):
        rows = jnp.concatenate([total[chunk_at(me, order[at + k], chunk), :] for k in range(2)], axis=0)
        target = keep if at < half else send
        row = (at % half) * chunk
        target[row : row + 2 * chunk, :] = rows.astype(bf16)


def group_grad(me, pairs, vectors, counts, order, after=()):
    rows, depth = pairs[0][0].shape
    jobs = tuple(right.shape[0] if right.ndim == 3 else 0 for _, right in pairs)
    width = sum((right.shape[0] if right.ndim == 3 else 1) * right.shape[-1] for _, right in pairs)
    chunk = depth // len(order)
    extra = counts is not None
    width += 128 if extra else 0
    tall = depth // 2
    operands = [a for pair in pairs for a in pair] + list(vectors)
    scratch = [pltpu.VMEM((depth, width), f32)]
    if extra:
        scratch += [pltpu.VMEM((len(order), 8, 128), f32), pltpu.VMEM((8, depth), f32)]
    return run(
        functools.partial(group_grad_kernel, order=order, chunk=chunk, jobs=jobs, counts=counts),
        after,
        (me, *operands),
        [smem()] + [fixed(a.shape) for a in operands],
        48,
        grid=(1,),
        out_specs=[fixed((tall, width))] * 2,
        out_shape=[jax.ShapeDtypeStruct((tall, width), bf16)] * 2,
        scratch_shapes=scratch,
        cost_estimate=cost(0, 0),
        name="group_grad",
    )


def halving_order(stages, n_seq):
    bits = [bit * (n_seq if axis == "dp" else 1) for axis, bit in stages]
    count = len(bits)
    return [
        sum(bit for at, bit in enumerate(bits) if (place >> (count - 1 - at)) & 1) for place in range(1 << count)
    ]


def renew(values, chunk):
    groups = values.reshape(-1, chunk // 8, 8, values.shape[1])
    vector = groups[:, 0] + groups[:, 1]
    high = vector.astype(bf16).astype(f32)
    rest = [groups[:, k] for k in range(2, chunk // 8)]
    return jnp.stack([high, vector - high, *rest], axis=1).reshape(values.shape)


def add_kernel(*refs, plans):
    count = sum(1 + gots for gots, _, _ in plans)
    ins, outs = list(refs[:count]), list(refs[count:])
    for gots, parts, chunk in plans:
        terms = [ins.pop(0) for _ in range(1 + gots)]
        part_rows = terms[0].shape[0] // parts
        whole_rows = part_rows % 16 == 0
        if not whole_rows:
            total = sum(term[...].astype(f32) for term in terms[1:]) + terms[0][...].astype(f32)
        for part in range(parts):
            out = outs.pop(0)
            rows = slice(part * part_rows, (part + 1) * part_rows)
            if whole_rows:
                values = sum(term[rows, :].astype(f32) for term in terms[1:]) + terms[0][rows, :].astype(f32)
            else:
                values = total[rows]
            if chunk:
                out[:, :-128] = values[:, :-128].astype(out.dtype)
                out[:, -128:] = renew(values[:, -128:], chunk).astype(out.dtype)
            else:
                out[...] = values.astype(out.dtype)


class Halving:
    def __init__(self, halves, stages, fine=0):
        self.keep, *self.sends = halves
        self.stages = stages
        self.fine = fine
        self.gots = None

    def post(self):
        stage = self.stages[0]
        self.stages = self.stages[1:]
        self.gots = []
        for part, send in enumerate(self.sends, 1):
            masks = {}
            for at, (axis, bit) in enumerate(stage):
                if (part >> (len(stage) - 1 - at)) & 1:
                    masks[axis] = masks.get(axis, 0) ^ bit
            axes = tuple(masks)
            if len(axes) == 1:
                size, mask, name = lax.axis_size(axes[0]), masks[axes[0]], axes[0]
            else:
                n_seq = lax.axis_size("seq")
                size = lax.axis_size("dp") * n_seq
                mask, name = masks["dp"] * n_seq + masks["seq"], ("dp", "seq")
            self.gots.append(lax.ppermute(send, name, [(i, i ^ mask) for i in range(size)]))


def advance(streams, passed, after, hold=()):
    adding = [stream for stream in streams if stream.gots is not None]
    fresh = [stream for stream in streams if stream.gots is None]
    passed = list(passed) + [send for stream in fresh for send in stream.sends]
    steps = 2 if sum(stream.keep.size for stream in adding) > 3 << 18 and not any(s.fine for s in adding) else 1
    operands, in_specs, out_specs, shapes, plans, loose = [], [], [], [], [], []
    for stream in adding:
        rows, width = stream.keep.shape
        tile = width // steps
        loose += [len(operands) + 1 + k for k in range(len(stream.gots))]
        operands += [stream.keep, *stream.gots]
        in_specs += [pl.BlockSpec((rows, tile), lambda j: (0, j))] * (1 + len(stream.gots))
        parts = 1 << len(stream.stages[0]) if stream.stages else 1
        plans.append((len(stream.gots), parts, stream.fine))
        new = [jax.ShapeDtypeStruct((rows // parts, width), bf16 if stream.stages else f32)] * parts
        shapes += new
        out_specs += [pl.BlockSpec((rows // parts, tile), lambda j: (0, j))] * parts
    first_in, first_out = len(operands), len(shapes)

    def body(*refs):
        add_kernel(*refs[:first_in], *refs[first_in + len(passed) :][:first_out], plans=plans)

    outs = run(
        body,
        after,
        operands + passed,
        in_specs + [pl.BlockSpec(memory_space=pl.ANY)] * len(passed),
        40,
        aliases={first_in + k: first_out + k for k in range(len(passed))},
        loose=loose,
        grid=(steps,),
        out_specs=out_specs + [pl.BlockSpec(memory_space=pl.ANY)] * len(passed),
        out_shape=shapes + [jax.ShapeDtypeStruct(a.shape, a.dtype) for a in passed],
        cost_estimate=cost(0, 0),
        name="add",
    )
    done = (outs[0],)
    outs = list(outs)
    for stream, (_, parts, _) in zip(adding, plans, strict=True):
        new = [outs.pop(0) for _ in range(parts)]
        if stream.stages:
            stream.keep, *stream.sends = new
            if stream in hold:
                stream.gots = None
            else:
                stream.post()
        else:
            stream.total = new[0]
    others = len(outs) - sum(len(stream.sends) for stream in fresh)
    others, outs = outs[:others], outs[others:]
    for stream in fresh:
        stream.sends = [outs.pop(0) for _ in stream.sends]
        stream.post()
    return done, others


def finish_kernel(most_keep, most_got, keep, *refs, split, gots):
    qkv_out, out_out, pool_out, gains, biases, up_bias, classes, class_bias = refs[gots:]
    chunk, width = out_out.shape
    most = most_keep[...].astype(f32) + most_got[...].astype(f32)
    total = sum(ref[...].astype(f32) for ref in refs[:gots]) + keep[...].astype(f32)
    for third in range(3):
        start = third * width
        qkv_out[:, start : start + split] = most[:, third * split : (third + 1) * split]
        rest = width - split
        qkv_out[:, start + split : start + width] = total[:, third * rest : (third + 1) * rest]
    out_out[...] = most[:, 3 * split : 3 * split + width]
    pool_out[...] = most[:, 3 * split + width :]
    vector = total[0:8, -128:] + total[8:16, -128:]
    for row, source in enumerate((3, 0)):
        gains[row : row + 1, :] = vector[source : source + 1, :chunk]
    for row, source in enumerate((6, 7, 4, 5, 1, 2)):
        biases[row : row + 1, :] = vector[source : source + 1, :chunk]
    ramp = vector[:, chunk : 2 * chunk]
    biases[6:7, :] = ramp[1:2, :]
    half = up_bias.shape[1] // 2
    for row in range(2):
        up_bias[:, row * half : (row + 1) * half] = vector[row : row + 1, 2 * chunk : 2 * chunk + half]
    classes[...] = ramp[2 : 2 + CLASSES, :]
    class_bias[...] = jnp.transpose(vector)[chunk : chunk + 1, 2 + CLASSES : 2 + 2 * CLASSES]


def finish(most, last, split, width, up_size, after):
    chunk = most.keep.shape[0]
    sizes = [(chunk, 3 * width), (chunk, width), (chunk, width), (2, chunk), (7, chunk), (1, up_size), (CLASSES, chunk)]
    sizes.append((1, CLASSES))
    operands = (most.keep, *most.gots, last.keep, *last.gots)
    return run(
        functools.partial(finish_kernel, split=split, gots=len(last.gots)),
        after,
        operands,
        [fixed(a.shape) for a in operands],
        16,
        loose=(1, *range(3, len(operands))),
        grid=(1,),
        out_specs=[fixed(size) for size in sizes],
        out_shape=[jax.ShapeDtypeStruct(size, f32) for size in sizes],
        cost_estimate=cost(0, 0),
        name="finish",
    )


def bits_of(size):
    return [1 << k for k in range(size.bit_length() - 1)]


def shards(
    hidden_in,
    lengths,
    labels,
    out_cotangent,
    qkv_weight,
    out_weight,
    up_weight,
    down_weight,
    pool_weight,
    class_weight,
    norm_gains,
    biases,
    up_bias,
    class_bias,
):
    positions, group, width = hidden_in.shape
    n_seq = lax.axis_size("seq")
    n_dp = lax.axis_size("dp")
    n_all = n_seq * n_dp
    seq_at = lax.axis_index("seq")
    me = lax.axis_index("dp") * n_seq + seq_at
    per = group // n_seq
    info = seq_at[None].astype(jnp.int32)
    me_info = me[None].astype(jnp.int32)
    classes = class_weight.shape[1]
    class_rows = jnp.zeros((128, width), bf16).at[:classes].set(class_weight.T)
    class_shift = jnp.full((1, 128), neg_big, f32).at[0, :classes].set(class_bias)

    seq_bits = [("seq", b) for b in bits_of(n_seq)]
    dp_bits = [("dp", b) for b in bits_of(n_dp)]
    chunk = width // n_all
    halved = chunk % 8 == 0

    x_send = split_rows(info, hidden_in.reshape(positions * group, width), positions, group, n_seq)
    x_parts = exchange(x_send)
    cot_send = split_rows(
        info, out_cotangent.reshape(positions * group, width), positions, group, n_seq, after=(x_send[0],)
    )
    cots = exchange(cot_send)
    x_rows, qkv, context, lse, n_one, q_one = attend(
        info, lengths, x_parts, qkv_weight, out_weight, biases, after=(cot_send[0],)
    )
    outs = feed(
        info, labels, cots, n_one, up_weight, up_bias[None, :], down_weight, norm_gains, biases, pool_weight,
        class_rows, class_shift,
    )
    middle_low, act, slope, grad_two, branch_grad, ramp_first, ramp_pre, ramp_out, sums_two, ramp_sums = outs[:10]
    final_parts = outs[10:]

    near = [seq_bits[:1], dp_bits[:1], seq_bits[1:]]
    one_way = [[entry] for entry in seq_bits[:1] + dp_bits[:1] + seq_bits[1:] + dp_bits[1:]]
    three_way = one_way[:3] + [dp_bits[1:]]
    two_way = near[:1] + [near[1] + near[2]] + [[entry] for entry in dp_bits[1:]]
    flat = [entry for stage in one_way for entry in stage]
    places = halving_order(flat, n_seq)
    bits = tuple(bit * (n_seq if axis == "dp" else 1) for axis, bit in flat)
    streams = {}
    done = (branch_grad,)

    def stage(*names, passed=(), hold=()):
        nonlocal done
        if halved:
            done, passed = advance(
                [streams[name] for name in names], passed, done, [streams[name] for name in hold]
            )
        return passed

    def start(name, halves, stages, fine=0):
        nonlocal done
        streams[name] = Halving(halves, stages, fine)
        done = (halves[0],)

    if halved:
        start("down", tall_grad(me_info, act, branch_grad, bits, after=done), two_way)
    stage("down")
    filled = ()
    sums_one, up_sums = [], []
    blocks = 2 * per
    for first, steps in ((0, 1), (1, blocks - 1)):
        filled = feed_back(
            first, steps, blocks, grad_two, branch_grad, slope, n_one, q_one, down_weight, up_weight, out_weight,
            norm_gains, filled, after=done,
        )
        sums_one.append(filled[4])
        up_sums.append(filled[5])
        filled = filled[:4]
        done = (sums_one[-1],)
        if first == 0:
            stage("down")
    pre_grad, grad_one, mix_grad, context_grad = filled
    if halved:
        start("up", wide_grad(me_info, middle_low, pre_grad, places, 1024, after=done), two_way)
    final_parts = exchange([final_parts[0], *stage("down", "up", passed=final_parts[1:])])

    count = width // PAIR // 3
    grads, qkv_sums = [], []
    for first, groups in ((0, 1), (count, 2)):
        grad, qkv_sum = attend_back(
            info, lengths, qkv, context_grad, context, lse, n_seq, first, count, groups, after=done
        )
        grads.append(grad)
        qkv_sums.append(qkv_sum)
        done = (qkv_sum,)
        if first == 0:
            if halved:
                pairs = [(x_rows, grad), (context, mix_grad), (ramp_first, ramp_pre)]
                start("most", group_grad(me_info, pairs, (), None, places, after=done), one_way)
            final_parts = [final_parts[0], *stage("down", "up", "most", passed=final_parts[1:], hold=("down",))]
    back = input_grad(grads, qkv_weight, grad_one, per, n_seq, after=done)
    done = (back[0],)
    if halved:
        pairs = [(x_rows, grad) for grad in grads[1:]]
        vectors = (sums_two, ramp_sums, *sums_one, *up_sums, *qkv_sums)
        start("last", group_grad(me_info, pairs, vectors, (len(sums_one), len(qkv_sums)), places, after=done), three_way, fine=chunk)
    back_parts = exchange(
        [back[0], *stage("up", "most", "last", passed=back[1:], hold=("up",))]
    )
    hidden_out = merge_rows(info, final_parts, bf16, after=done)
    done = (hidden_out,)
    back_parts = [back[0], *stage("down", "up", "most", "last", passed=back_parts[1:])]
    grad_in = merge_rows(info, back_parts, f32, after=done)
    done = (grad_in,)
    stage("down", "up", "most", "last")
    stage("up", "most", "last")
    if halved:
        qkv_total, out_total, pool_total, gains_sum, biases_sum, up_bias_sum, class_sum, class_bias_sum = finish(
            streams["most"], streams["last"], count * PAIR, width, up_weight.shape[1] // n_all, done
        )
        up_bias_sum = up_bias_sum[0]
        class_sum = jnp.transpose(class_sum)
        class_bias_sum = class_bias_sum[0]
        up_total = streams["up"].total
        down_total = streams["down"].total
    else:

        def scatter(value):
            return lax.psum_scatter(value, ("dp", "seq"), scatter_dimension=0, tiled=True)

        wide = jnp.concatenate([grad[t] for t in range(3) for grad in grads], axis=1)
        qkv_total = scatter(tn(x_rows, wide))
        out_total = scatter(tn(context, mix_grad))
        up_total = scatter(tn(middle_low, pre_grad))
        down_total = scatter(tn(act, branch_grad))
        pool_total = scatter(
            lax.dot_general(ramp_first, ramp_pre, (((0,), (0,)), ((), ())), precision=highest)
        )
        table = jnp.concatenate(
            [sums_two[:3], sum(sums_one)[:3], jnp.concatenate(qkv_sums, axis=1)[:2], ramp_sums], axis=0
        )
        table = jnp.transpose(table.reshape(16, n_all, chunk), (1, 0, 2)).reshape(n_all, 16 * chunk)
        table = scatter(jnp.concatenate([table, sum(up_sums).reshape(n_all, -1)], axis=1))[0]
        vec = table[: 8 * chunk].reshape(8, chunk)
        ramp_vec = table[8 * chunk : 16 * chunk].reshape(8, chunk)
        up_bias_sum = table[16 * chunk :]
        gains_sum = jnp.stack([vec[3], vec[0]])
        biases_sum = jnp.stack([vec[6], vec[7], vec[4], vec[5], vec[1], vec[2], ramp_vec[1]])
        class_sum = jnp.transpose(ramp_vec[2 : 2 + classes])
        class_bias_sum = ramp_vec[2 + classes : 2 + 2 * classes, 0]
    ramp_logits = ramp_out.reshape(per, REC, -1)[:, 0, :classes]
    return (
        hidden_out.reshape(positions, group, width),
        ramp_logits,
        grad_in.reshape(positions, group, width),
        qkv_total,
        out_total,
        up_total,
        down_total,
        pool_total,
        class_sum,
        gains_sum,
        biases_sum,
        up_bias_sum,
        class_bias_sum,
    )


def solution(mesh):
    every = ("dp", "seq")
    rows = P("seq", "dp", None)
    return jax.shard_map(
        shards,
        mesh=mesh,
        in_specs=(rows, P("dp"), P(every), rows) + (P(),) * 10,
        out_specs=(
            rows,
            P(every, None),
            rows,
            P(every, None),
            P(every, None),
            P(every, None),
            P(every, None),
            P(every, None),
            P(every, None),
            P(None, every),
            P(None, every),
            P(every),
            P(),
        ),
        check_vma=False,
    )
```

```python
import functools

import jax
import jax.numpy as jnp
from jax import lax
from jax.experimental import pallas as pl
from jax.experimental.pallas import tpu as pltpu
from jax.sharding import PartitionSpec as P

HEAD_DIM = 64
PAIR = 2 * HEAD_DIM
REC = 8
CLASSES = 3
FEED_PARTS = 2

eps = 1e-12
neg_big = -1e30
highest = lax.Precision.HIGHEST
f32 = jnp.float32
bf16 = jnp.bfloat16
MIB = 1 << 20


def nn(left, right):
    return lax.dot_general(left, right, (((1,), (0,)), ((), ())), preferred_element_type=f32)


def nt(left, right):
    return lax.dot_general(left, right, (((1,), (1,)), ((), ())), preferred_element_type=f32)


def tn(left, right):
    return lax.dot_general(left, right, (((0,), (0,)), ((), ())), preferred_element_type=f32)


def cost(flops, nbytes, trans=0):
    return pl.CostEstimate(flops=1, bytes_accessed=1, transcendentals=0)


def smem():
    return pl.BlockSpec(memory_space=pltpu.SMEM)


def in_vmem():
    return pl.BlockSpec(memory_space=pltpu.VMEM)


def fixed(shape):
    return pl.BlockSpec(shape, lambda *_: (0,) * len(shape))


def once(shape):
    return pl.BlockSpec(shape, lambda *_: (0,) * len(shape), pipeline_mode=pl.Buffered(1))


def run(kernel, after, operands, in_specs, limit, out_shape, aliases=None, loose=(), **kwargs):
    skip = len(after)
    operands = [
        a
        if k in loose or spec.memory_space in (pltpu.VMEM, pltpu.SMEM)
        else pltpu.with_memory_space_constraint(a, pltpu.HBM)
        for k, (a, spec) in enumerate(zip(operands, in_specs, strict=True))
    ]
    after = [pltpu.with_memory_space_constraint(a, pltpu.HBM) for a in after]
    single = not isinstance(out_shape, list)
    shapes = [pltpu.HBM(a.shape, a.dtype) for a in ([out_shape] if single else out_shape)]

    def body(*refs):
        kernel(*refs[skip:])

    return pl.pallas_call(
        body,
        in_specs=[pl.BlockSpec(memory_space=pl.ANY)] * skip + list(in_specs),
        out_shape=shapes[0] if single else shapes,
        input_output_aliases={k + skip: v for k, v in (aliases or {}).items()},
        compiler_params=pltpu.CompilerParams(vmem_limit_bytes=limit * MIB),
        **kwargs,
    )(*after, *operands)


def three_parts(value):
    hi = value.astype(bf16)
    rest = value - hi.astype(f32)
    mid = rest.astype(bf16)
    low = (rest - mid.astype(f32)).astype(bf16)
    return jnp.concatenate([hi, mid, low], axis=0)


def fine_dot(dot, value, weight):
    rows = value.shape[0]
    parts = dot(jnp.concatenate([three_parts(value)], axis=0), weight)
    return parts[:rows] + parts[rows : 2 * rows] + parts[2 * rows :]


def split_kernel(info, rows, *outs):
    chunks = len(outs)
    per, span, _ = outs[0].shape
    group = chunks * per
    block = 16 * group
    own = info[0]
    dest = lax.broadcasted_iota(jnp.int32, (block, block), 0)
    source = lax.broadcasted_iota(jnp.int32, (block, block), 1)
    chunk = dest // (16 * per)
    wanted = (dest % 16) * group + per * (chunk ^ own) + (dest // 16) % per
    perm = jnp.where(source == wanted, 1.0, 0.0).astype(bf16)
    for b in range(span // 16):
        moved = nn(perm, rows[b * block : (b + 1) * block, :]).astype(bf16)
        for c in range(chunks):
            for q in range(per):
                at = (c * per + q) * 16
                outs[c][q, b * 16 : (b + 1) * 16, :] = moved[at : at + 16]


def split_rows(info, rows, positions, group, chunks, after=()):
    width = rows.shape[1]
    per = group // chunks
    steps = 2
    span = positions // steps
    return run(
        split_kernel,
        after,
        (info, rows),
        [smem(), pl.BlockSpec((span * group, width), lambda i: (i, 0))],
        16,
        grid=(steps,),
        out_specs=[pl.BlockSpec((per, span, width), lambda i: (0, i, 0))] * chunks,
        out_shape=[jax.ShapeDtypeStruct((per, positions, width), bf16)] * chunks,
        cost_estimate=cost(2 * rows.size * 16 * group, 4 * rows.size),
        name="split_rows",
    )


def merge_kernel(info, *refs):
    ins, out = refs[:-1], refs[-1]
    chunks = len(ins)
    per, span, _ = ins[0].shape
    group = chunks * per
    block = 16 * group
    own = info[0]
    dest = lax.broadcasted_iota(jnp.int32, (block, block), 0)
    source = lax.broadcasted_iota(jnp.int32, (block, block), 1)
    seq = dest % group
    wanted = (((seq // per) ^ own) * per + seq % per) * 16 + dest // group
    perm = jnp.where(source == wanted, 1.0, 0.0).astype(bf16)
    for b in range(span // 16):
        rows = jnp.concatenate(
            [ins[c][q, b * 16 : (b + 1) * 16, :] for c in range(chunks) for q in range(per)], axis=0
        )
        out[b * block : (b + 1) * block, :] = nn(perm, rows).astype(out.dtype)


def merge_rows(info, parts, dtype, after=()):
    chunks = len(parts)
    per, positions, width = parts[0].shape
    group = per * chunks
    steps = 2
    span = positions // steps
    return run(
        merge_kernel,
        after,
        (info, *parts),
        [smem()] + [pl.BlockSpec((per, span, width), lambda i: (0, i, 0))] * chunks,
        16,
        grid=(steps,),
        out_specs=pl.BlockSpec((span * group, width), lambda i: (i, 0)),
        out_shape=jax.ShapeDtypeStruct((positions * group, width), dtype),
        cost_estimate=cost(2 * positions * group * width * 16 * group, 6 * positions * group * width),
        name="merge_rows",
    )


def exchange(parts):
    size = lax.axis_size("seq")
    return [parts[0]] + [
        lax.ppermute(parts[c], "seq", [(i, i ^ c) for i in range(size)]) for c in range(1, size)
    ]


def row_stats(resid):
    mean = jnp.mean(resid, axis=-1, keepdims=True)
    centred = resid - mean
    scale = lax.rsqrt(jnp.mean(centred * centred, axis=-1, keepdims=True) + eps)
    return centred * scale, scale


def attend_kernel(info, lengths, *refs):
    chunks = len(refs) - 10
    parts = refs[:chunks]
    qkv_w, out_w, biases, x_out, qkv, context, lse, normed, scale, stats = refs[chunks:]
    width = out_w.shape[0]
    span = parts[0].shape[1]
    length = chunks * span
    pairs = width // PAIR
    own = info[0]
    live_len = lengths[own * pl.num_programs(0) + pl.program_id(0)]
    x_out[...] = jnp.concatenate([part[0] for part in parts], axis=0)
    for third in range(3):
        cols = slice(third * width, (third + 1) * width)
        block = nn(x_out[...], qkv_w[:, cols])
        if third == 0:
            block = block + biases[0:1, :]
        elif third == 2:
            block = block + biases[1:2, :]
        qkv[:, cols] = block.astype(bf16)
    lane = lax.broadcasted_iota(jnp.int32, (length, PAIR), 1)
    row = lax.broadcasted_iota(jnp.int32, (length, PAIR), 0)
    pos = ((row // span) ^ own) * span + row % span
    key_ext = jnp.where((lane == 0) & (pos >= live_len), neg_big, 0.0).astype(bf16)
    query_ext = jnp.where(lane == 0, 1.0, 0.0).astype(bf16)
    low_half = lane < HEAD_DIM
    masks = [jnp.where(low_half, 1.0, 0.0).astype(bf16), jnp.where(low_half, 0.0, 1.0).astype(bf16)]
    stats[...] = jnp.zeros_like(stats)

    def one_pair(i, carry):
        start = pl.multiple_of(i * PAIR, PAIR)
        queries = qkv[:, pl.ds(start, PAIR)] * bf16(HEAD_DIM**-0.5)
        keys = jnp.concatenate([qkv[:, pl.ds(start + width, PAIR)], key_ext], axis=1)
        values = qkv[:, pl.ds(start + 2 * width, PAIR)]
        total = None
        tops = []
        for head in range(2):
            scores = nt(jnp.concatenate([queries * masks[head], query_ext], axis=1), keys)
            top = jnp.max(scores, axis=1, keepdims=True)
            weights = jnp.exp(scores - top).astype(bf16)
            part = nn(weights, jnp.concatenate([values * masks[head], masks[head]], axis=1))
            total = part if total is None else total + part
            tops.append(top)
        row_total = total[:, PAIR:]
        context[:, pl.ds(start, PAIR)] = (total[:, :PAIR] / row_total).astype(bf16)
        log_total = jnp.where(low_half, tops[0], tops[1]) + jnp.log(row_total)
        swapped = pltpu.roll(log_total, HEAD_DIM, 1)
        stats[...] = jnp.where(
            lane == 2 * i, log_total, jnp.where(lane == 2 * i + 1, swapped, stats[...])
        )
        return carry

    lax.fori_loop(0, pairs, one_pair, 0, unroll=pairs)
    lse[0] = jnp.transpose(stats[...])[: lse.shape[1], :]
    resid = x_out[...].astype(f32) + (nn(context[...], out_w[...]) + biases[2:3, :])
    n_one, q_one = row_stats(resid)
    normed[...] = n_one
    scale[...] = q_one


def attend(info, lengths, parts, qkv_w, out_w, biases, after=()):
    chunks = len(parts)
    per, span, width = parts[0].shape
    length = chunks * span
    rows = per * length
    heads = width // HEAD_DIM
    head_rows = -(-heads // 8) * 8
    by_seq = lambda i: (i, 0)
    return run(
        attend_kernel,
        after,
        (info, lengths, *parts, qkv_w, out_w, biases),
        [smem()] * 2
        + [pl.BlockSpec((1, span, width), lambda i: (i, 0, 0))] * chunks
        + [in_vmem(), once(out_w.shape), once(biases.shape)],
        30,
        grid=(per,),
        out_specs=[
            pl.BlockSpec((length, width), by_seq),
            pl.BlockSpec((length, 3 * width), by_seq),
            pl.BlockSpec((length, width), by_seq),
            pl.BlockSpec((1, head_rows, length), lambda i: (i, 0, 0)),
            pl.BlockSpec((length, width), by_seq),
            pl.BlockSpec((length, 1), by_seq),
        ],
        out_shape=[
            jax.ShapeDtypeStruct((rows, width), bf16),
            jax.ShapeDtypeStruct((rows, 3 * width), bf16),
            jax.ShapeDtypeStruct((rows, width), bf16),
            jax.ShapeDtypeStruct((per, head_rows, length), f32),
            jax.ShapeDtypeStruct((rows, width), f32),
            jax.ShapeDtypeStruct((rows, 1), f32),
        ],
        scratch_shapes=[pltpu.VMEM((length, PAIR), f32)],
        cost_estimate=cost(
            8 * rows * width * width + 8 * rows * length * width, 20 * rows * width + 8 * width * width,
            rows * length * heads,
        ),
        name="attend",
    )


def gelu_pair(x):
    scaled = x * 0.5**0.5
    cdf = 0.5 + 0.5 * lax.erf(scaled)
    bell = jnp.exp(scaled * -scaled)
    return x * cdf, cdf + scaled * bell * (1.0 / jnp.pi) ** 0.5


def norm_back(upper, normed, scale, gain):
    scaled = upper * gain
    mean_part = jnp.mean(scaled, axis=-1, keepdims=True)
    proj_part = jnp.mean(scaled * normed, axis=-1, keepdims=True)
    return scale * (scaled - mean_part - normed * proj_part)


def col_sum(values):
    return jnp.sum(values, axis=0, keepdims=True)


def feed_kernel(info, labels, *refs):
    chunks = (len(refs) - 20) // 2
    cots = refs[:chunks]
    normed, up_w, up_b, down_w, gains, biases, pool_w, class_w, class_b = refs[chunks : chunks + 9]
    middle_out, act, slope, grad_two, branch_grad = refs[chunks + 9 : chunks + 14]
    ramp_first, ramp_pre, ramp_out, sums, ramp_sums = refs[chunks + 14 : chunks + 19]
    finals = refs[chunks + 19 : -1]
    n_two = refs[-1]
    span = finals[0].shape[1]
    own = info[0]

    @pl.when(pl.program_id(0) == 0)
    def _():
        sums[...] = jnp.zeros_like(sums)
        ramp_sums[...] = jnp.zeros_like(ramp_sums)

    hidden = up_w.shape[1]
    tile = 256
    length = chunks * span
    block = length // FEED_PARTS
    scales = []
    for part in range(FEED_PARTS):
        rows = slice(part * block, (part + 1) * block)
        middle = normed[rows, :] * gains[0:1, :] + biases[3:4, :]
        middle_out[rows, :] = middle.astype(bf16)
        for j in range(hidden // tile):
            cols = slice(j * tile, (j + 1) * tile)
            pre = nn(middle_out[rows, :], up_w[:, cols]) + up_b[:, cols]
            value, grad = gelu_pair(pre)
            act[rows, cols] = value.astype(bf16)
            slope[rows, cols] = grad.astype(bf16)
        branch = nn(act[rows, :], down_w[...]) + biases[4:5, :]
        middle = normed[rows, :] * gains[0:1, :] + biases[3:4, :]
        normed_two, q_two = row_stats(middle + branch)
        n_two[rows, :] = normed_two
        scales.append(q_two)
    for c in range(chunks):
        rows = slice(c * span, (c + 1) * span)
        finals[c][0] = (n_two[rows, :] * gains[1:2, :] + biases[5:6, :]).astype(bf16)
    label = labels[pl.program_id(0)]
    start = pl.multiple_of(own * span, 8)
    first = (n_two[pl.ds(start, REC), :] * gains[1:2, :] + biases[5:6, :]).astype(bf16)
    pooled = jnp.tanh(nn(first, pool_w[...]) + biases[6:7, :])
    logits = fine_dot(nt, pooled, class_w[...]) + class_b[...]
    expo = jnp.exp(logits - jnp.max(logits, axis=1, keepdims=True))
    lane = lax.broadcasted_iota(jnp.int32, logits.shape, 1)
    g_logits = expo / jnp.sum(expo, axis=1, keepdims=True) - jnp.where(lane == label, 1.0, 0.0)
    g_pre = fine_dot(nn, g_logits, class_w[...]) * (1.0 - pooled * pooled)
    g_first = fine_dot(nt, g_pre, pool_w[...])
    first_row = lax.broadcasted_iota(jnp.int32, (REC, 1), 0) == 0
    ramp_first[...] = jnp.where(first_row, first.astype(f32), 0.0)
    ramp_pre[...] = jnp.where(first_row, g_pre, 0.0)
    ramp_out[...] = logits
    ramp_sums[1:2, :] += g_pre[0:1, :]
    for c in range(CLASSES):
        at_class = jnp.sum(jnp.where(lane == c, g_logits, 0.0), axis=1, keepdims=True)[0:1, :]
        ramp_sums[2 + c : 3 + c, :] += at_class * pooled[0:1, :]
        ramp_sums[2 + CLASSES + c : 3 + CLASSES + c, :] += at_class + jnp.zeros_like(pooled[0:1, :])
    sum_rows = [0.0, 0.0, 0.0]
    for part in range(FEED_PARTS):
        rows = slice(part * block, (part + 1) * block)
        here = cots[part * chunks // FEED_PARTS : (part + 1) * chunks // FEED_PARTS]
        cot = jnp.concatenate([chunk[0] for chunk in here], axis=0).astype(f32)
        row = part * block + lax.broadcasted_iota(jnp.int32, (block, 1), 0)
        g_final = cot + jnp.where(row == own * span, g_first[0:1, :], 0.0)
        normed_two = n_two[rows, :]
        g_two = norm_back(g_final, normed_two, scales[part], gains[1:2, :])
        grad_two[rows, :] = g_two
        low = g_two.astype(bf16)
        branch_grad[rows, :] = low
        for k, values in enumerate((g_final * normed_two, low.astype(f32), g_final)):
            sum_rows[k] = sum_rows[k] + col_sum(values)
    for k in range(3):
        sums[k : k + 1, :] += sum_rows[k]


def feed(info, labels, cots, normed, up_w, up_b, down_w, gains, biases, pool_w, class_w, class_b, after=()):
    chunks = len(cots)
    per, span, _ = cots[0].shape
    rows, width = normed.shape
    length = rows // per
    hidden = up_w.shape[1]
    by_seq = lambda i: (i, 0)
    row_block = pl.BlockSpec((length, width), by_seq)
    wide_block = pl.BlockSpec((length, hidden), by_seq)
    part = pl.BlockSpec((1, span, width), lambda i: (i, 0, 0))
    consts = (up_w, up_b, down_w, gains, biases, pool_w, class_w, class_b)
    return run(
        feed_kernel,
        after,
        (info, labels, *cots, normed, *consts),
        [smem()] * 2 + [part] * chunks + [row_block, in_vmem()] + [once(a.shape) for a in consts[1:]],
        44,
        grid=(per,),
        out_specs=[
            row_block, wide_block, wide_block, row_block, row_block,
            pl.BlockSpec((REC, width), by_seq), pl.BlockSpec((REC, width), by_seq),
            pl.BlockSpec((REC, class_b.shape[1]), by_seq), fixed((8, width)), fixed((8, width)),
        ]
        + [part] * chunks,
        out_shape=[
            jax.ShapeDtypeStruct((rows, width), bf16),
            jax.ShapeDtypeStruct((rows, hidden), bf16),
            jax.ShapeDtypeStruct((rows, hidden), bf16),
            jax.ShapeDtypeStruct((rows, width), f32),
            jax.ShapeDtypeStruct((rows, width), bf16),
            jax.ShapeDtypeStruct((per * REC, width), f32),
            jax.ShapeDtypeStruct((per * REC, width), f32),
            jax.ShapeDtypeStruct((per * REC, class_b.shape[1]), f32),
            jax.ShapeDtypeStruct((8, width), f32),
            jax.ShapeDtypeStruct((8, width), f32),
        ]
        + [jax.ShapeDtypeStruct((per, span, width), bf16)] * chunks,
        scratch_shapes=[pltpu.VMEM((length, width), f32)],
        cost_estimate=cost(4 * rows * width * hidden, 4 * rows * hidden + 4 * width * hidden + 12 * rows * width),
        name="feed",
    )


def feed_back_kernel(*refs, carried):
    grad_two, branch_grad, slope, n_one, q_one, down_w, up_w, out_w, gains = refs[:9]
    pre_grad, grad_one, mix_grad, context_grad, sums, up_sums = refs[9 + carried :]

    @pl.when(pl.program_id(0) == 0)
    def _():
        sums[...] = jnp.zeros_like(sums)
        up_sums[...] = jnp.zeros_like(up_sums)

    hidden = up_w.shape[1]
    tile = 256
    for j in range(hidden // tile):
        cols = slice(j * tile, (j + 1) * tile)
        pre = nt(branch_grad[...], down_w[cols, :]) * slope[:, cols].astype(f32)
        low = pre.astype(bf16)
        pre_grad[:, cols] = low
        up_sums[:, cols] += col_sum(low.astype(f32))
    g_middle = grad_two[...] + nt(pre_grad[...], up_w[...])
    normed = n_one[...]
    sums[0:1, :] += col_sum(g_middle * normed)
    sums[2:3, :] += col_sum(g_middle)
    g_one = norm_back(g_middle, normed, q_one[...], gains[0:1, :])
    grad_one[...] = g_one
    mix_grad[...] = g_one.astype(bf16)
    sums[1:2, :] += col_sum(mix_grad[...].astype(f32))
    context_grad[...] = nt(mix_grad[...], out_w[...]).astype(bf16)


def feed_back(first, steps, blocks, grad_two, branch_grad, slope, n_one, q_one, down_w, up_w, out_w, gains, before, after=()):
    rows, width = grad_two.shape
    hidden = slope.shape[1]
    block = rows // blocks
    by_row = lambda i: (first + i, 0)
    row_block = pl.BlockSpec((block, width), by_row)
    wide_block = pl.BlockSpec((block, hidden), by_row)
    thin_block = pl.BlockSpec((block, 1), by_row)
    return run(
        functools.partial(feed_back_kernel, carried=len(before)),
        after,
        (grad_two, branch_grad, slope, n_one, q_one, down_w, up_w, out_w, gains, *before),
        [row_block, row_block, wide_block, row_block, thin_block]
        + [in_vmem()] * 2
        + [once(out_w.shape), once(gains.shape)]
        + [pl.BlockSpec(memory_space=pl.ANY)] * len(before),
        32,
        aliases={9 + k: k for k in range(len(before))},
        grid=(steps,),
        out_specs=[wide_block, row_block, row_block, row_block, fixed((8, width)), fixed((1, hidden))],
        out_shape=[
            jax.ShapeDtypeStruct((rows, hidden), bf16),
            jax.ShapeDtypeStruct((rows, width), f32),
            jax.ShapeDtypeStruct((rows, width), bf16),
            jax.ShapeDtypeStruct((rows, width), bf16),
            jax.ShapeDtypeStruct((8, width), f32),
            jax.ShapeDtypeStruct((1, hidden), f32),
        ],
        cost_estimate=cost(0, 0),
        name="feed_back",
    )


def attend_back_kernel(info, lengths, queries_in, keys_in, values_in, context_grad, context, lse, grads, sums, *, chunks, first):
    length, cols = queries_in.shape
    first = first + pl.program_id(0) * (cols // PAIR)
    at_seq = pl.program_id(1)
    span = length // chunks
    own = info[0]
    live_len = lengths[own * pl.num_programs(1) + at_seq]
    factor = HEAD_DIM**-0.5
    lane = lax.broadcasted_iota(jnp.int32, (length, PAIR), 1)
    row = lax.broadcasted_iota(jnp.int32, (length, PAIR), 0)
    pos = ((row // span) ^ own) * span + row % span
    key_ext = jnp.where((lane == 0) & (pos >= live_len), neg_big, 0.0).astype(bf16)
    query_ext = jnp.where(lane == 0, 1.0, 0.0).astype(bf16)
    low_half = lane < HEAD_DIM
    masks = [jnp.where(low_half, 1.0, 0.0).astype(bf16), jnp.where(low_half, 0.0, 1.0).astype(bf16)]
    picks = jnp.where(
        lax.broadcasted_iota(jnp.int32, (8, PAIR), 1) // HEAD_DIM
        == lax.broadcasted_iota(jnp.int32, (8, PAIR), 0),
        1.0,
        0.0,
    ).astype(bf16)
    parts = 1
    block = length // parts

    @pl.when(at_seq == 0)
    def _():
        sums[...] = jnp.zeros_like(sums)

    for pair in range(cols // PAIR):
        at = slice(pair * PAIR, (pair + 1) * PAIR)
        queries = queries_in[:, at] * bf16(factor)
        keys = jnp.concatenate([keys_in[:, at], key_ext], axis=1)
        values = values_in[:, at]
        ctx_grad = context_grad[:, at]
        product = ctx_grad.astype(f32) * context[:, at].astype(f32)
        high = product.astype(bf16)
        low = (product - high.astype(f32)).astype(bf16)
        row_dots = nt(picks, high) + nt(picks, low)
        g_queries = None
        g_keys = [None] * parts
        g_values = [None] * parts
        for head in range(2):
            masked_q = queries * masks[head]
            long_q = jnp.concatenate([masked_q, query_ext], axis=1)
            masked_g = ctx_grad * masks[head]
            masked_k = keys_in[:, at] * masks[head]
            log_total = lse[0, pl.ds(2 * (first + pair) + head, 1), :]
            row_dot = row_dots[head : head + 1, :]
            for c in range(parts):
                rows = slice(c * block, (c + 1) * block)
                weights = jnp.exp(nt(keys[rows], long_q) - log_total)
                part = nn(weights.astype(bf16), masked_g)
                g_values[c] = part if g_values[c] is None else g_values[c] + part
                g_scores = (weights * (nt(values[rows], masked_g) - row_dot)).astype(bf16)
                part = nn(g_scores, masked_q)
                g_keys[c] = part if g_keys[c] is None else g_keys[c] + part
                part = tn(g_scores, masked_k[rows])
                g_queries = part if g_queries is None else g_queries + part
        grads[0, :, at] = (g_queries * factor).astype(bf16)
        for c in range(parts):
            rows = slice(c * block, (c + 1) * block)
            grads[1, rows, at] = g_keys[c].astype(bf16)
            grads[2, rows, at] = g_values[c].astype(bf16)
        sums[0:1, at] += col_sum(grads[0, :, at].astype(f32))
        sums[1:2, at] += col_sum(grads[2, :, at].astype(f32))


def attend_back(info, lengths, qkv, context_grad, context, lse, chunks, first, count, groups, after=()):
    rows, width = context.shape
    per, head_rows, length = lse.shape
    cols = count * PAIR
    blocks = width // cols
    spec = lambda third: pl.BlockSpec((length, cols), lambda g, q: (q, third * blocks + first // count + g))
    return run(
        functools.partial(attend_back_kernel, chunks=chunks, first=first),
        after,
        (info, lengths, qkv, qkv, qkv, context_grad, context, lse),
        [
            smem(),
            smem(),
            spec(0),
            spec(1),
            spec(2),
            spec(0),
            spec(0),
            pl.BlockSpec((1, head_rows, length), lambda g, q: (q, 0, 0)),
        ],
        40,
        grid=(groups, per),
        out_specs=[
            pl.BlockSpec((3, length, cols), lambda g, q: (0, q, g)),
            pl.BlockSpec((8, cols), lambda g, q: (0, g)),
        ],
        out_shape=[
            jax.ShapeDtypeStruct((3, rows, groups * cols), bf16),
            jax.ShapeDtypeStruct((8, groups * cols), f32),
        ],
        cost_estimate=cost(0, 0),
        name="attend_back",
    )


def input_grad_kernel(*refs, groups):
    grads = refs[:groups]
    qkv_w, grad_one = refs[groups : groups + 2]
    outs = refs[groups + 2 :]
    width = grad_one.shape[1]
    total = grad_one[...]
    offset = 0
    for grad in grads:
        each = grad.shape[2]
        for third in range(3):
            start = third * width + offset
            total = total + nt(grad[third], qkv_w[:, start : start + each])
        offset += each
    span = outs[0].shape[1]
    for c, out in enumerate(outs):
        out[0] = total[c * span : (c + 1) * span].astype(bf16)


def input_grad(grads, qkv_w, grad_one, per, chunks, after=()):
    groups = len(grads)
    rows, width = grad_one.shape
    length = rows // per
    span = length // chunks
    return run(
        functools.partial(input_grad_kernel, groups=groups),
        after,
        (*grads, qkv_w, grad_one),
        [pl.BlockSpec((3, length, grad.shape[2]), lambda i: (0, i, 0)) for grad in grads]
        + [in_vmem(), pl.BlockSpec((length, width), lambda i: (i, 0))],
        32,
        grid=(per,),
        out_specs=[pl.BlockSpec((1, span, width), lambda i: (i, 0, 0))] * chunks,
        out_shape=[jax.ShapeDtypeStruct((per, span, width), bf16)] * chunks,
        cost_estimate=cost(6 * rows * width * width, 12 * rows * width + 6 * width * width),
        name="input_grad",
    )


def chunk_at(me, relative, chunk):
    return pl.ds(pl.multiple_of((me ^ relative) * chunk, 8), chunk)


def tall_grad_kernel(info, left, right, keep, send, total, keep_near, send_near, sems, *, bits, chunk):
    total[...] = tn(left[...], right[...])
    here = left.shape[1] // chunk
    me = info[0]

    def copy(other, place, number):
        near, far = ((keep_near, keep), (send_near, send))[other]
        rows = pl.ds(place, chunk)
        return pltpu.make_async_copy(near.at[rows, :], far.at[rows, :], sems.at[other, number])

    for other, near in enumerate((keep_near, send_near)):
        for k in range(0, here, 2):
            source = k + ((me % 2) ^ other)
            relative = (pl.program_id(0) * here + source) ^ me
            place = 0
            for at, bit in enumerate(bits[1:]):
                place = place + ((relative // bit) % 2) * (1 << (len(bits) - 2 - at))
            rows = total[pl.ds(pl.multiple_of(source * chunk, 8), chunk), :]
            start = pl.multiple_of(place * chunk, 16)
            near[pl.ds(start, chunk), :] = rows.astype(bf16)
            copy(other, start, (pl.program_id(0) * here + k) // 2).start()

    @pl.when(pl.program_id(0) == pl.num_programs(0) - 1)
    def _():
        for other in range(2):
            for number in range(1 << (len(bits) - 1)):
                copy(other, 0, number).wait()


def tall_grad(me, left, right, bits, after=()):
    rows, depth = left.shape
    width = right.shape[1]
    chunk = depth >> len(bits)
    block = 8 * chunk
    half = pltpu.VMEM((depth // 2, width), bf16)
    return run(
        functools.partial(tall_grad_kernel, bits=bits, chunk=chunk),
        after,
        (me, left, right),
        [smem(), pl.BlockSpec((rows, block), lambda j: (0, j)), once((rows, width))],
        40,
        grid=(depth // block,),
        out_specs=[pl.BlockSpec(memory_space=pl.ANY)] * 2,
        out_shape=[jax.ShapeDtypeStruct((depth // 2, width), bf16)] * 2,
        scratch_shapes=[
            pltpu.VMEM((block, width), f32), half, half, pltpu.SemaphoreType.DMA((2, 1 << (len(bits) - 1)))
        ],
        cost_estimate=cost(0, 0),
        name="tall_grad",
    )


def wide_grad_kernel(info, left, right, keep, send, left_t, total, *, order, chunk):
    @pl.when(pl.program_id(0) == 0)
    def _():
        left_t[...] = jnp.transpose(left[...])

    me = info[0]
    half = len(order) // 2
    parts, _, tile = total.shape
    for part in range(parts):
        cols = slice(part * tile, (part + 1) * tile)
        total[part] = nn(left_t[...], right[:, cols])
        for at in range(0, len(order), 2):
            rows = jnp.concatenate([total[part, chunk_at(me, order[at + k], chunk), :] for k in range(2)], axis=0)
            target = keep if at < half else send
            row = (at % half) * chunk
            target[row : row + 2 * chunk, cols] = rows.astype(bf16)


def wide_grad(me, left, right, order, tile, after=()):
    rows, depth = left.shape
    width = right.shape[1]
    return run(
        functools.partial(wide_grad_kernel, order=order, chunk=depth // len(order)),
        after,
        (me, left, right),
        [smem(), fixed((rows, depth)), pl.BlockSpec((rows, tile), lambda j: (0, j))],
        32,
        grid=(width // tile,),
        out_specs=[pl.BlockSpec((depth // 2, tile), lambda j: (0, j))] * 2,
        out_shape=[jax.ShapeDtypeStruct((depth // 2, width), bf16)] * 2,
        scratch_shapes=[pltpu.VMEM((depth, rows), bf16), pltpu.VMEM((tile // 256, depth, 256), f32)],
        cost_estimate=cost(2 * rows * depth * width, 2 * rows * (depth + width) + 2 * depth * width),
        name="wide_grad",
    )


def fill_table(table, near, vectors, counts, chunk):
    per, groups = counts
    sums_two, ramp_sums = vectors[:2]
    sums_one = vectors[2 : 2 + per]
    up_sums = vectors[2 + per : 2 + 2 * per]
    qkv_sums = vectors[2 + 2 * per :]
    near[0:3, :] = sums_two[0:3, :]
    near[3:6, :] = sum(ref[0:3, :] for ref in sums_one)
    offset = 0
    for ref in qkv_sums:
        near[6:8, offset : offset + ref.shape[1]] = ref[0:2, :]
        offset += ref.shape[1]
    ups = sum(ref[...] for ref in up_sums)
    owners = table.shape[0]
    wide = ups.shape[1] // owners // 2
    table[...] = jnp.zeros_like(table)
    for k in range(owners):
        cols = slice(k * chunk, (k + 1) * chunk)
        table[k, :, 0:chunk] = near[:, cols]
        table[k, :, chunk : 2 * chunk] = ramp_sums[:, cols]
        for row in range(2):
            start = (2 * k + row) * wide
            table[k, row : row + 1, 2 * chunk : 2 * chunk + wide] = ups[:, start : start + wide]


def group_grad_kernel(info, *refs, order, chunk, jobs, counts):
    extra = counts is not None
    scratch = 3 if extra else 1
    keep, send = refs[-2 - scratch : -scratch]
    total = refs[-scratch]
    at_ref = 0
    column = 0
    for thirds in jobs:
        left, right = refs[at_ref : at_ref + 2]
        at_ref += 2
        if left.shape[0] < 128:
            high = right[...].astype(bf16)
            low = (right[...] - high.astype(f32)).astype(bf16)
            lefts = left[...].astype(bf16)
            product = tn(jnp.concatenate([lefts, lefts], axis=0), jnp.concatenate([high, low], axis=0))
            total[:, column : column + high.shape[1]] = product
            column += high.shape[1]
            continue
        left_t = jnp.transpose(left[...])
        for third in range(thirds or 1):
            block = right[third] if thirds else right[...]
            total[:, column : column + block.shape[1]] = nn(left_t, block)
            column += block.shape[1]
    me = info[0]
    half = len(order) // 2
    if extra:
        table, near = refs[-2:]
        fill_table(table, near, refs[at_ref : at_ref + 2 + 2 * counts[0] + counts[1]], counts, chunk)
        for k in range(len(order)):
            high = table[k].astype(bf16).astype(f32)
            total[k * chunk : k * chunk + 8, column:] = high
            total[k * chunk + 8 : k * chunk + 16, column:] = table[k] - high
            total[k * chunk + 16 : (k + 1) * chunk, column:] = jnp.zeros((chunk - 16, high.shape[1]), f32)
    for at in range(0, len(order), 2):
        rows = jnp.concatenate([total[chunk_at(me, order[at + k], chunk), :] for k in range(2)], axis=0)
        target = keep if at < half else send
        row = (at % half) * chunk
        target[row : row + 2 * chunk, :] = rows.astype(bf16)


def group_grad(me, pairs, vectors, counts, order, after=()):
    rows, depth = pairs[0][0].shape
    jobs = tuple(right.shape[0] if right.ndim == 3 else 0 for _, right in pairs)
    width = sum((right.shape[0] if right.ndim == 3 else 1) * right.shape[-1] for _, right in pairs)
    chunk = depth // len(order)
    extra = counts is not None
    width += 128 if extra else 0
    tall = depth // 2
    operands = [a for pair in pairs for a in pair] + list(vectors)
    scratch = [pltpu.VMEM((depth, width), f32)]
    if extra:
        scratch += [pltpu.VMEM((len(order), 8, 128), f32), pltpu.VMEM((8, depth), f32)]
    return run(
        functools.partial(group_grad_kernel, order=order, chunk=chunk, jobs=jobs, counts=counts),
        after,
        (me, *operands),
        [smem()] + [fixed(a.shape) for a in operands],
        48,
        grid=(1,),
        out_specs=[fixed((tall, width))] * 2,
        out_shape=[jax.ShapeDtypeStruct((tall, width), bf16)] * 2,
        scratch_shapes=scratch,
        cost_estimate=cost(0, 0),
        name="group_grad",
    )


def halving_order(stages, n_seq):
    bits = [bit * (n_seq if axis == "dp" else 1) for axis, bit in stages]
    count = len(bits)
    return [
        sum(bit for at, bit in enumerate(bits) if (place >> (count - 1 - at)) & 1) for place in range(1 << count)
    ]


def renew(values, chunk):
    groups = values.reshape(-1, chunk // 8, 8, values.shape[1])
    vector = groups[:, 0] + groups[:, 1]
    high = vector.astype(bf16).astype(f32)
    rest = [groups[:, k] for k in range(2, chunk // 8)]
    return jnp.stack([high, vector - high, *rest], axis=1).reshape(values.shape)


def add_kernel(*refs, plans):
    count = sum(1 + gots for gots, _, _ in plans)
    ins, outs = list(refs[:count]), list(refs[count:])
    for gots, parts, chunk in plans:
        terms = [ins.pop(0) for _ in range(1 + gots)]
        part_rows = terms[0].shape[0] // parts
        whole_rows = part_rows % 16 == 0
        if not whole_rows:
            total = sum(term[...].astype(f32) for term in terms[1:]) + terms[0][...].astype(f32)
        for part in range(parts):
            out = outs.pop(0)
            rows = slice(part * part_rows, (part + 1) * part_rows)
            if whole_rows:
                values = sum(term[rows, :].astype(f32) for term in terms[1:]) + terms[0][rows, :].astype(f32)
            else:
                values = total[rows]
            if chunk:
                out[:, :-128] = values[:, :-128].astype(out.dtype)
                out[:, -128:] = renew(values[:, -128:], chunk).astype(out.dtype)
            else:
                out[...] = values.astype(out.dtype)


class Halving:
    def __init__(self, halves, stages, fine=0):
        self.keep, *self.sends = halves
        self.stages = stages
        self.fine = fine
        self.gots = None

    def post(self):
        stage = self.stages[0]
        self.stages = self.stages[1:]
        self.gots = []
        for part, send in enumerate(self.sends, 1):
            masks = {}
            for at, (axis, bit) in enumerate(stage):
                if (part >> (len(stage) - 1 - at)) & 1:
                    masks[axis] = masks.get(axis, 0) ^ bit
            axes = tuple(masks)
            if len(axes) == 1:
                size, mask, name = lax.axis_size(axes[0]), masks[axes[0]], axes[0]
            else:
                n_seq = lax.axis_size("seq")
                size = lax.axis_size("dp") * n_seq
                mask, name = masks["dp"] * n_seq + masks["seq"], ("dp", "seq")
            self.gots.append(lax.ppermute(send, name, [(i, i ^ mask) for i in range(size)]))


def advance(streams, passed, after, hold=()):
    adding = [stream for stream in streams if stream.gots is not None]
    fresh = [stream for stream in streams if stream.gots is None]
    passed = list(passed) + [send for stream in fresh for send in stream.sends]
    steps = 2 if sum(stream.keep.size for stream in adding) > 3 << 18 and not any(s.fine for s in adding) else 1
    operands, in_specs, out_specs, shapes, plans, loose = [], [], [], [], [], []
    for stream in adding:
        rows, width = stream.keep.shape
        tile = width // steps
        loose += [len(operands) + 1 + k for k in range(len(stream.gots))]
        operands += [stream.keep, *stream.gots]
        in_specs += [pl.BlockSpec((rows, tile), lambda j: (0, j))] * (1 + len(stream.gots))
        parts = 1 << len(stream.stages[0]) if stream.stages else 1
        plans.append((len(stream.gots), parts, stream.fine))
        new = [jax.ShapeDtypeStruct((rows // parts, width), bf16 if stream.stages else f32)] * parts
        shapes += new
        out_specs += [pl.BlockSpec((rows // parts, tile), lambda j: (0, j))] * parts
    first_in, first_out = len(operands), len(shapes)

    def body(*refs):
        add_kernel(*refs[:first_in], *refs[first_in + len(passed) :][:first_out], plans=plans)

    outs = run(
        body,
        after,
        operands + passed,
        in_specs + [pl.BlockSpec(memory_space=pl.ANY)] * len(passed),
        40,
        aliases={first_in + k: first_out + k for k in range(len(passed))},
        loose=loose,
        grid=(steps,),
        out_specs=out_specs + [pl.BlockSpec(memory_space=pl.ANY)] * len(passed),
        out_shape=shapes + [jax.ShapeDtypeStruct(a.shape, a.dtype) for a in passed],
        cost_estimate=cost(0, 0),
        name="add",
    )
    done = (outs[0],)
    outs = list(outs)
    for stream, (_, parts, _) in zip(adding, plans, strict=True):
        new = [outs.pop(0) for _ in range(parts)]
        if stream.stages:
            stream.keep, *stream.sends = new
            if stream in hold:
                stream.gots = None
            else:
                stream.post()
        else:
            stream.total = new[0]
    others = len(outs) - sum(len(stream.sends) for stream in fresh)
    others, outs = outs[:others], outs[others:]
    for stream in fresh:
        stream.sends = [outs.pop(0) for _ in stream.sends]
        stream.post()
    return done, others


def finish_kernel(most_keep, most_got, keep, *refs, split, gots):
    qkv_out, out_out, pool_out, gains, biases, up_bias, classes, class_bias = refs[gots:]
    chunk, width = out_out.shape
    most = most_keep[...].astype(f32) + most_got[...].astype(f32)
    total = sum(ref[...].astype(f32) for ref in refs[:gots]) + keep[...].astype(f32)
    for third in range(3):
        start = third * width
        qkv_out[:, start : start + split] = most[:, third * split : (third + 1) * split]
        rest = width - split
        qkv_out[:, start + split : start + width] = total[:, third * rest : (third + 1) * rest]
    out_out[...] = most[:, 3 * split : 3 * split + width]
    pool_out[...] = most[:, 3 * split + width :]
    vector = total[0:8, -128:] + total[8:16, -128:]
    for row, source in enumerate((3, 0)):
        gains[row : row + 1, :] = vector[source : source + 1, :chunk]
    for row, source in enumerate((6, 7, 4, 5, 1, 2)):
        biases[row : row + 1, :] = vector[source : source + 1, :chunk]
    ramp = vector[:, chunk : 2 * chunk]
    biases[6:7, :] = ramp[1:2, :]
    half = up_bias.shape[1] // 2
    for row in range(2):
        up_bias[:, row * half : (row + 1) * half] = vector[row : row + 1, 2 * chunk : 2 * chunk + half]
    classes[...] = ramp[2 : 2 + CLASSES, :]
    class_bias[...] = jnp.transpose(vector)[chunk : chunk + 1, 2 + CLASSES : 2 + 2 * CLASSES]


def finish(most, last, split, width, up_size, after):
    chunk = most.keep.shape[0]
    sizes = [(chunk, 3 * width), (chunk, width), (chunk, width), (2, chunk), (7, chunk), (1, up_size), (CLASSES, chunk)]
    sizes.append((1, CLASSES))
    operands = (most.keep, *most.gots, last.keep, *last.gots)
    return run(
        functools.partial(finish_kernel, split=split, gots=len(last.gots)),
        after,
        operands,
        [fixed(a.shape) for a in operands],
        16,
        loose=(1, *range(3, len(operands))),
        grid=(1,),
        out_specs=[fixed(size) for size in sizes],
        out_shape=[jax.ShapeDtypeStruct(size, f32) for size in sizes],
        cost_estimate=cost(0, 0),
        name="finish",
    )


def bits_of(size):
    return [1 << k for k in range(size.bit_length() - 1)]


def shards(
    hidden_in,
    lengths,
    labels,
    out_cotangent,
    qkv_weight,
    out_weight,
    up_weight,
    down_weight,
    pool_weight,
    class_weight,
    norm_gains,
    biases,
    up_bias,
    class_bias,
):
    positions, group, width = hidden_in.shape
    n_seq = lax.axis_size("seq")
    n_dp = lax.axis_size("dp")
    n_all = n_seq * n_dp
    seq_at = lax.axis_index("seq")
    me = lax.axis_index("dp") * n_seq + seq_at
    per = group // n_seq
    info = seq_at[None].astype(jnp.int32)
    me_info = me[None].astype(jnp.int32)
    classes = class_weight.shape[1]
    class_rows = jnp.zeros((128, width), bf16).at[:classes].set(class_weight.T)
    class_shift = jnp.full((1, 128), neg_big, f32).at[0, :classes].set(class_bias)

    seq_bits = [("seq", b) for b in bits_of(n_seq)]
    dp_bits = [("dp", b) for b in bits_of(n_dp)]
    chunk = width // n_all
    halved = chunk % 8 == 0

    x_send = split_rows(info, hidden_in.reshape(positions * group, width), positions, group, n_seq)
    x_parts = exchange(x_send)
    cot_send = split_rows(
        info, out_cotangent.reshape(positions * group, width), positions, group, n_seq, after=(x_send[0],)
    )
    cots = exchange(cot_send)
    x_rows, qkv, context, lse, n_one, q_one = attend(
        info, lengths, x_parts, qkv_weight, out_weight, biases, after=(cot_send[0],)
    )
    outs = feed(
        info, labels, cots, n_one, up_weight, up_bias[None, :], down_weight, norm_gains, biases, pool_weight,
        class_rows, class_shift,
    )
    middle_low, act, slope, grad_two, branch_grad, ramp_first, ramp_pre, ramp_out, sums_two, ramp_sums = outs[:10]
    final_parts = outs[10:]

    near = [seq_bits[:1], dp_bits[:1], seq_bits[1:]]
    one_way = [[entry] for entry in seq_bits[:1] + dp_bits[:1] + seq_bits[1:] + dp_bits[1:]]
    three_way = one_way[:3] + [dp_bits[1:]]
    two_way = near[:1] + [near[1] + near[2]] + [[entry] for entry in dp_bits[1:]]
    flat = [entry for stage in one_way for entry in stage]
    places = halving_order(flat, n_seq)
    bits = tuple(bit * (n_seq if axis == "dp" else 1) for axis, bit in flat)
    streams = {}
    done = (branch_grad,)

    def stage(*names, passed=(), hold=()):
        nonlocal done
        if halved:
            done, passed = advance(
                [streams[name] for name in names], passed, done, [streams[name] for name in hold]
            )
        return passed

    def start(name, halves, stages, fine=0):
        nonlocal done
        streams[name] = Halving(halves, stages, fine)
        done = (halves[0],)

    if halved:
        start("down", tall_grad(me_info, act, branch_grad, bits, after=done), two_way)
    stage("down")
    filled = ()
    sums_one, up_sums = [], []
    blocks = 2 * per
    for first, steps in ((0, 1), (1, blocks - 1)):
        filled = feed_back(
            first, steps, blocks, grad_two, branch_grad, slope, n_one, q_one, down_weight, up_weight, out_weight,
            norm_gains, filled, after=done,
        )
        sums_one.append(filled[4])
        up_sums.append(filled[5])
        filled = filled[:4]
        done = (sums_one[-1],)
        if first == 0:
            stage("down")
    pre_grad, grad_one, mix_grad, context_grad = filled
    if halved:
        start("up", wide_grad(me_info, middle_low, pre_grad, places, 1024, after=done), two_way)
    final_parts = exchange([final_parts[0], *stage("down", "up", passed=final_parts[1:])])

    count = width // PAIR // 3
    grads, qkv_sums = [], []
    for first, groups in ((0, 1), (count, 2)):
        grad, qkv_sum = attend_back(
            info, lengths, qkv, context_grad, context, lse, n_seq, first, count, groups, after=done
        )
        grads.append(grad)
        qkv_sums.append(qkv_sum)
        done = (qkv_sum,)
        if first == 0:
            if halved:
                pairs = [(x_rows, grad), (context, mix_grad), (ramp_first, ramp_pre)]
                start("most", group_grad(me_info, pairs, (), None, places, after=done), one_way)
            final_parts = [final_parts[0], *stage("down", "up", "most", passed=final_parts[1:], hold=("down",))]
    back = input_grad(grads, qkv_weight, grad_one, per, n_seq, after=done)
    done = (back[0],)
    if halved:
        pairs = [(x_rows, grad) for grad in grads[1:]]
        vectors = (sums_two, ramp_sums, *sums_one, *up_sums, *qkv_sums)
        start("last", group_grad(me_info, pairs, vectors, (len(sums_one), len(qkv_sums)), places, after=done), three_way, fine=chunk)
    back_parts = exchange(
        [back[0], *stage("up", "most", "last", passed=back[1:], hold=("up",))]
    )
    hidden_out = merge_rows(info, final_parts, bf16, after=done)
    done = (hidden_out,)
    back_parts = [back[0], *stage("down", "up", "most", "last", passed=back_parts[1:])]
    grad_in = merge_rows(info, back_parts, f32, after=done)
    done = (grad_in,)
    stage("down", "up", "most", "last")
    stage("up", "most", "last")
    if halved:
        qkv_total, out_total, pool_total, gains_sum, biases_sum, up_bias_sum, class_sum, class_bias_sum = finish(
            streams["most"], streams["last"], count * PAIR, width, up_weight.shape[1] // n_all, done
        )
        up_bias_sum = up_bias_sum[0]
        class_sum = jnp.transpose(class_sum)
        class_bias_sum = class_bias_sum[0]
        up_total = streams["up"].total
        down_total = streams["down"].total
    else:

        def scatter(value):
            return lax.psum_scatter(value, ("dp", "seq"), scatter_dimension=0, tiled=True)

        wide = jnp.concatenate([grad[t] for t in range(3) for grad in grads], axis=1)
        qkv_total = scatter(tn(x_rows, wide))
        out_total = scatter(tn(context, mix_grad))
        up_total = scatter(tn(middle_low, pre_grad))
        down_total = scatter(tn(act, branch_grad))
        pool_total = scatter(
            lax.dot_general(ramp_first, ramp_pre, (((0,), (0,)), ((), ())), precision=highest)
        )
        table = jnp.concatenate(
            [sums_two[:3], sum(sums_one)[:3], jnp.concatenate(qkv_sums, axis=1)[:2], ramp_sums], axis=0
        )
        table = jnp.transpose(table.reshape(16, n_all, chunk), (1, 0, 2)).reshape(n_all, 16 * chunk)
        table = scatter(jnp.concatenate([table, sum(up_sums).reshape(n_all, -1)], axis=1))[0]
        vec = table[: 8 * chunk].reshape(8, chunk)
        ramp_vec = table[8 * chunk : 16 * chunk].reshape(8, chunk)
        up_bias_sum = table[16 * chunk :]
        gains_sum = jnp.stack([vec[3], vec[0]])
        biases_sum = jnp.stack([vec[6], vec[7], vec[4], vec[5], vec[1], vec[2], ramp_vec[1]])
        class_sum = jnp.transpose(ramp_vec[2 : 2 + classes])
        class_bias_sum = ramp_vec[2 + classes : 2 + 2 * classes, 0]
    ramp_logits = ramp_out.reshape(per, REC, -1)[:, 0, :classes]
    return (
        hidden_out.reshape(positions, group, width),
        ramp_logits,
        grad_in.reshape(positions, group, width),
        qkv_total,
        out_total,
        up_total,
        down_total,
        pool_total,
        class_sum,
        gains_sum,
        biases_sum,
        up_bias_sum,
        class_bias_sum,
    )


def solution(mesh):
    every = ("dp", "seq")
    rows = P("seq", "dp", None)
    return jax.shard_map(
        shards,
        mesh=mesh,
        in_specs=(rows, P("dp"), P(every), rows) + (P(),) * 10,
        out_specs=(
            rows,
            P(every, None),
            rows,
            P(every, None),
            P(every, None),
            P(every, None),
            P(every, None),
            P(every, None),
            P(every, None),
            P(None, every),
            P(None, every),
            P(every),
            P(),
        ),
        check_vma=False,
    )
```
